32 devices in a mesh: row: 4 (over z), col: 8 (over y, x, core).
Axes of the slice: x: 2, y: 2, z: 4, core: 2. Of those that a mesh axis runs over, the one named last changes fastest.
Arguments:
- t2_pairs: bfloat16 [8, 8, 16, 16, 64, 64], P('row', None, None, None, 'col'), may hold values from -6 to 6
- cycle_ints: bfloat16 [8192, 8192], P('row', 'col'), may hold values from -0.1875 to 0.1875
- eps_occ: float32 [8, 16], replicated, may hold values from -2 to -0.4
- eps_virt: float32 [8, 64], replicated, may hold values from 0.2 to 3
- occ_count: int32 [8], replicated, may hold values from 8 to 16, as said below
- virt_count: int32 [8], replicated, may hold values from 32 to 64, as said below
- window_irrep: int32 [1], replicated, may hold values from 0 to 7
Outputs:
- update: float32 [8192, 8192], P('row', 'col')
The draws below stay inside these ranges and needn't reach their ends.
Inputs may be any that keep to these rules, and one draw needn't show every extreme that they name: `occ_count`: at least half of the slots; one irrep fills all 16, and another holds exactly the least. `virt_count`: at least half of the slots; one irrep fills all 64, and another holds exactly the least.
All inputs are finite; a program needn't handle non-finite values.
Results may differ from the reference program's by a relative error of at most 0.0003.
Values may be sent and summed in bfloat16 or wider, within the bound.
No kernel may reach another device: no remote copies, remote signals or barrier semaphores. Data moves between devices by JAX's collectives and lax.ppermute only.
A program may use at most 128 MiB of HBM per device.

```python
import jax
import jax.numpy as jnp
from jax import lax

NIRREP = 8
OCC_CAP = 16
VIR_CAP = 64
PH_DIM = 8192


def capped_counts(key, capacity):
    key_one, key_two, key_three = jax.random.split(jax.random.fold_in(key, 7), 3)
    least = max(capacity // 2, 1)
    counts = jax.random.randint(key_one, (NIRREP,), least, capacity + 1)
    fullest = jax.random.randint(key_two, (), 0, NIRREP)
    offset = jax.random.randint(key_three, (), 1, NIRREP)
    emptiest = (fullest + offset) % NIRREP
    irreps = jnp.arange(NIRREP)
    counts = jnp.where(irreps == fullest, capacity, counts)
    counts = jnp.where(irreps == emptiest, least, counts)
    return counts.astype(jnp.int32)


def draw_occ_count(key, part):
    return capped_counts(jax.random.fold_in(key, 11), OCC_CAP)


def draw_virt_count(key, part):
    return capped_counts(jax.random.fold_in(key, 23), VIR_CAP)


def block_levels(key, dims, pieces, low, largest):
    level, own = 1.0, jax.random.fold_in(key, 6)
    for position, shards_of in pieces:
        steps = jnp.exp(jax.random.uniform(jax.random.fold_in(own, position), (shards_of,), jnp.float32, low / len(pieces), largest / len(pieces)))
        level = level * jnp.repeat(steps, dims[position] // shards_of).reshape([-1 if axis == position else 1 for axis in range(len(dims))])
    return level


def gaussian(stream_key, shape, deviation, limit, shards=(), kind=jnp.bfloat16):
    result = deviation * jax.random.normal(stream_key, shape, jnp.float32)
    if shards:
        result = result * block_levels(stream_key, shape, shards, -0.22, 0.18)
    return jnp.clip(result, -limit, limit).astype(kind)


def setup_inputs(seed: int = 0) -> dict:
    key_list = jax.random.split(jax.random.key(seed), 8)
    return {
        "t2_pairs": gaussian(key_list[0], (NIRREP, NIRREP, OCC_CAP, OCC_CAP, VIR_CAP, VIR_CAP), 1.0, 6.0, ((0, 4), (4, 8))),
        "cycle_ints": gaussian(key_list[1], (PH_DIM, PH_DIM), (PH_DIM // 8) ** -0.5, 0.1875, ((0, 4), (1, 8))),
        "eps_occ": jnp.clip(jax.random.uniform(key_list[2], (NIRREP, OCC_CAP), jnp.float32, -2.0, -0.4), -2.0, -0.4),
        "eps_virt": jnp.clip(jax.random.uniform(key_list[3], (NIRREP, VIR_CAP), jnp.float32, 0.2, 3.0), 0.2, 3.0),
        "occ_count": draw_occ_count(jax.random.fold_in(key_list[7], 71), 0),
        "virt_count": draw_virt_count(jax.random.fold_in(key_list[7], 71), 0),
        "window_irrep": jax.random.randint(key_list[6], (1,), 0, 8).astype(jnp.int32),
    }


def ph_vectors(eps_occ, eps_virt, occ_count, virt_count, window_irrep):
    irreps = jnp.arange(NIRREP, dtype=jnp.int32)
    partner = jnp.bitwise_xor(irreps, window_irrep[0])
    onehot = (partner[:, None] == irreps[None, :])
    virt_rows = jnp.dot(onehot.astype(jnp.float32), eps_virt, precision=lax.Precision.HIGHEST)
    virt_live = jnp.sum(jnp.where(onehot, virt_count[None, :], 0), axis=1)
    energy = eps_occ[:, None, :] - virt_rows[:, :, None]
    slots_occ = jnp.arange(OCC_CAP, dtype=jnp.int32)
    slots_virt = jnp.arange(VIR_CAP, dtype=jnp.int32)
    live = (slots_occ[None, None, :] < occ_count[:, None, None]) & (slots_virt[None, :, None] < virt_live[:, None, None])
    return energy.reshape(-1), live.reshape(-1)


def reference(t2_pairs, cycle_ints, eps_occ, eps_virt, occ_count, virt_count, window_irrep):
    energy, live = ph_vectors(eps_occ, eps_virt, occ_count, virt_count, window_irrep)
    amps = jnp.transpose(t2_pairs, (0, 4, 2, 1, 5, 3)).reshape(PH_DIM, PH_DIM)
    both = live[:, None] & live[None, :]
    amps = jnp.where(both, amps, jnp.zeros_like(amps)).astype(jnp.bfloat16)
    cycle = jnp.dot(cycle_ints, amps, preferred_element_type=jnp.float32)
    denom = energy[:, None] + energy[None, :]
    return jnp.where(both, cycle / denom, jnp.float32(0.0))
```

```python
import functools

import jax
import jax.numpy as jnp
from jax import lax
from jax.experimental import pallas as pl
from jax.experimental.pallas import tpu as pltpu
from jax.sharding import PartitionSpec as P

NIRREP = 8
OCC_CAP = 16
VIR_CAP = 64
BLOCK = VIR_CAP * OCC_CAP
SIZES = (512, 640, 768, 896, 1024)
F32 = jnp.float32
BF16 = jnp.bfloat16
I32 = jnp.int32
VMEM_BYTES = 56 * 1024 * 1024


def iota(shape, dim):
    return lax.broadcasted_iota(I32, shape, dim)


def params():
    return pltpu.CompilerParams(vmem_limit_bytes=VMEM_BYTES)


def cost(flops, nbytes):
    return pl.CostEstimate(flops=flops, bytes_accessed=nbytes, transcendentals=0)


def pair_scalars(occ, virt, win, pair):
    first = 2 * pair
    o_a, o_b = occ[first], occ[first + 1]
    v_a, v_b = virt[first ^ win[0]], virt[(first + 1) ^ win[0]]
    return (o_a, o_b), (v_a, v_b), (o_a * ((v_a + 1) >> 1), o_a * (v_a >> 1))


def place(q, p, second, counts):
    (o_a, o_b), (v_a, v_b), (start_even, start_odd) = counts
    o = jnp.where(second, o_b, o_a)
    v = jnp.where(second, v_b, v_a)
    start = jnp.where(second, jnp.where((q & 1) == 0, start_even, start_odd), 0)
    return jnp.where((p < o) & (q < v), start + (q >> 1) * o + p, -1)


def one_hot(left, right):
    return jnp.where(left == right, 1.0, 0.0).astype(BF16)


def dot(a, b):
    return jnp.dot(a, b, preferred_element_type=F32)


def prep_kernel(size, occ, virt, win, t2_ref, even_ref, odd_ref, x_ref):
    counts = pair_scalars(occ, virt, win, pl.program_id(0))
    row = iota((256, 1), 0)
    source = (((row >> 6) & 1) << 7) | (((row >> 2) & 15) << 3) | ((row & 3) << 1) | (row >> 7)
    by_parity = one_hot(iota((256, 256), 1), source)
    targets = []
    for half in range(2):
        for group in range(4):
            parts = [
                t2_ref[:, half, :, 4 * group + i].astype(F32).reshape(256, VIR_CAP) for i in range(4)
            ]
            x = jnp.concatenate(parts, axis=1).astype(BF16)
            at = (4 * half + group) * 256
            x_ref[:, at : at + 256] = dot(by_parity, x).astype(BF16)
            r = iota((256, 1), 0)
            p, q = 4 * group + (r >> 6), r & 63
            spot = place(q, p, half == 1, counts)
            targets.append(jnp.where(spot >= 0, spot + (q & 1) * size, -1))
    for start in range(0, 2 * size, 256):
        acc = jnp.zeros((256, 256), F32)
        lane = iota((256, 256), 1) + start
        for chunk in range(8):
            acc += dot(x_ref[:, chunk * 256 : chunk * 256 + 256], one_hot(targets[chunk], lane))
        acc = acc.astype(BF16)
        for part in range(2):
            at = start + 128 * part
            core, col = at // size, at % size
            tile = acc[:, 128 * part : 128 * part + 128]
            even_ref[core, :, col : col + 128] = tile[:128]
            odd_ref[core, :, col : col + 128] = tile[128:]


def prep(size, scalars, t2):
    shape = jax.ShapeDtypeStruct((NIRREP, 128, size), BF16)
    block = pl.BlockSpec((2, 128, size), lambda k, *_: (k, 0, 0))
    return pl.pallas_call(
        functools.partial(prep_kernel, size),
        out_shape=(shape, shape),
        grid_spec=pltpu.PrefetchScalarGridSpec(
            num_scalar_prefetch=3,
            grid=(NIRREP // 2,),
            in_specs=[
                pl.BlockSpec((2, 2, OCC_CAP, OCC_CAP, 8, VIR_CAP), lambda k, *_: (0, k, 0, 0, 0, 0))
            ],
            out_specs=[block, block],
            scratch_shapes=[pltpu.VMEM((256, 2048), BF16)],
        ),
        compiler_params=params(),
        cost_estimate=cost(2 * 4 * 256 * 2048 * 2 * size, 12 * 2**20),
        name="prep_amplitudes",
    )(*scalars, t2)


def rows_kernel(size, parity, occ, virt, win, at, x_ref, out_ref, sel_ref):
    @pl.when(pl.program_id(0) == 0)
    def _():
        counts = pair_scalars(occ, virt, win, at[0])
        i = iota((1, BLOCK), 1)
        q = 8 * (i >> 7) + 2 * (i & 3) + parity
        spot = place(q, (i >> 2) & 15, ((i >> 6) & 1) == 1, counts)
        for r in range(0, size, 128):
            sel_ref[r : r + 128, :] = one_hot(iota((128, BLOCK), 0) + r, spot)

    x = x_ref[...].reshape(BLOCK, 128)
    out_ref[...] = dot(sel_ref[...], x).astype(BF16)


def compact_rows(size, parity, scalars, at, x):
    return pl.pallas_call(
        functools.partial(rows_kernel, size, parity),
        out_shape=jax.ShapeDtypeStruct((size, size), BF16),
        grid_spec=pltpu.PrefetchScalarGridSpec(
            num_scalar_prefetch=4,
            grid=(size // 128,),
            in_specs=[pl.BlockSpec((NIRREP, 128, 128), lambda n, *_: (0, 0, n))],
            out_specs=pl.BlockSpec((size, 128), lambda n, *_: (0, n)),
            scratch_shapes=[pltpu.VMEM((size, BLOCK), BF16)],
        ),
        compiler_params=params(),
        cost_estimate=cost(2 * size * BLOCK * size, 4 * size * BLOCK),
        name="compact_rows",
    )(*scalars, at, x)


def ints_kernel(size, occ, virt, win, at, mine_ref, other_ref, out_ref, sel_ref, cols_ref):
    plane, dev = at[0], at[1]
    parity = dev & 1

    @pl.when(pl.program_id(0) == 0)
    def _():
        counts = pair_scalars(occ, virt, win, plane)
        i = iota((1, BLOCK), 1)
        q = 2 * ((i >> 4) & 31) + parity
        spot = place(q, i & 15, (i >> 9) == 1, counts)
        for r in range(0, size, 128):
            sel_ref[r : r + 128, :] = one_hot(iota((128, BLOCK), 0) + r, spot)

    counts = pair_scalars(occ, virt, win, dev >> 1)
    i = iota((BLOCK, 1), 0)
    q, p = i >> 4, i & 15
    lane = iota((BLOCK, 256), 1) + pl.program_id(0) * 256
    acc = None
    for ref, second in ((mine_ref, parity == 1), (other_ref, parity == 0)):
        spot = place(q, p, second, counts)
        target = jnp.where(spot >= 0, spot + (q & 1) * size, -1)
        part = dot(ref[...], one_hot(target, lane))
        acc = part if acc is None else acc + part
    cols_ref[...] = acc.astype(BF16)
    out_ref[...] = dot(sel_ref[...], cols_ref[...]).astype(BF16)


def compact_ints(size, scalars, at, mine, other):
    whole = pl.BlockSpec((BLOCK, BLOCK), lambda n, *_: (0, 0))
    return pl.pallas_call(
        functools.partial(ints_kernel, size),
        out_shape=jax.ShapeDtypeStruct((size, 2 * size), BF16),
        grid_spec=pltpu.PrefetchScalarGridSpec(
            num_scalar_prefetch=4,
            grid=(2 * size // 256,),
            in_specs=[whole, whole],
            out_specs=pl.BlockSpec((size, 256), lambda n, *_: (0, n)),
            scratch_shapes=[pltpu.VMEM((size, BLOCK), BF16), pltpu.VMEM((BLOCK, 256), BF16)],
        ),
        compiler_params=params(),
        cost_estimate=cost(2 * 2 * BLOCK * BLOCK * 2 * size, 4 * BLOCK * BLOCK + 4 * size * size),
        name="compact_ints",
    )(*scalars, at, mine, other)


def product(size, occ, virt, win, at, ints_ref, own_refs, sib_refs, wide_ref):
    dev = at[1]
    parity = dev & 1
    counts = pair_scalars(occ, virt, win, dev >> 1)
    i = iota((1, 256), 1) + pl.program_id(0) * 256
    q = i >> 4
    spot = place(q, i & 15, parity == 1, counts)
    spot_own = jnp.where((q & 1) == parity, spot, -1)
    spot_sib = jnp.where((q & 1) == parity, -1, spot)
    r = iota((size, 256), 0)
    own_sel = one_hot(r, spot_own)
    sib_sel = one_hot(r, spot_sib)
    for piece in range(2):
        wide = dot(own_refs[piece][...], own_sel) + dot(sib_refs[piece][...], sib_sel)
        wide_ref[piece * size : (piece + 1) * size, :] = wide.astype(BF16)
    return [dot(ints_ref[0, half], wide_ref[...]) for half in range(2)]


def first_kernel(size, occ, virt, win, at, inner, ints_ref, t0, t1, s0, s1, acc_ref, wide_ref):
    parts = product(size, occ, virt, win, at, ints_ref, (t0, t1), (s0, s1), wide_ref)
    for half in range(2):
        acc_ref[half] = parts[half]


def next_kernel(size, occ, virt, win, at, inner, ints_ref, t0, t1, s0, s1, old_ref, acc_ref, wide_ref):
    parts = product(size, occ, virt, win, at, ints_ref, (t0, t1), (s0, s1), wide_ref)
    for half in range(2):
        acc_ref[half] = old_ref[half] + parts[half]


def last_kernel(
    size, occ, virt, win, at, inner, ints_ref, t0, t1, s0, s1, old_ref, evirt, eocc_ref, ecol_ref, out_ref, wide_ref, sum_ref
):
    parts = product(size, occ, virt, win, at, ints_ref, (t0, t1), (s0, s1), wide_ref)
    for half in range(2):
        sum_ref[half, :size, :] = old_ref[half] + parts[half]
    plane, dev = at[0], at[1]
    i = iota((1, 256), 1) + pl.program_id(0) * 256
    col_live = ((i & 15) < occ[dev]) & ((i >> 4) < virt[dev ^ win[0]])
    col_energy = ecol_ref[...]
    _, _, starts = pair_scalars(occ, virt, win, plane)
    p = iota((OCC_CAP, 1), 0)
    for h in range(2):
        irrep = 2 * plane + h
        o, partner = occ[irrep], irrep ^ win[0]
        v = virt[partner]
        occ_energy = eocc_ref[h]
        row_live = (p < o) & col_live
        for q in range(VIR_CAP):
            start = (q >> 1) * o
            if h == 1:
                start = start + starts[q & 1]
            start = jnp.minimum(start, size)
            rows = sum_ref[q & 1, pl.ds(pl.multiple_of((start >> 3) << 3, 8), OCC_CAP + 8), :]
            rows = pltpu.roll(rows, OCC_CAP + 8 - (start & 7), 0)[:OCC_CAP]
            denom = (occ_energy - evirt[partner, q]) + col_energy
            at_row = (h * VIR_CAP + q) * OCC_CAP
            out_ref[at_row : at_row + OCC_CAP, :] = jnp.where(row_live & (q < v), rows / denom, 0.0)


def multiply(size, scalars, at, inner, ints, own, sib, acc=None, energies=None):
    square = pl.BlockSpec((size, size), lambda n, *_: (0, 0))
    tile = pl.BlockSpec((2, size, 256), lambda n, *_: (0, 0, n))
    in_specs = [
        pl.BlockSpec((1, 2, size, 2 * size), lambda n, o, v, w, a, k: (k[0], 0, 0, 0)),
        square, square, square, square,
    ]
    operands = [ints, *own, *sib]
    scratch = [pltpu.VMEM((2 * size, 256), BF16)]
    out_shape = jax.ShapeDtypeStruct((2, size, BLOCK), F32)
    out_specs = tile
    aliases = {}
    kernel = first_kernel
    if acc is not None:
        kernel = next_kernel
        in_specs.append(tile)
        operands.append(acc)
        if energies is None:
            aliases = {10: 0}
    if energies is not None:
        kernel = last_kernel
        in_specs += [
            pl.BlockSpec(memory_space=pltpu.SMEM),
            pl.BlockSpec((2, OCC_CAP, 1), lambda n, *_: (0, 0, 0)),
            pl.BlockSpec((1, 256), lambda n, *_: (0, n)),
        ]
        operands += list(energies)
        scratch.append(pltpu.VMEM((2, size + OCC_CAP + 8, 256), F32))
        out_shape = jax.ShapeDtypeStruct((2 * BLOCK, BLOCK), F32)
        out_specs = pl.BlockSpec((2 * BLOCK, 256), lambda n, *_: (0, n))
    return pl.pallas_call(
        functools.partial(kernel, size),
        out_shape=out_shape,
        grid_spec=pltpu.PrefetchScalarGridSpec(
            num_scalar_prefetch=5,
            grid=(BLOCK // 256,),
            in_specs=in_specs,
            out_specs=out_specs,
            scratch_shapes=scratch,
        ),
        input_output_aliases=aliases,
        compiler_params=params(),
        cost_estimate=cost(16 * size * size * BLOCK, 16 * size * size + 16 * size * BLOCK),
        name="multiply",
    )(*scalars, at, inner, *operands)


def ring_order(n):
    return list(range(0, 1)) + list(range(1, n, 2)) + [i for i in range(n - 1, 0, -1) if i % 2 == 0]


def branch(size, nrow, ncol, t2, ints, occ, virt, win, eps_virt, occ_rows, col_energy, at, sources):
    scalars = (occ, virt, win)
    order = ring_order(nrow)
    ring = [(order[i], order[(i + 1) % nrow]) for i in range(nrow)]
    swap = [(c, c ^ 1) for c in range(ncol)]

    rows = ints.reshape(2, VIR_CAP // 2, 2, OCC_CAP, BLOCK)
    parity = at[1] & 1
    mine = lax.dynamic_index_in_dim(rows, parity, 2, keepdims=False).reshape(BLOCK, BLOCK)
    other = lax.dynamic_index_in_dim(rows, 1 - parity, 2, keepdims=False).reshape(BLOCK, BLOCK)
    other = lax.ppermute(other, "col", swap)

    pieces = prep(size, scalars, t2)
    held = []
    for s in range(2):
        moved = lax.all_to_all(pieces[s], "col", split_axis=0, concat_axis=0, tiled=True)
        held.append(compact_rows(size, s, scalars, at, moved))
    small = compact_ints(size, scalars, at, mine, other)
    panel = lax.all_gather(small, "col", axis=0, tiled=False).reshape(ncol // 2, 2, size, 2 * size)
    acc = None
    for step in range(nrow):
        sib = [lax.ppermute(x, "col", swap) for x in held]
        later = None
        if step < nrow - 1:
            later = [lax.ppermute(x, "row", ring) for x in held]
        inner = sources[step : step + 1]
        energies = (eps_virt, occ_rows, col_energy) if step == nrow - 1 else None
        acc = multiply(size, scalars, at, inner, panel, held, sib, acc, energies)
        held = later
    return acc


def live_device(nrow, ncol, t2, ints, eps_occ, eps_virt, occ, virt, win):
    row, col = lax.axis_index("row"), lax.axis_index("col")
    irreps = jnp.arange(NIRREP, dtype=I32)
    partner_hot = (irreps ^ win[0])[:, None] == irreps[None, :]
    virt_of = jnp.sum(jnp.where(partner_hot, virt[None, :], 0), axis=1)
    even = (occ * ((virt_of + 1) >> 1)).reshape(NIRREP // 2, 2)
    most = jnp.max(jnp.sum(even, axis=1))
    index = jnp.sum((most > jnp.array(SIZES[:-1], I32)).astype(I32))
    occ_rows = lax.dynamic_slice(eps_occ, (2 * row, 0), (2, OCC_CAP)).reshape(2, OCC_CAP, 1)
    col_occ = lax.dynamic_slice(eps_occ, (col, 0), (1, OCC_CAP))
    col_virt = lax.dynamic_slice(eps_virt, (col ^ win[0], 0), (1, VIR_CAP))
    col_energy = (col_occ[:, None, :] - col_virt[:, :, None]).reshape(1, BLOCK)
    at = jnp.stack([row, col]).astype(I32)
    order = ring_order(nrow)
    table = [[order[(order.index(z) - t) % nrow] for t in range(nrow)] for z in range(nrow)]
    sources = lax.dynamic_slice(jnp.array(table, I32), (row, 0), (1, nrow)).reshape(nrow)
    operands = (t2, ints, occ, virt, win, eps_virt, occ_rows, col_energy, at, sources)
    return lax.switch(index, [functools.partial(branch, size, nrow, ncol) for size in SIZES], *operands)


def ph_vectors(eps_occ, eps_virt, occ_count, virt_count, window_irrep):
    irreps = jnp.arange(NIRREP, dtype=I32)
    partner = jnp.bitwise_xor(irreps, window_irrep[0])
    onehot = partner[:, None] == irreps[None, :]
    virt_rows = jnp.dot(onehot.astype(F32), eps_virt, precision=lax.Precision.HIGHEST)
    virt_live = jnp.sum(jnp.where(onehot, virt_count[None, :], 0), axis=1)
    energy = eps_occ[:, None, :] - virt_rows[:, :, None]
    slots_occ = jnp.arange(OCC_CAP, dtype=I32)
    slots_virt = jnp.arange(VIR_CAP, dtype=I32)
    live = (slots_occ[None, None, :] < occ_count[:, None, None]) & (
        slots_virt[None, :, None] < virt_live[:, None, None]
    )
    return (energy, live)


def any_device(t2_pairs, cycle_ints, eps_occ, eps_virt, occ_count, virt_count, window_irrep):
    irrep_local = t2_pairs.shape[0]
    virt_local = t2_pairs.shape[4]
    total = NIRREP * VIR_CAP * OCC_CAP
    energy, live = ph_vectors(eps_occ, eps_virt, occ_count, virt_count, window_irrep)
    row_index = lax.axis_index("row")
    col_index = lax.axis_index("col")
    zero_index = jnp.int32(0)
    source_live = lax.dynamic_slice(
        live,
        (row_index * irrep_local, col_index * virt_local, zero_index),
        (irrep_local, virt_local, OCC_CAP),
    )
    full_live = live.reshape(-1)
    ordered = jnp.transpose(t2_pairs, (0, 4, 2, 1, 5, 3)).reshape(
        irrep_local, virt_local, OCC_CAP, total
    )
    keep = source_live[:, :, :, None] & full_live[None, None, None, :]
    ordered = jnp.where(keep, ordered, jnp.zeros_like(ordered))
    moved = lax.all_to_all(ordered, "col", split_axis=3, concat_axis=1, tiled=True)
    amp_local = moved.reshape(irrep_local * VIR_CAP * OCC_CAP, moved.shape[3])
    amp_panel = lax.all_gather(amp_local, "row", axis=0, tiled=True)
    ints_panel = lax.all_gather(cycle_ints, "col", axis=1, tiled=True)
    cycle = jnp.dot(ints_panel, amp_panel, preferred_element_type=F32)
    rows_here, cols_here = cycle.shape
    flat_energy = energy.reshape(-1)
    row_start, col_start = row_index * rows_here, col_index * cols_here
    row_energy = lax.dynamic_slice_in_dim(flat_energy, row_start, rows_here, 0)
    col_energy = lax.dynamic_slice_in_dim(flat_energy, col_start, cols_here, 0)
    row_live = lax.dynamic_slice_in_dim(full_live, row_start, rows_here, 0)
    col_live = lax.dynamic_slice_in_dim(full_live, col_start, cols_here, 0)
    denom = row_energy[:, None] + col_energy[None, :]
    return jnp.where(row_live[:, None] & col_live[None, :], cycle / denom, F32(0.0))


def solution(mesh):
    nrow, ncol = mesh.shape["row"], mesh.shape["col"]
    placed = (P("row", None, None, None, "col", None), P("row", "col"), P(), P(), P(), P(), P())
    body = any_device
    if 2 * nrow == NIRREP and ncol == NIRREP:
        body = functools.partial(live_device, nrow, ncol)
    return jax.shard_map(body, mesh=mesh, in_specs=placed, out_specs=P("row", "col"), check_vma=False)
```

```python
import functools

import jax
import jax.numpy as jnp
from jax import lax
from jax.experimental import pallas as pl
from jax.experimental.pallas import tpu as pltpu
from jax.sharding import PartitionSpec as P

NIRREP = 8
OCC_CAP = 16
VIR_CAP = 64
BLOCK = VIR_CAP * OCC_CAP
SIZES = (512, 640, 768, 896, 1024)
F32 = jnp.float32
BF16 = jnp.bfloat16
I32 = jnp.int32
VMEM_BYTES = 56 * 1024 * 1024


def iota(shape, dim):
    return lax.broadcasted_iota(I32, shape, dim)


def params():
    return pltpu.CompilerParams(vmem_limit_bytes=VMEM_BYTES)


def cost(flops, nbytes):
    return pl.CostEstimate(flops=flops, bytes_accessed=nbytes, transcendentals=0)


def pair_scalars(occ, virt, win, pair):
    first = 2 * pair
    o_a, o_b = occ[first], occ[first + 1]
    v_a, v_b = virt[first ^ win[0]], virt[(first + 1) ^ win[0]]
    return (o_a, o_b), (v_a, v_b), (o_a * ((v_a + 1) >> 1), o_a * (v_a >> 1))


def place(q, p, second, counts):
    (o_a, o_b), (v_a, v_b), (start_even, start_odd) = counts
    o = jnp.where(second, o_b, o_a)
    v = jnp.where(second, v_b, v_a)
    start = jnp.where(second, jnp.where((q & 1) == 0, start_even, start_odd), 0)
    return jnp.where((p < o) & (q < v), start + (q >> 1) * o + p, -1)


def one_hot(left, right):
    return jnp.where(left == right, 1.0, 0.0).astype(BF16)


def dot(a, b):
    return jnp.dot(a, b, preferred_element_type=F32)


def prep_kernel(size, occ, virt, win, at, t2_ref, even_ref, odd_ref, at_ref, x_ref):
    at_ref[0] = at[0]
    at_ref[1] = at[1]
    counts = pair_scalars(occ, virt, win, pl.program_id(0))
    row = iota((256, 1), 0)
    source = (((row >> 6) & 1) << 7) | (((row >> 2) & 15) << 3) | ((row & 3) << 1) | (row >> 7)
    by_parity = one_hot(iota((256, 256), 1), source)
    targets = []
    for half in range(2):
        for group in range(4):
            parts = [
                t2_ref[:, half, :, 4 * group + i].astype(F32).reshape(256, VIR_CAP) for i in range(4)
            ]
            x = jnp.concatenate(parts, axis=1).astype(BF16)
            at = (4 * half + group) * 256
            x_ref[:, at : at + 256] = dot(by_parity, x).astype(BF16)
            r = iota((256, 1), 0)
            p, q = 4 * group + (r >> 6), r & 63
            spot = place(q, p, half == 1, counts)
            targets.append(jnp.where(spot >= 0, spot + (q & 1) * size, -1))
    for start in range(0, 2 * size, 256):
        acc = jnp.zeros((256, 256), F32)
        lane = iota((256, 256), 1) + start
        for chunk in range(8):
            acc += dot(x_ref[:, chunk * 256 : chunk * 256 + 256], one_hot(targets[chunk], lane))
        acc = acc.astype(BF16)
        for part in range(2):
            at = start + 128 * part
            core, col = at // size, at % size
            tile = acc[:, 128 * part : 128 * part + 128]
            even_ref[core, :, col : col + 128] = tile[:128]
            odd_ref[core, :, col : col + 128] = tile[128:]


def prep(size, scalars, at, t2):
    shape = jax.ShapeDtypeStruct((NIRREP, 128, size), BF16)
    block = pl.BlockSpec((2, 128, size), lambda k, *_: (k, 0, 0))
    return pl.pallas_call(
        functools.partial(prep_kernel, size),
        out_shape=(shape, shape, jax.ShapeDtypeStruct((2,), I32)),
        grid_spec=pltpu.PrefetchScalarGridSpec(
            num_scalar_prefetch=4,
            grid=(NIRREP // 2,),
            in_specs=[
                pl.BlockSpec((2, 2, OCC_CAP, OCC_CAP, 8, VIR_CAP), lambda k, *_: (0, k, 0, 0, 0, 0))
            ],
            out_specs=[block, block, pl.BlockSpec(memory_space=pltpu.SMEM)],
            scratch_shapes=[pltpu.VMEM((256, 2048), BF16)],
        ),
        compiler_params=params(),
        cost_estimate=cost(2 * 4 * 256 * 2048 * 2 * size, 12 * 2**20),
        name="prep_amplitudes",
    )(*scalars, at, t2)


def rows_kernel(rows, parity, occ, virt, win, at, x_ref, passed_in, out_ref, passed_out, sel_ref):
    counts = pair_scalars(occ, virt, win, at[0])
    i = iota((1, BLOCK), 1)
    q = 8 * (i >> 7) + 2 * (i & 3) + parity
    spot = place(q, (i >> 2) & 15, ((i >> 6) & 1) == 1, counts)
    for r in range(0, rows, 64):
        sel_ref[r : r + 64, :] = one_hot(iota((64, BLOCK), 0) + r, spot)
    out_ref[...] = dot(sel_ref[...], x_ref[...].reshape(BLOCK, x_ref.shape[2])).astype(BF16)


def compact_rows(rows, cols, parity, scalars, at, x, passed):
    whole = pl.BlockSpec(memory_space=pl.ANY)
    return pl.pallas_call(
        functools.partial(rows_kernel, rows, parity),
        out_shape=(
            jax.ShapeDtypeStruct((rows, cols), BF16),
            jax.ShapeDtypeStruct(passed.shape, passed.dtype),
        ),
        grid_spec=pltpu.PrefetchScalarGridSpec(
            num_scalar_prefetch=4,
            grid=(1,),
            in_specs=[pl.BlockSpec((NIRREP, 128, cols), lambda n, *_: (0, 0, 0)), whole],
            out_specs=[pl.BlockSpec((rows, cols), lambda n, *_: (0, 0)), whole],
            scratch_shapes=[pltpu.VMEM((rows, BLOCK), BF16)],
        ),
        input_output_aliases={5: 1},
        compiler_params=params(),
        cost_estimate=cost(4 * rows * BLOCK * cols, 4 * rows * BLOCK),
        name="compact_rows",
    )(*scalars, at, x, passed)


def ints_kernel(rows, cols, occ, virt, win, at, mine_ref, other_ref, out_ref, sel_ref, cols_ref):
    plane, dev = at[0], at[1]
    parity = dev & 1

    @pl.when(pl.program_id(0) == 0)
    def _():
        counts = pair_scalars(occ, virt, win, plane)
        i = iota((1, BLOCK), 1)
        q = 2 * ((i >> 4) & 31) + parity
        spot = place(q, i & 15, (i >> 9) == 1, counts)
        for r in range(0, rows, 64):
            sel_ref[r : r + 64, :] = one_hot(iota((64, BLOCK), 0) + r, spot)

    counts = pair_scalars(occ, virt, win, dev >> 1)
    i = iota((BLOCK, 1), 0)
    q, p = i >> 4, i & 15
    lane = iota((BLOCK, 256), 1) + pl.program_id(0) * 256
    acc = None
    for ref, second in ((mine_ref, parity == 1), (other_ref, parity == 0)):
        spot = place(q, p, second, counts)
        target = jnp.where(spot >= 0, spot + (q & 1) * cols, -1)
        part = dot(ref[...], one_hot(target, lane))
        acc = part if acc is None else acc + part
    cols_ref[...] = acc.astype(BF16)
    out_ref[...] = dot(sel_ref[...], cols_ref[...]).astype(BF16)


def compact_ints(rows, cols, scalars, at, mine, other):
    whole = pl.BlockSpec((BLOCK, BLOCK), lambda n, *_: (0, 0))
    return pl.pallas_call(
        functools.partial(ints_kernel, rows, cols),
        out_shape=jax.ShapeDtypeStruct((rows, 2 * cols), BF16),
        grid_spec=pltpu.PrefetchScalarGridSpec(
            num_scalar_prefetch=4,
            grid=(2 * cols // 256,),
            in_specs=[whole, whole],
            out_specs=pl.BlockSpec((rows, 256), lambda n, *_: (0, n)),
            scratch_shapes=[pltpu.VMEM((rows, BLOCK), BF16), pltpu.VMEM((BLOCK, 256), BF16)],
        ),
        compiler_params=params(),
        cost_estimate=cost(16 * BLOCK * BLOCK * cols, 4 * BLOCK * BLOCK + 4 * rows * cols),
        name="compact_ints",
    )(*scalars, at, mine, other)


def column_selections(cols, occ, virt, win, dev):
    parity = dev & 1
    counts = pair_scalars(occ, virt, win, dev >> 1)
    i = iota((1, 256), 1) + pl.program_id(0) * 256
    q = i >> 4
    spot = place(q, i & 15, parity == 1, counts)
    r = iota((cols, 256), 0)
    own = one_hot(r, jnp.where((q & 1) == parity, spot, -1))
    sib = one_hot(r, jnp.where((q & 1) == parity, -1, spot))
    return own, sib


def widened(own_ref, sib_ref, selections):
    return (dot(own_ref[...], selections[0]) + dot(sib_ref[...], selections[1])).astype(BF16)


def widen_kernel(rows, cols, occ, virt, win, at, t0, t1, s0, s1, *refs):
    wide_ref = refs[-1]
    selections = column_selections(cols, occ, virt, win, at[1])
    for piece, (own, sib) in enumerate(((t0, s0), (t1, s1))):
        wide_ref[0, piece * cols : piece * cols + rows, :] = widened(own, sib, selections)
        if rows < cols:
            wide_ref[0, piece * cols + rows : (piece + 1) * cols, :] = jnp.zeros((cols - rows, 256), BF16)


def widen(rows, cols, slot, slots, scalars, at, own, sib, wide=None):
    square = pl.BlockSpec((rows, cols), lambda n, *_: (0, 0))
    operands = [*own, *sib]
    in_specs = [square] * 4
    aliases = {}
    if wide is not None:
        operands.append(wide)
        in_specs.append(pl.BlockSpec(memory_space=pl.ANY))
        aliases = {8: 0}
    return pl.pallas_call(
        functools.partial(widen_kernel, rows, cols),
        out_shape=jax.ShapeDtypeStruct((slots, 2 * cols, BLOCK), BF16),
        grid_spec=pltpu.PrefetchScalarGridSpec(
            num_scalar_prefetch=4,
            grid=(BLOCK // 256,),
            in_specs=in_specs,
            out_specs=pl.BlockSpec((1, 2 * cols, 256), lambda n, *_: (slot, 0, n)),
        ),
        input_output_aliases=aliases,
        compiler_params=params(),
        cost_estimate=cost(16 * rows * cols * BLOCK, 8 * rows * cols + 4 * cols * BLOCK),
        name="widen",
    )(*scalars, at, *operands)


def product_kernel(inner, ints_ref, wide_ref, acc_ref):
    step = pl.program_id(0)
    at = pl.ds(pl.multiple_of(pl.program_id(1) * 256, 256), 256)

    @pl.when(step == 0)
    def _():
        for half in range(2):
            acc_ref[half, :, at] = dot(ints_ref[0, half], wide_ref[0])

    @pl.when(step > 0)
    def _():
        for half in range(2):
            acc_ref[half, :, at] += dot(ints_ref[0, half], wide_ref[0])


def product(rows, cols, inner, ints, wide):
    slots = wide.shape[0]
    return pl.pallas_call(
        product_kernel,
        out_shape=jax.ShapeDtypeStruct((2, rows, BLOCK), F32),
        grid_spec=pltpu.PrefetchScalarGridSpec(
            num_scalar_prefetch=1,
            grid=(slots, BLOCK // 256),
            in_specs=[
                pl.BlockSpec((1, 2, rows, 2 * cols), lambda t, n, k: (k[t], 0, 0, 0)),
                pl.BlockSpec((1, 2 * cols, 256), lambda t, n, k: (t, 0, n)),
            ],
            out_specs=pl.BlockSpec((2, rows, BLOCK), lambda t, n, k: (0, 0, 0)),
        ),
        compiler_params=params(),
        cost_estimate=cost(16 * slots * rows * cols * BLOCK, slots * 4 * cols * (rows + BLOCK)),
        name="product",
    )(inner, ints, wide)


def piece_kernel(rows, cols, occ, virt, win, at, inner, ints_ref, own_ref, sib_ref, old_ref, acc_ref):
    wide = widened(own_ref, sib_ref, column_selections(cols, occ, virt, win, at[1]))
    for half in range(2):
        acc_ref[half] = old_ref[half] + dot(ints_ref[0, half][:, :rows], wide)


def last_kernel(
    rows, cols, occ, virt, win, at, inner, ints_ref, own_ref, sib_ref, old_ref, evirt, eocc_ref, ecol_ref, out_ref, sum_ref
):
    plane, dev = at[0], at[1]
    wide = widened(own_ref, sib_ref, column_selections(cols, occ, virt, win, dev))
    for half in range(2):
        sum_ref[half, :rows, :] = old_ref[half] + dot(ints_ref[0, half][:, :rows], wide)
    i = iota((1, 256), 1) + pl.program_id(0) * 256
    col_live = ((i & 15) < occ[dev]) & ((i >> 4) < virt[dev ^ win[0]])
    col_energy = ecol_ref[...]
    _, _, starts = pair_scalars(occ, virt, win, plane)
    p = iota((OCC_CAP, 1), 0)
    for h in range(2):
        irrep = 2 * plane + h
        o, partner = occ[irrep], irrep ^ win[0]
        v = virt[partner]
        occ_energy = eocc_ref[h]
        row_live = (p < o) & col_live
        for q in range(VIR_CAP):
            start = (q >> 1) * o
            if h == 1:
                start = start + starts[q & 1]
            start = jnp.minimum(start, rows)
            block = sum_ref[q & 1, pl.ds(pl.multiple_of((start >> 3) << 3, 8), OCC_CAP + 8), :]
            block = pltpu.roll(block, OCC_CAP + 8 - (start & 7), 0)[:OCC_CAP]
            denom = (occ_energy - evirt[partner, q]) + col_energy
            at_row = (h * VIR_CAP + q) * OCC_CAP
            out_ref[at_row : at_row + OCC_CAP, :] = jnp.where(row_live & (q < v), block / denom, 0.0)


def piece_product(rows, cols, piece, scalars, at, inner, ints, own, sib, acc, energies=None):
    square = pl.BlockSpec((rows, cols), lambda n, *_: (0, 0))
    tile = pl.BlockSpec((2, rows, 256), lambda n, *_: (0, 0, n))
    in_specs = [
        pl.BlockSpec((1, 2, rows, cols), lambda n, o, v, w, a, k: (k[0], 0, 0, piece)),
        square, square, tile,
    ]
    operands = [ints, own, sib, acc]
    kernel, scratch, aliases = piece_kernel, [], {8: 0}
    out_shape, out_specs = jax.ShapeDtypeStruct((2, rows, BLOCK), F32), tile
    if energies is not None:
        kernel, aliases = last_kernel, {}
        in_specs += [
            pl.BlockSpec(memory_space=pltpu.SMEM),
            pl.BlockSpec((2, OCC_CAP, 1), lambda n, *_: (0, 0, 0)),
            pl.BlockSpec((1, 256), lambda n, *_: (0, n)),
        ]
        operands += list(energies)
        scratch = [pltpu.VMEM((2, rows + OCC_CAP + 8, 256), F32)]
        out_shape = jax.ShapeDtypeStruct((2 * BLOCK, BLOCK), F32)
        out_specs = pl.BlockSpec((2 * BLOCK, 256), lambda n, *_: (0, n))
    return pl.pallas_call(
        functools.partial(kernel, rows, cols),
        out_shape=out_shape,
        grid_spec=pltpu.PrefetchScalarGridSpec(
            num_scalar_prefetch=5,
            grid=(BLOCK // 256,),
            in_specs=in_specs,
            out_specs=out_specs,
            scratch_shapes=scratch,
        ),
        input_output_aliases=aliases,
        compiler_params=params(),
        cost_estimate=cost(16 * rows * cols * BLOCK, 8 * rows * cols + 16 * rows * BLOCK),
        name="piece_product",
    )(*scalars, at, inner, *operands)


def after_kernel(x_in, y_in, x_out, y_out):
    pass


def after(x, y):
    whole = pl.BlockSpec(memory_space=pl.ANY)
    return pl.pallas_call(
        after_kernel,
        out_shape=tuple(jax.ShapeDtypeStruct(z.shape, z.dtype) for z in (x, y)),
        in_specs=[whole, whole],
        out_specs=(whole, whole),
        input_output_aliases={0: 0, 1: 1},
        name="after",
    )(x, y)


def ring_order(n):
    return list(range(0, 1)) + list(range(1, n, 2)) + [i for i in range(n - 1, 0, -1) if i % 2 == 0]


def branch(rows, nrow, ncol, t2, ints, occ, virt, win, eps_virt, occ_rows, col_energy, at, sources):
    cols = -(-rows // 128) * 128
    scalars = (occ, virt, win)
    order = ring_order(nrow)
    ring = [(order[i], order[(i + 1) % nrow]) for i in range(nrow)]
    swap = [(c, c ^ 1) for c in range(ncol)]

    def to_sibling(x):
        return lax.ppermute(x, "col", swap)

    def around(x):
        return lax.ppermute(x, "row", ring)

    def exchange(x):
        return lax.all_to_all(x, "col", split_axis=0, concat_axis=0, tiled=True)

    even, odd, then = prep(cols, scalars, at, t2)
    even = exchange(even)
    by_parity = ints.reshape(2, VIR_CAP // 2, 2, OCC_CAP, BLOCK)
    parity = then[1] & 1
    mine = lax.dynamic_index_in_dim(by_parity, parity, 2, keepdims=False).reshape(BLOCK, BLOCK)
    other = lax.dynamic_index_in_dim(by_parity, 1 - parity, 2, keepdims=False).reshape(BLOCK, BLOCK)
    small = compact_ints(rows, cols, scalars, at, mine, to_sibling(other))
    even, odd = compact_rows(rows, cols, 0, scalars, at, even, odd)
    odd, small = compact_rows(rows, cols, 1, scalars, at, exchange(odd), small)
    panel = lax.all_gather(small, "col", axis=0, tiled=False).reshape(ncol // 2, 2, rows, 2 * cols)

    held = [even, odd]
    wide = None
    for step in range(nrow - 1):
        later = [around(x) for x in held]
        sib = [to_sibling(x) for x in held]
        wide = widen(rows, cols, step, nrow - 1, scalars, at, held, sib, wide)
        held = later
    acc = product(rows, cols, sources[: nrow - 1], panel, wide)
    last = sources[nrow - 1 :]
    own, acc = after(held[0], acc)
    acc = piece_product(rows, cols, 0, scalars, at, last, panel, own, to_sibling(own), acc)
    own, acc = after(held[1], acc)
    energies = (eps_virt, occ_rows, col_energy)
    return piece_product(rows, cols, 1, scalars, at, last, panel, own, to_sibling(own), acc, energies)


def live_device(nrow, ncol, t2, ints, eps_occ, eps_virt, occ, virt, win):
    row, col = lax.axis_index("row"), lax.axis_index("col")
    irreps = jnp.arange(NIRREP, dtype=I32)
    partner_hot = (irreps ^ win[0])[:, None] == irreps[None, :]
    virt_of = jnp.sum(jnp.where(partner_hot, virt[None, :], 0), axis=1)
    even = (occ * ((virt_of + 1) >> 1)).reshape(NIRREP // 2, 2)
    most = jnp.max(jnp.sum(even, axis=1))
    index = jnp.sum((most > jnp.array(SIZES[:-1], I32)).astype(I32))
    occ_rows = lax.dynamic_slice(eps_occ, (2 * row, 0), (2, OCC_CAP)).reshape(2, OCC_CAP, 1)
    col_occ = lax.dynamic_slice(eps_occ, (col, 0), (1, OCC_CAP))
    col_virt = lax.dynamic_slice(eps_virt, (col ^ win[0], 0), (1, VIR_CAP))
    col_energy = (col_occ[:, None, :] - col_virt[:, :, None]).reshape(1, BLOCK)
    at = jnp.stack([row, col]).astype(I32)
    order = ring_order(nrow)
    table = [[order[(order.index(z) - t) % nrow] for t in range(nrow)] for z in range(nrow)]
    sources = lax.dynamic_slice(jnp.array(table, I32), (row, 0), (1, nrow)).reshape(nrow)
    operands = (t2, ints, occ, virt, win, eps_virt, occ_rows, col_energy, at, sources)
    return lax.switch(index, [functools.partial(branch, size, nrow, ncol) for size in SIZES], *operands)


def ph_vectors(eps_occ, eps_virt, occ_count, virt_count, window_irrep):
    irreps = jnp.arange(NIRREP, dtype=I32)
    partner = jnp.bitwise_xor(irreps, window_irrep[0])
    onehot = partner[:, None] == irreps[None, :]
    virt_rows = jnp.dot(onehot.astype(F32), eps_virt, precision=lax.Precision.HIGHEST)
    virt_live = jnp.sum(jnp.where(onehot, virt_count[None, :], 0), axis=1)
    energy = eps_occ[:, None, :] - virt_rows[:, :, None]
    slots_occ = jnp.arange(OCC_CAP, dtype=I32)
    slots_virt = jnp.arange(VIR_CAP, dtype=I32)
    live = (slots_occ[None, None, :] < occ_count[:, None, None]) & (
        slots_virt[None, :, None] < virt_live[:, None, None]
    )
    return (energy, live)


def any_device(t2_pairs, cycle_ints, eps_occ, eps_virt, occ_count, virt_count, window_irrep):
    irrep_local = t2_pairs.shape[0]
    virt_local = t2_pairs.shape[4]
    total = NIRREP * VIR_CAP * OCC_CAP
    energy, live = ph_vectors(eps_occ, eps_virt, occ_count, virt_count, window_irrep)
    row_index = lax.axis_index("row")
    col_index = lax.axis_index("col")
    zero_index = jnp.int32(0)
    source_live = lax.dynamic_slice(
        live,
        (row_index * irrep_local, col_index * virt_local, zero_index),
        (irrep_local, virt_local, OCC_CAP),
    )
    full_live = live.reshape(-1)
    ordered = jnp.transpose(t2_pairs, (0, 4, 2, 1, 5, 3)).reshape(
        irrep_local, virt_local, OCC_CAP, total
    )
    keep = source_live[:, :, :, None] & full_live[None, None, None, :]
    ordered = jnp.where(keep, ordered, jnp.zeros_like(ordered))
    moved = lax.all_to_all(ordered, "col", split_axis=3, concat_axis=1, tiled=True)
    amp_local = moved.reshape(irrep_local * VIR_CAP * OCC_CAP, moved.shape[3])
    amp_panel = lax.all_gather(amp_local, "row", axis=0, tiled=True)
    ints_panel = lax.all_gather(cycle_ints, "col", axis=1, tiled=True)
    cycle = jnp.dot(ints_panel, amp_panel, preferred_element_type=F32)
    rows_here, cols_here = cycle.shape
    flat_energy = energy.reshape(-1)
    row_start, col_start = row_index * rows_here, col_index * cols_here
    row_energy = lax.dynamic_slice_in_dim(flat_energy, row_start, rows_here, 0)
    col_energy = lax.dynamic_slice_in_dim(flat_energy, col_start, cols_here, 0)
    row_live = lax.dynamic_slice_in_dim(full_live, row_start, rows_here, 0)
    col_live = lax.dynamic_slice_in_dim(full_live, col_start, cols_here, 0)
    denom = row_energy[:, None] + col_energy[None, :]
    return jnp.where(row_live[:, None] & col_live[None, :], cycle / denom, F32(0.0))


def solution(mesh):
    nrow, ncol = mesh.shape["row"], mesh.shape["col"]
    placed = (P("row", None, None, None, "col", None), P("row", "col"), P(), P(), P(), P(), P())
    body = any_device
    if 2 * nrow == NIRREP and ncol == NIRREP:
        body = functools.partial(live_device, nrow, ncol)
    return jax.shard_map(body, mesh=mesh, in_specs=placed, out_specs=P("row", "col"), check_vma=False)
```

```python
import functools

import jax
import jax.numpy as jnp
from jax import lax
from jax.experimental import pallas as pl
from jax.experimental.pallas import tpu as pltpu
from jax.sharding import PartitionSpec as P

NIRREP = 8
OCC_CAP = 16
VIR_CAP = 64
BLOCK = VIR_CAP * OCC_CAP
SIZES = (512, 576, 640, 704, 736, 768, 832, 896, 960, 1024)
F32 = jnp.float32
BF16 = jnp.bfloat16
I32 = jnp.int32
VMEM_BYTES = 56 * 1024 * 1024


def iota(shape, dim):
    return lax.broadcasted_iota(I32, shape, dim)


def params():
    return pltpu.CompilerParams(vmem_limit_bytes=VMEM_BYTES)


def cost(flops, nbytes):
    return pl.CostEstimate(flops=flops, bytes_accessed=nbytes, transcendentals=0)


def pair_scalars(occ, virt, win, pair):
    first = 2 * pair
    o_a, o_b = occ[first], occ[first + 1]
    v_a, v_b = virt[first ^ win[0]], virt[(first + 1) ^ win[0]]
    return (o_a, o_b), (v_a, v_b), (o_a * ((v_a + 1) >> 1), o_a * (v_a >> 1))


def place(q, p, second, counts):
    (o_a, o_b), (v_a, v_b), (start_even, start_odd) = counts
    o = jnp.where(second, o_b, o_a)
    v = jnp.where(second, v_b, v_a)
    start = jnp.where(second, jnp.where((q & 1) == 0, start_even, start_odd), 0)
    return jnp.where((p < o) & (q < v), start + (q >> 1) * o + p, -1)


def one_hot(left, right):
    return jnp.where(left == right, 1.0, 0.0).astype(BF16)


def dot(a, b):
    return jnp.dot(a, b, preferred_element_type=F32)


def prep_kernel(size, occ, virt, win, at, t2_ref, even_ref, odd_ref, at_ref, x_ref):
    at_ref[0] = at[0]
    at_ref[1] = at[1]
    counts = pair_scalars(occ, virt, win, pl.program_id(0))
    row = iota((256, 1), 0)
    source = (((row >> 6) & 1) << 7) | (((row >> 2) & 15) << 3) | ((row & 3) << 1) | (row >> 7)
    by_parity = one_hot(iota((256, 256), 1), source)
    targets = []
    for half in range(2):
        for group in range(4):
            parts = [
                t2_ref[:, half, :, 4 * group + i].astype(F32).reshape(256, VIR_CAP) for i in range(4)
            ]
            x = jnp.concatenate(parts, axis=1).astype(BF16)
            at = (4 * half + group) * 256
            x_ref[:, at : at + 256] = dot(by_parity, x).astype(BF16)
            r = iota((256, 1), 0)
            p, q = 4 * group + (r >> 6), r & 63
            spot = place(q, p, half == 1, counts)
            targets.append(jnp.where(spot >= 0, spot + (q & 1) * size, -1))
    for start in range(0, 2 * size, 256):
        acc = jnp.zeros((256, 256), F32)
        lane = iota((256, 256), 1) + start
        for chunk in range(8):
            acc += dot(x_ref[:, chunk * 256 : chunk * 256 + 256], one_hot(targets[chunk], lane))
        acc = acc.astype(BF16)
        for part in range(2):
            at = start + 128 * part
            core, col = at // size, at % size
            tile = acc[:, 128 * part : 128 * part + 128]
            even_ref[core, :, col : col + 128] = tile[:128]
            odd_ref[core, :, col : col + 128] = tile[128:]


def prep(size, scalars, at, t2):
    shape = jax.ShapeDtypeStruct((NIRREP, 128, size), BF16)
    block = pl.BlockSpec((2, 128, size), lambda k, *_: (k, 0, 0))
    return pl.pallas_call(
        functools.partial(prep_kernel, size),
        out_shape=(shape, shape, jax.ShapeDtypeStruct((2,), I32)),
        grid_spec=pltpu.PrefetchScalarGridSpec(
            num_scalar_prefetch=4,
            grid=(NIRREP // 2,),
            in_specs=[
                pl.BlockSpec((2, 2, OCC_CAP, OCC_CAP, 8, VIR_CAP), lambda k, *_: (0, k, 0, 0, 0, 0))
            ],
            out_specs=[block, block, pl.BlockSpec(memory_space=pltpu.SMEM)],
            scratch_shapes=[pltpu.VMEM((256, 2048), BF16)],
        ),
        compiler_params=params(),
        cost_estimate=cost(2 * 4 * 256 * 2048 * 2 * size, 12 * 2**20),
        name="prep_amplitudes",
    )(*scalars, at, t2)


def rows_kernel(rows, parity, count, occ, virt, win, at, x_ref, *refs):
    out_ref, sel_ref = refs[count], refs[-1]
    counts = pair_scalars(occ, virt, win, at[0])
    i = iota((1, BLOCK), 1)
    q = 8 * (i >> 7) + 2 * (i & 3) + parity
    spot = place(q, (i >> 2) & 15, ((i >> 6) & 1) == 1, counts)
    for r in range(0, rows, 32):
        sel_ref[r : r + 32, :] = one_hot(iota((32, BLOCK), 0) + r, spot)
    out_ref[...] = dot(sel_ref[...], x_ref[...].reshape(BLOCK, x_ref.shape[2])).astype(BF16)


def compact_rows(rows, cols, parity, scalars, at, x, passed=(), awaited=()):
    whole = pl.BlockSpec(memory_space=pl.ANY)
    return pl.pallas_call(
        functools.partial(rows_kernel, rows, parity, len(passed) + len(awaited)),
        out_shape=[jax.ShapeDtypeStruct((rows, cols), BF16)]
        + [jax.ShapeDtypeStruct(y.shape, y.dtype) for y in passed],
        grid_spec=pltpu.PrefetchScalarGridSpec(
            num_scalar_prefetch=4,
            grid=(1,),
            in_specs=[pl.BlockSpec((NIRREP, 128, cols), lambda n, *_: (0, 0, 0))]
            + [whole] * (len(passed) + len(awaited)),
            out_specs=[pl.BlockSpec((rows, cols), lambda n, *_: (0, 0))] + [whole] * len(passed),
            scratch_shapes=[pltpu.VMEM((rows, BLOCK), BF16)],
        ),
        input_output_aliases={5 + i: 1 + i for i in range(len(passed))},
        compiler_params=params(),
        cost_estimate=cost(4 * rows * BLOCK * cols, 4 * rows * BLOCK),
        name="compact_rows",
    )(*scalars, at, x, *passed, *awaited)


def ints_kernel(rows, cols, occ, virt, win, at, mine_ref, other_ref, out_ref, sel_ref, cols_ref):
    plane, dev = at[0], at[1]
    parity = dev & 1

    @pl.when(pl.program_id(0) == 0)
    def _():
        counts = pair_scalars(occ, virt, win, plane)
        i = iota((1, BLOCK), 1)
        q = 2 * ((i >> 4) & 31) + parity
        spot = place(q, i & 15, (i >> 9) == 1, counts)
        for r in range(0, rows, 32):
            sel_ref[r : r + 32, :] = one_hot(iota((32, BLOCK), 0) + r, spot)

    counts = pair_scalars(occ, virt, win, dev >> 1)
    i = iota((BLOCK, 1), 0)
    q, p = i >> 4, i & 15
    lane = iota((BLOCK, 256), 1) + pl.program_id(0) * 256
    acc = None
    for ref, second in ((mine_ref, parity == 1), (other_ref, parity == 0)):
        spot = place(q, p, second, counts)
        target = jnp.where(spot >= 0, spot + (q & 1) * cols, -1)
        part = dot(ref[...].reshape(BLOCK, BLOCK), one_hot(target, lane))
        acc = part if acc is None else acc + part
    cols_ref[...] = acc.astype(BF16)
    out_ref[...] = dot(sel_ref[...], cols_ref[...]).astype(BF16)


def compact_ints(rows, cols, scalars, at, mine, other):
    mine_spec = pl.BlockSpec(
        (2, VIR_CAP // 2, 1, OCC_CAP, BLOCK), lambda n, o, v, w, a: (0, 0, a[1] & 1, 0, 0)
    )
    whole = pl.BlockSpec((BLOCK, BLOCK), lambda n, *_: (0, 0))
    return pl.pallas_call(
        functools.partial(ints_kernel, rows, cols),
        out_shape=jax.ShapeDtypeStruct((rows, 2 * cols), BF16),
        grid_spec=pltpu.PrefetchScalarGridSpec(
            num_scalar_prefetch=4,
            grid=(2 * cols // 256,),
            in_specs=[mine_spec, whole],
            out_specs=pl.BlockSpec((rows, 256), lambda n, *_: (0, n)),
            scratch_shapes=[pltpu.VMEM((rows, BLOCK), BF16), pltpu.VMEM((BLOCK, 256), BF16)],
        ),
        compiler_params=params(),
        cost_estimate=cost(16 * BLOCK * BLOCK * cols, 4 * BLOCK * BLOCK + 4 * rows * cols),
        name="compact_ints",
    )(*scalars, at, mine, other)


def widen_tile(rows, cols, tile, occ, virt, win, dev, own_refs, sib_refs, wide_ref):
    parity = dev & 1
    counts = pair_scalars(occ, virt, win, dev >> 1)
    (o_a, o_b), _, (start_even, start_odd) = counts
    second = parity == 1
    o = jnp.where(second, o_b, o_a)
    i = iota((1, 256), 1) + tile * 256
    q = i >> 4
    spot = place(q, i & 15, second, counts)
    r = iota((256, 256), 0)
    picks = []
    for s in (parity, 1 - parity):
        start = jnp.where(second, jnp.where(s == 0, start_even, start_odd), 0) + 8 * tile * o
        start = jnp.minimum((start >> 7) << 7, cols - 256)
        window = pl.ds(pl.multiple_of(start, 128), 256)
        picks.append((window, one_hot(r + start, jnp.where((q & 1) == s, spot, -1))))
    for piece in range(2):
        x = dot(own_refs[piece][:, picks[0][0]], picks[0][1])
        x += dot(sib_refs[piece][:, picks[1][0]], picks[1][1])
        wide_ref[piece * cols : piece * cols + rows, :] = x.astype(BF16)
        if rows < cols:
            wide_ref[piece * cols + rows : (piece + 1) * cols, :] = jnp.zeros((cols - rows, 256), BF16)


def widen_kernel(rows, cols, occ, virt, win, at, t0, t1, s0, s1, *refs):
    widen_tile(rows, cols, pl.program_id(0), occ, virt, win, at[1], (t0, t1), (s0, s1), refs[-1].at[0])


def widen(rows, cols, slot, slots, scalars, at, own, sib, wide=None):
    square = pl.BlockSpec((rows, cols), lambda n, *_: (0, 0))
    operands = [*own, *sib]
    in_specs = [square] * 4
    aliases = {}
    if wide is not None:
        operands.append(wide)
        in_specs.append(pl.BlockSpec(memory_space=pl.ANY))
        aliases = {8: 0}
    return pl.pallas_call(
        functools.partial(widen_kernel, rows, cols),
        out_shape=jax.ShapeDtypeStruct((slots, 2 * cols, BLOCK), BF16),
        grid_spec=pltpu.PrefetchScalarGridSpec(
            num_scalar_prefetch=4,
            grid=(BLOCK // 256,),
            in_specs=in_specs,
            out_specs=pl.BlockSpec((1, 2 * cols, 256), lambda n, *_: (slot, 0, n)),
        ),
        input_output_aliases=aliases,
        compiler_params=params(),
        cost_estimate=cost(8 * rows * 512 * BLOCK, 8 * rows * cols + 4 * cols * BLOCK),
        name="widen",
    )(*scalars, at, *operands)


def ints_dot(ints_ref, wide):
    _, _, rows, width = ints_ref.shape
    return dot(ints_ref[0].reshape(2 * rows, width), wide).reshape(2, rows, 256)


def product_kernel(inner, ints_ref, wide_ref, acc_ref):
    at = pl.ds(pl.multiple_of(pl.program_id(1) * 256, 256), 256)

    @pl.when(pl.program_id(0) == 0)
    def _():
        acc_ref[:, :, at] = ints_dot(ints_ref, wide_ref[0])

    @pl.when(pl.program_id(0) > 0)
    def _():
        acc_ref[:, :, at] += ints_dot(ints_ref, wide_ref[0])


def product(rows, cols, inner, ints, wide):
    slots = wide.shape[0]
    return pl.pallas_call(
        product_kernel,
        out_shape=jax.ShapeDtypeStruct((2, rows, BLOCK), F32),
        grid_spec=pltpu.PrefetchScalarGridSpec(
            num_scalar_prefetch=1,
            grid=(slots, BLOCK // 256),
            in_specs=[
                pl.BlockSpec((1, 2, rows, 2 * cols), lambda t, n, k: (k[t], 0, 0, 0)),
                pl.BlockSpec((1, 2 * cols, 256), lambda t, n, k: (t, 0, n)),
            ],
            out_specs=pl.BlockSpec((2, rows, BLOCK), lambda t, n, k: (0, 0, 0)),
        ),
        compiler_params=params(),
        cost_estimate=cost(16 * slots * rows * cols * BLOCK, slots * 4 * cols * (rows + BLOCK)),
        name="product",
    )(inner, ints, wide)


def last_kernel(
    rows, cols, occ, virt, win, at, inner,
    ints_ref, t0, t1, s0, s1, old_ref, evirt, eocc_ref, ecol_ref, out_ref, wide_ref, sum_ref,
):
    plane, dev = at[0], at[1]
    widen_tile(rows, cols, pl.program_id(0), occ, virt, win, dev, (t0, t1), (s0, s1), wide_ref)
    sum_ref[:, :rows, :] = old_ref[...] + ints_dot(ints_ref, wide_ref[...])
    i = iota((1, 256), 1) + pl.program_id(0) * 256
    col_live = ((i & 15) < occ[dev]) & ((i >> 4) < virt[dev ^ win[0]])
    col_energy = ecol_ref[...]
    _, _, starts = pair_scalars(occ, virt, win, plane)
    p = iota((OCC_CAP, 1), 0)
    for h in range(2):
        irrep = 2 * plane + h
        o, partner = occ[irrep], irrep ^ win[0]
        v = virt[partner]
        occ_energy = eocc_ref[h]
        row_live = (p < o) & col_live
        for q in range(VIR_CAP):
            start = (q >> 1) * o
            if h == 1:
                start = start + starts[q & 1]
            start = jnp.minimum(start, rows)
            block = sum_ref[q & 1, pl.ds(pl.multiple_of((start >> 3) << 3, 8), OCC_CAP + 8), :]
            block = pltpu.roll(block, OCC_CAP + 8 - (start & 7), 0)[:OCC_CAP]
            denom = (occ_energy - evirt[partner, q]) + col_energy
            at_row = (h * VIR_CAP + q) * OCC_CAP
            out_ref[at_row : at_row + OCC_CAP, :] = jnp.where(row_live & (q < v), block / denom, 0.0)


def last(rows, cols, scalars, at, inner, ints, own, sib, acc, energies):
    square = pl.BlockSpec((rows, cols), lambda n, *_: (0, 0))
    return pl.pallas_call(
        functools.partial(last_kernel, rows, cols),
        out_shape=jax.ShapeDtypeStruct((2 * BLOCK, BLOCK), F32),
        grid_spec=pltpu.PrefetchScalarGridSpec(
            num_scalar_prefetch=5,
            grid=(BLOCK // 256,),
            in_specs=[
                pl.BlockSpec((1, 2, rows, 2 * cols), lambda n, o, v, w, a, k: (k[0], 0, 0, 0)),
                square, square, square, square,
                pl.BlockSpec((2, rows, 256), lambda n, *_: (0, 0, n)),
                pl.BlockSpec(memory_space=pltpu.SMEM),
                pl.BlockSpec((2, OCC_CAP, 1), lambda n, *_: (0, 0, 0)),
                pl.BlockSpec((1, 256), lambda n, *_: (0, n)),
            ],
            out_specs=pl.BlockSpec((2 * BLOCK, 256), lambda n, *_: (0, n)),
            scratch_shapes=[
                pltpu.VMEM((2 * cols, 256), BF16),
                pltpu.VMEM((2, rows + OCC_CAP + 8, 256), F32),
            ],
        ),
        compiler_params=params(),
        cost_estimate=cost(16 * rows * cols * BLOCK, 8 * rows * cols + 16 * rows * BLOCK),
        name="last_product",
    )(*scalars, at, inner, ints, *own, *sib, acc, *energies)


def after_kernel(x_in, y_in, z_in, x_out, y_out):
    pass


def after(x, y, z):
    whole = pl.BlockSpec(memory_space=pl.ANY)
    return pl.pallas_call(
        after_kernel,
        out_shape=tuple(jax.ShapeDtypeStruct(w.shape, w.dtype) for w in (x, y)),
        in_specs=[whole, whole, whole],
        out_specs=(whole, whole),
        input_output_aliases={0: 0, 1: 1},
        name="after",
    )(x, y, z)


def ring_order(n):
    return list(range(0, 1)) + list(range(1, n, 2)) + [i for i in range(n - 1, 0, -1) if i % 2 == 0]


def branch(rows, nrow, ncol, t2, ints, occ, virt, win, eps_virt, occ_rows, col_energy, at, sources):
    cols = -(-rows // 128) * 128
    scalars = (occ, virt, win)
    order = ring_order(nrow)
    ring = [(order[i], order[(i + 1) % nrow]) for i in range(nrow)]
    swap = [(c, c ^ 1) for c in range(ncol)]

    def to_sibling(x):
        return lax.ppermute(x, "col", swap)

    def around(x):
        return lax.ppermute(x, "row", ring)

    def exchange(x):
        return lax.all_to_all(x, "col", split_axis=0, concat_axis=0, tiled=True)

    even, odd, then = prep(cols, scalars, at, t2)
    even = exchange(even)
    mine = ints.reshape(2, VIR_CAP // 2, 2, OCC_CAP, BLOCK)
    other = lax.dynamic_index_in_dim(mine, 1 - (then[1] & 1), 2, keepdims=False).reshape(BLOCK, BLOCK)
    small = compact_ints(rows, cols, scalars, at, mine, to_sibling(other))
    even, odd, small = compact_rows(rows, cols, 0, scalars, at, even, passed=(odd, small))
    panel = lax.all_gather(small, "col", axis=0, tiled=False).reshape(ncol // 2, 2, rows, 2 * cols)
    even_next = around(even)
    (odd,) = compact_rows(rows, cols, 1, scalars, at, exchange(odd), awaited=(even_next,))

    held = [even, odd]
    wide = None
    for step in range(nrow - 1):
        later = [even_next if step == 0 else around(held[0]), around(held[1])]
        sib = [to_sibling(x) for x in held]
        wide = widen(rows, cols, step, nrow - 1, scalars, at, held, sib, wide)
        held = later
    acc = product(rows, cols, sources[: nrow - 1], panel, wide)
    own = after(held[0], held[1], acc)
    sib = [to_sibling(x) for x in own]
    energies = (eps_virt, occ_rows, col_energy)
    return last(rows, cols, scalars, at, sources[nrow - 1 :], panel, own, sib, acc, energies)


def live_device(nrow, ncol, t2, ints, eps_occ, eps_virt, occ, virt, win):
    row, col = lax.axis_index("row"), lax.axis_index("col")
    irreps = jnp.arange(NIRREP, dtype=I32)
    partner_hot = (irreps ^ win[0])[:, None] == irreps[None, :]
    virt_of = jnp.sum(jnp.where(partner_hot, virt[None, :], 0), axis=1)
    even = (occ * ((virt_of + 1) >> 1)).reshape(NIRREP // 2, 2)
    most = jnp.max(jnp.sum(even, axis=1))
    index = jnp.sum((most > jnp.array(SIZES[:-1], I32)).astype(I32))
    occ_rows = lax.dynamic_slice(eps_occ, (2 * row, 0), (2, OCC_CAP)).reshape(2, OCC_CAP, 1)
    col_occ = lax.dynamic_slice(eps_occ, (col, 0), (1, OCC_CAP))
    col_virt = lax.dynamic_slice(eps_virt, (col ^ win[0], 0), (1, VIR_CAP))
    col_energy = (col_occ[:, None, :] - col_virt[:, :, None]).reshape(1, BLOCK)
    at = jnp.stack([row, col]).astype(I32)
    order = ring_order(nrow)
    table = [[order[(order.index(z) - t) % nrow] for t in range(nrow)] for z in range(nrow)]
    sources = lax.dynamic_slice(jnp.array(table, I32), (row, 0), (1, nrow)).reshape(nrow)
    operands = (t2, ints, occ, virt, win, eps_virt, occ_rows, col_energy, at, sources)
    return lax.switch(index, [functools.partial(branch, size, nrow, ncol) for size in SIZES], *operands)


def ph_vectors(eps_occ, eps_virt, occ_count, virt_count, window_irrep):
    irreps = jnp.arange(NIRREP, dtype=I32)
    partner = jnp.bitwise_xor(irreps, window_irrep[0])
    onehot = partner[:, None] == irreps[None, :]
    virt_rows = jnp.dot(onehot.astype(F32), eps_virt, precision=lax.Precision.HIGHEST)
    virt_live = jnp.sum(jnp.where(onehot, virt_count[None, :], 0), axis=1)
    energy = eps_occ[:, None, :] - virt_rows[:, :, None]
    slots_occ = jnp.arange(OCC_CAP, dtype=I32)
    slots_virt = jnp.arange(VIR_CAP, dtype=I32)
    live = (slots_occ[None, None, :] < occ_count[:, None, None]) & (
        slots_virt[None, :, None] < virt_live[:, None, None]
    )
    return (energy, live)


def any_device(t2_pairs, cycle_ints, eps_occ, eps_virt, occ_count, virt_count, window_irrep):
    irrep_local = t2_pairs.shape[0]
    virt_local = t2_pairs.shape[4]
    total = NIRREP * VIR_CAP * OCC_CAP
    energy, live = ph_vectors(eps_occ, eps_virt, occ_count, virt_count, window_irrep)
    row_index = lax.axis_index("row")
    col_index = lax.axis_index("col")
    zero_index = jnp.int32(0)
    source_live = lax.dynamic_slice(
        live,
        (row_index * irrep_local, col_index * virt_local, zero_index),
        (irrep_local, virt_local, OCC_CAP),
    )
    full_live = live.reshape(-1)
    ordered = jnp.transpose(t2_pairs, (0, 4, 2, 1, 5, 3)).reshape(
        irrep_local, virt_local, OCC_CAP, total
    )
    keep = source_live[:, :, :, None] & full_live[None, None, None, :]
    ordered = jnp.where(keep, ordered, jnp.zeros_like(ordered))
    moved = lax.all_to_all(ordered, "col", split_axis=3, concat_axis=1, tiled=True)
    amp_local = moved.reshape(irrep_local * VIR_CAP * OCC_CAP, moved.shape[3])
    amp_panel = lax.all_gather(amp_local, "row", axis=0, tiled=True)
    ints_panel = lax.all_gather(cycle_ints, "col", axis=1, tiled=True)
    cycle = jnp.dot(ints_panel, amp_panel, preferred_element_type=F32)
    rows_here, cols_here = cycle.shape
    flat_energy = energy.reshape(-1)
    row_start, col_start = row_index * rows_here, col_index * cols_here
    row_energy = lax.dynamic_slice_in_dim(flat_energy, row_start, rows_here, 0)
    col_energy = lax.dynamic_slice_in_dim(flat_energy, col_start, cols_here, 0)
    row_live = lax.dynamic_slice_in_dim(full_live, row_start, rows_here, 0)
    col_live = lax.dynamic_slice_in_dim(full_live, col_start, cols_here, 0)
    denom = row_energy[:, None] + col_energy[None, :]
    return jnp.where(row_live[:, None] & col_live[None, :], cycle / denom, F32(0.0))


def solution(mesh):
    nrow, ncol = mesh.shape["row"], mesh.shape["col"]
    placed = (P("row", None, None, None, "col", None), P("row", "col"), P(), P(), P(), P(), P())
    body = any_device
    if 2 * nrow == NIRREP and ncol == NIRREP:
        body = functools.partial(live_device, nrow, ncol)
    return jax.shard_map(body, mesh=mesh, in_specs=placed, out_specs=P("row", "col"), check_vma=False)
```

```python
import functools

import jax
import jax.numpy as jnp
from jax import lax
from jax.experimental import pallas as pl
from jax.experimental.pallas import tpu as pltpu
from jax.sharding import PartitionSpec as P

NIRREP = 8
OCC_CAP = 16
VIR_CAP = 64
BLOCK = VIR_CAP * OCC_CAP
SIZES = (640, 768, 896, 1024)
F32 = jnp.float32
BF16 = jnp.bfloat16
I32 = jnp.int32
VMEM_BYTES = 56 * 1024 * 1024


def iota(shape, dim):
    return lax.broadcasted_iota(I32, shape, dim)


def params():
    return pltpu.CompilerParams(vmem_limit_bytes=VMEM_BYTES)


def cost(flops, nbytes):
    return pl.CostEstimate(flops=flops, bytes_accessed=nbytes, transcendentals=0)


def pair_scalars(occ, virt, win, pair):
    first = 2 * pair
    o_a, o_b = occ[first], occ[first + 1]
    v_a, v_b = virt[first ^ win[0]], virt[(first + 1) ^ win[0]]
    return (o_a, o_b), (v_a, v_b), (o_a * ((v_a + 1) >> 1), o_a * (v_a >> 1))


def place(q, p, second, counts):
    (o_a, o_b), (v_a, v_b), (start_even, start_odd) = counts
    o = jnp.where(second, o_b, o_a)
    v = jnp.where(second, v_b, v_a)
    start = jnp.where(second, jnp.where((q & 1) == 0, start_even, start_odd), 0)
    return jnp.where((p < o) & (q < v), start + (q >> 1) * o + p, -1)


def one_hot(left, right):
    return jnp.where(left == right, 1.0, 0.0).astype(BF16)


def dot(a, b):
    return jnp.dot(a, b, preferred_element_type=F32)


def prep_kernel(size, occ, virt, win, at, t2_ref, even_ref, odd_ref, at_ref, x_ref):
    at_ref[0] = at[0]
    at_ref[1] = at[1]
    counts = pair_scalars(occ, virt, win, pl.program_id(0))
    row = iota((256, 1), 0)
    source = (((row >> 6) & 1) << 7) | (((row >> 2) & 15) << 3) | ((row & 3) << 1) | (row >> 7)
    by_parity = one_hot(iota((256, 256), 1), source)
    targets = []
    for half in range(2):
        for group in range(4):
            parts = [
                t2_ref[:, half, :, 4 * group + i].astype(F32).reshape(256, VIR_CAP) for i in range(4)
            ]
            x = jnp.concatenate(parts, axis=1).astype(BF16)
            at = (4 * half + group) * 256
            x_ref[:, at : at + 256] = dot(by_parity, x).astype(BF16)
            r = iota((256, 1), 0)
            p, q = 4 * group + (r >> 6), r & 63
            spot = place(q, p, half == 1, counts)
            targets.append(jnp.where(spot >= 0, spot + (q & 1) * size, -1))
    width = 256 if size % 256 == 0 else 128
    for core in range(2):

        @pl.loop(0, size // width)
        def _(n):
            first = pl.multiple_of(n * width, width)
            acc = jnp.zeros((256, width), F32)
            lane = iota((256, width), 1) + (first + core * size)
            for chunk in range(8):
                acc += dot(x_ref[:, chunk * 256 : chunk * 256 + 256], one_hot(targets[chunk], lane))
            acc = acc.astype(BF16)
            even_ref[core, :, pl.ds(first, width)] = acc[:128]
            odd_ref[core, :, pl.ds(first, width)] = acc[128:]


def prep(size, scalars, at, t2):
    shape = jax.ShapeDtypeStruct((NIRREP, 128, size), BF16)
    block = pl.BlockSpec((2, 128, size), lambda k, *_: (k, 0, 0))
    return pl.pallas_call(
        functools.partial(prep_kernel, size),
        out_shape=(shape, shape, jax.ShapeDtypeStruct((2,), I32)),
        grid_spec=pltpu.PrefetchScalarGridSpec(
            num_scalar_prefetch=4,
            grid=(NIRREP // 2,),
            in_specs=[
                pl.BlockSpec((2, 2, OCC_CAP, OCC_CAP, 8, VIR_CAP), lambda k, *_: (0, k, 0, 0, 0, 0))
            ],
            out_specs=[block, block, pl.BlockSpec(memory_space=pltpu.SMEM)],
            scratch_shapes=[pltpu.VMEM((256, 2048), BF16)],
        ),
        compiler_params=params(),
        cost_estimate=cost(2 * 4 * 256 * 2048 * 2 * size, 12 * 2**20),
        name="prep_amplitudes",
    )(*scalars, at, t2)


def fill_rows(rows, spot, sel_ref):
    @pl.loop(0, rows // 32)
    def _(n):
        first = pl.multiple_of(n * 32, 32)
        sel_ref[pl.ds(first, 32), :] = one_hot(iota((32, BLOCK), 0) + first, spot)


def rows_kernel(rows, parity, count, occ, virt, win, at, x_ref, *refs):
    out_ref, sel_ref = refs[count], refs[-1]
    counts = pair_scalars(occ, virt, win, at[0])
    i = iota((1, BLOCK), 1)
    q = 8 * (i >> 7) + 2 * (i & 3) + parity
    spot = place(q, (i >> 2) & 15, ((i >> 6) & 1) == 1, counts)
    fill_rows(rows, spot, sel_ref)
    width = 256 if out_ref.shape[1] % 256 == 0 else 128

    @pl.loop(0, out_ref.shape[1] // width)
    def _(n):
        lanes = pl.ds(pl.multiple_of(n * width, width), width)
        out_ref[:, lanes] = dot(sel_ref[...], x_ref[:, :, lanes].reshape(BLOCK, width)).astype(BF16)


def compact_rows(rows, cols, parity, scalars, at, x, passed=(), awaited=()):
    whole = pl.BlockSpec(memory_space=pl.ANY)
    return pl.pallas_call(
        functools.partial(rows_kernel, rows, parity, len(passed) + len(awaited)),
        out_shape=[jax.ShapeDtypeStruct((rows, cols), BF16)]
        + [jax.ShapeDtypeStruct(y.shape, y.dtype) for y in passed],
        grid_spec=pltpu.PrefetchScalarGridSpec(
            num_scalar_prefetch=4,
            grid=(1,),
            in_specs=[pl.BlockSpec((NIRREP, 128, cols), lambda n, *_: (0, 0, 0))]
            + [whole] * (len(passed) + len(awaited)),
            out_specs=[pl.BlockSpec((rows, cols), lambda n, *_: (0, 0))] + [whole] * len(passed),
            scratch_shapes=[pltpu.VMEM((rows, BLOCK), BF16)],
        ),
        input_output_aliases={5 + i: 1 + i for i in range(len(passed))},
        compiler_params=params(),
        cost_estimate=cost(4 * rows * BLOCK * cols, 4 * rows * BLOCK),
        name="compact_rows",
    )(*scalars, at, x, *passed, *awaited)


def ints_kernel(rows, cols, occ, virt, win, at, mine_ref, other_ref, out_ref, sel_ref, cols_ref):
    plane, dev = at[0], at[1]
    parity = dev & 1

    @pl.when(pl.program_id(0) == 0)
    def _():
        counts = pair_scalars(occ, virt, win, plane)
        i = iota((1, BLOCK), 1)
        q = 2 * ((i >> 4) & 31) + parity
        spot = place(q, i & 15, (i >> 9) == 1, counts)
        fill_rows(rows, spot, sel_ref)

    counts = pair_scalars(occ, virt, win, dev >> 1)
    i = iota((BLOCK, 1), 0)
    q, p = i >> 4, i & 15
    lane = iota((BLOCK, 256), 1) + pl.program_id(0) * 256
    acc = None
    for ref, second in ((mine_ref, parity == 1), (other_ref, parity == 0)):
        spot = place(q, p, second, counts)
        target = jnp.where(spot >= 0, spot + (q & 1) * cols, -1)
        part = dot(ref[...].reshape(BLOCK, BLOCK), one_hot(target, lane))
        acc = part if acc is None else acc + part
    cols_ref[...] = acc.astype(BF16)
    out_ref[...] = dot(sel_ref[...], cols_ref[...]).astype(BF16)


def compact_ints(rows, cols, scalars, at, mine, other):
    mine_spec = pl.BlockSpec(
        (2, VIR_CAP // 2, 1, OCC_CAP, BLOCK), lambda n, o, v, w, a: (0, 0, a[1] & 1, 0, 0)
    )
    whole = pl.BlockSpec((BLOCK, BLOCK), lambda n, *_: (0, 0))
    return pl.pallas_call(
        functools.partial(ints_kernel, rows, cols),
        out_shape=jax.ShapeDtypeStruct((rows, 2 * cols), BF16),
        grid_spec=pltpu.PrefetchScalarGridSpec(
            num_scalar_prefetch=4,
            grid=(2 * cols // 256,),
            in_specs=[mine_spec, whole],
            out_specs=pl.BlockSpec((rows, 256), lambda n, *_: (0, n)),
            scratch_shapes=[pltpu.VMEM((rows, BLOCK), BF16), pltpu.VMEM((BLOCK, 256), BF16)],
        ),
        compiler_params=params(),
        cost_estimate=cost(16 * BLOCK * BLOCK * cols, 4 * BLOCK * BLOCK + 4 * rows * cols),
        name="compact_ints",
    )(*scalars, at, mine, other)


def widen_tile(rows, cols, tile, occ, virt, win, dev, own_refs, sib_refs, wide_ref):
    parity = dev & 1
    counts = pair_scalars(occ, virt, win, dev >> 1)
    (o_a, o_b), _, (start_even, start_odd) = counts
    second = parity == 1
    o = jnp.where(second, o_b, o_a)
    i = iota((1, 256), 1) + tile * 256
    q = i >> 4
    spot = place(q, i & 15, second, counts)
    r = iota((256, 256), 0)
    picks = []
    for s in (parity, 1 - parity):
        start = jnp.where(second, jnp.where(s == 0, start_even, start_odd), 0) + 8 * tile * o
        start = jnp.minimum((start >> 7) << 7, cols - 256)
        window = pl.ds(pl.multiple_of(start, 128), 256)
        picks.append((window, one_hot(r + start, jnp.where((q & 1) == s, spot, -1))))
    for piece in range(2):
        x = dot(own_refs[piece][:, picks[0][0]], picks[0][1])
        x += dot(sib_refs[piece][:, picks[1][0]], picks[1][1])
        wide_ref[piece * cols : piece * cols + rows, :] = x.astype(BF16)
        if rows < cols:
            wide_ref[piece * cols + rows : (piece + 1) * cols, :] = jnp.zeros((cols - rows, 256), BF16)


def widen_kernel(rows, cols, slots, occ, virt, win, at, *refs):
    wide_ref = refs[-1]
    for slot in range(slots):

        @pl.when(pl.program_id(0) == slot)
        def _():
            t0, t1, s0, s1 = refs[4 * slot : 4 * slot + 4]
            tile = pl.program_id(1)
            widen_tile(rows, cols, tile, occ, virt, win, at[1], (t0, t1), (s0, s1), wide_ref.at[0])


def widen(rows, cols, scalars, at, blocks):
    slots = len(blocks) // 4
    square = pl.BlockSpec((rows, cols), lambda t, n, *_: (0, 0), pipeline_mode=pl.Buffered(1))
    return pl.pallas_call(
        functools.partial(widen_kernel, rows, cols, slots),
        out_shape=jax.ShapeDtypeStruct((slots, 2 * cols, BLOCK), BF16),
        grid_spec=pltpu.PrefetchScalarGridSpec(
            num_scalar_prefetch=4,
            grid=(slots, BLOCK // 256),
            in_specs=[square] * len(blocks),
            out_specs=pl.BlockSpec((1, 2 * cols, 256), lambda t, n, *_: (t, 0, n)),
        ),
        compiler_params=params(),
        cost_estimate=cost(slots * 8 * rows * 512 * BLOCK, slots * (8 * rows * cols + 4 * cols * BLOCK)),
        name="widen",
    )(*scalars, at, *blocks)


def ints_dot(ints_ref, wide):
    _, _, rows, width = ints_ref.shape
    return dot(ints_ref[0].reshape(2 * rows, width), wide).reshape(2, rows, 256)


def product_kernel(inner, ints_ref, wide_ref, acc_ref):
    at = pl.ds(pl.multiple_of(pl.program_id(1) * 256, 256), 256)

    @pl.when(pl.program_id(0) == 0)
    def _():
        acc_ref[:, :, at] = jnp.zeros((2, acc_ref.shape[1], 256), F32)

    acc_ref[:, :, at] += ints_dot(ints_ref, wide_ref[0])


def product(rows, cols, inner, ints, wide):
    slots = wide.shape[0]
    return pl.pallas_call(
        product_kernel,
        out_shape=jax.ShapeDtypeStruct((2, rows, BLOCK), F32),
        grid_spec=pltpu.PrefetchScalarGridSpec(
            num_scalar_prefetch=1,
            grid=(slots, BLOCK // 256),
            in_specs=[
                pl.BlockSpec((1, 2, rows, 2 * cols), lambda t, n, k: (k[t], 0, 0, 0)),
                pl.BlockSpec((1, 2 * cols, 256), lambda t, n, k: (t, 0, n)),
            ],
            out_specs=pl.BlockSpec((2, rows, BLOCK), lambda t, n, k: (0, 0, 0)),
        ),
        compiler_params=params(),
        cost_estimate=cost(16 * slots * rows * cols * BLOCK, slots * 4 * cols * (rows + BLOCK)),
        name="product",
    )(inner, ints, wide)


def last_kernel(
    rows, cols, occ, virt, win, at, inner,
    ints_ref, t0, t1, s0, s1, old_ref, evirt, eocc_ref, ecol_ref, out_ref, wide_ref, sum_ref,
):
    plane, dev = at[0], at[1]
    widen_tile(rows, cols, pl.program_id(0), occ, virt, win, dev, (t0, t1), (s0, s1), wide_ref)
    sum_ref[:, :rows, :] = old_ref[...] + ints_dot(ints_ref, wide_ref[...])
    i = iota((1, 256), 1) + pl.program_id(0) * 256
    col_live = ((i & 15) < occ[dev]) & ((i >> 4) < virt[dev ^ win[0]])
    col_energy = ecol_ref[...]
    _, _, starts = pair_scalars(occ, virt, win, plane)
    p = iota((OCC_CAP, 1), 0)
    for h in range(2):
        irrep = 2 * plane + h
        o, partner = occ[irrep], irrep ^ win[0]
        v = virt[partner]
        occ_energy = eocc_ref[h]
        row_live = (p < o) & col_live

        @pl.loop(0, VIR_CAP // 2)
        def _(half_q):
            for s in range(2):
                q = 2 * half_q + s
                start = half_q * o
                if h == 1:
                    start = start + starts[s]
                start = jnp.minimum(start, rows)
                block = sum_ref[s, pl.ds(pl.multiple_of((start >> 3) << 3, 8), OCC_CAP + 8), :]
                block = pltpu.roll(block, OCC_CAP + 8 - (start & 7), 0)[:OCC_CAP]
                denom = (occ_energy - evirt[partner, q]) + col_energy
                value = jnp.where(row_live & (q < v), block / denom, 0.0)
                at_row = pl.multiple_of((h * VIR_CAP + q) * OCC_CAP, OCC_CAP)
                out_ref[pl.ds(at_row, OCC_CAP), :] = value


def last(rows, cols, scalars, at, inner, ints, own, sib, acc, energies):
    square = pl.BlockSpec((rows, cols), lambda n, *_: (0, 0))
    return pl.pallas_call(
        functools.partial(last_kernel, rows, cols),
        out_shape=jax.ShapeDtypeStruct((2 * BLOCK, BLOCK), F32),
        grid_spec=pltpu.PrefetchScalarGridSpec(
            num_scalar_prefetch=5,
            grid=(BLOCK // 256,),
            in_specs=[
                pl.BlockSpec((1, 2, rows, 2 * cols), lambda n, o, v, w, a, k: (k[0], 0, 0, 0)),
                square, square, square, square,
                pl.BlockSpec((2, rows, 256), lambda n, *_: (0, 0, n)),
                pl.BlockSpec(memory_space=pltpu.SMEM),
                pl.BlockSpec((2, OCC_CAP, 1), lambda n, *_: (0, 0, 0)),
                pl.BlockSpec((1, 256), lambda n, *_: (0, n)),
            ],
            out_specs=pl.BlockSpec((2 * BLOCK, 256), lambda n, *_: (0, n)),
            scratch_shapes=[
                pltpu.VMEM((2 * cols, 256), BF16),
                pltpu.VMEM((2, rows + OCC_CAP + 8, 256), F32),
            ],
        ),
        compiler_params=params(),
        cost_estimate=cost(16 * rows * cols * BLOCK, 8 * rows * cols + 16 * rows * BLOCK),
        name="last_product",
    )(*scalars, at, inner, ints, *own, *sib, acc, *energies)


def after_kernel(x_in, y_in, z_in, x_out, y_out):
    pass


def after(x, y, z):
    whole = pl.BlockSpec(memory_space=pl.ANY)
    return pl.pallas_call(
        after_kernel,
        out_shape=tuple(jax.ShapeDtypeStruct(w.shape, w.dtype) for w in (x, y)),
        in_specs=[whole, whole, whole],
        out_specs=(whole, whole),
        input_output_aliases={0: 0, 1: 1},
        name="after",
    )(x, y, z)


def ring_order(n):
    return list(range(0, 1)) + list(range(1, n, 2)) + [i for i in range(n - 1, 0, -1) if i % 2 == 0]


def branch(rows, nrow, ncol, t2, ints, occ, virt, win, eps_virt, occ_rows, col_energy, at, sources):
    cols = -(-rows // 128) * 128
    scalars = (occ, virt, win)
    order = ring_order(nrow)
    ring = [(order[i], order[(i + 1) % nrow]) for i in range(nrow)]
    swap = [(c, c ^ 1) for c in range(ncol)]

    def to_sibling(x):
        return lax.ppermute(x, "col", swap)

    def around(x):
        return lax.ppermute(x, "row", ring)

    def exchange(x):
        return lax.all_to_all(x, "col", split_axis=0, concat_axis=0, tiled=True)

    even, odd, then = prep(cols, scalars, at, t2)
    even = exchange(even)
    mine = ints.reshape(2, VIR_CAP // 2, 2, OCC_CAP, BLOCK)
    other = lax.dynamic_index_in_dim(mine, 1 - (then[1] & 1), 2, keepdims=False).reshape(BLOCK, BLOCK)
    small = compact_ints(rows, cols, scalars, at, mine, to_sibling(other))
    even, odd, small = compact_rows(rows, cols, 0, scalars, at, even, passed=(odd, small))
    even_next = around(even)
    odd, small = compact_rows(
        rows, cols, 1, scalars, at, exchange(odd), passed=(small,), awaited=(even_next,)
    )
    panel = lax.all_gather(small, "col", axis=0, tiled=False).reshape(ncol // 2, 2, rows, 2 * cols)

    held = [even, odd]
    blocks = []
    for step in range(nrow - 1):
        later = [even_next if step == 0 else around(held[0]), around(held[1])]
        blocks += held + [to_sibling(x) for x in held]
        held = later
    wide = widen(rows, cols, scalars, at, blocks)
    acc = product(rows, cols, sources[: nrow - 1], panel, wide)
    own = after(held[0], held[1], acc)
    sib = [to_sibling(x) for x in own]
    energies = (eps_virt, occ_rows, col_energy)
    return last(rows, cols, scalars, at, sources[nrow - 1 :], panel, own, sib, acc, energies)


def choose_kernel(occ, virt, win, index_ref):
    index = jnp.int32(0)
    for pair in range(NIRREP // 2):
        (o_a, o_b), (v_a, v_b), _ = pair_scalars(occ, virt, win, pair)
        most = o_a * ((v_a + 1) >> 1) + o_b * ((v_b + 1) >> 1)
        need = sum((most > size).astype(I32) for size in SIZES[:-1])
        index = jnp.maximum(index, need)
    index_ref[0] = index


def choose(occ, virt, win):
    smem = pl.BlockSpec(memory_space=pltpu.SMEM)
    return pl.pallas_call(
        choose_kernel,
        out_shape=jax.ShapeDtypeStruct((1,), I32),
        in_specs=[smem] * 3,
        out_specs=smem,
        name="choose",
    )(occ, virt, win)[0]


def live_device(nrow, ncol, t2, ints, eps_occ, eps_virt, occ, virt, win):
    row, col = lax.axis_index("row"), lax.axis_index("col")
    index = choose(occ, virt, win)
    occ_rows = lax.dynamic_slice(eps_occ, (2 * row, 0), (2, OCC_CAP)).reshape(2, OCC_CAP, 1)
    col_occ = lax.dynamic_slice(eps_occ, (col, 0), (1, OCC_CAP))
    col_virt = lax.dynamic_slice(eps_virt, (col ^ win[0], 0), (1, VIR_CAP))
    col_energy = (col_occ[:, None, :] - col_virt[:, :, None]).reshape(1, BLOCK)
    at = jnp.stack([row, col]).astype(I32)
    order = ring_order(nrow)
    table = [[order[(order.index(z) - t) % nrow] for t in range(nrow)] for z in range(nrow)]
    sources = lax.dynamic_slice(jnp.array(table, I32), (row, 0), (1, nrow)).reshape(nrow)
    operands = (t2, ints, occ, virt, win, eps_virt, occ_rows, col_energy, at, sources)
    return lax.switch(index, [functools.partial(branch, size, nrow, ncol) for size in SIZES], *operands)


def ph_vectors(eps_occ, eps_virt, occ_count, virt_count, window_irrep):
    irreps = jnp.arange(NIRREP, dtype=I32)
    partner = jnp.bitwise_xor(irreps, window_irrep[0])
    onehot = partner[:, None] == irreps[None, :]
    virt_rows = jnp.dot(onehot.astype(F32), eps_virt, precision=lax.Precision.HIGHEST)
    virt_live = jnp.sum(jnp.where(onehot, virt_count[None, :], 0), axis=1)
    energy = eps_occ[:, None, :] - virt_rows[:, :, None]
    slots_occ = jnp.arange(OCC_CAP, dtype=I32)
    slots_virt = jnp.arange(VIR_CAP, dtype=I32)
    live = (slots_occ[None, None, :] < occ_count[:, None, None]) & (
        slots_virt[None, :, None] < virt_live[:, None, None]
    )
    return (energy, live)


def any_device(t2_pairs, cycle_ints, eps_occ, eps_virt, occ_count, virt_count, window_irrep):
    irrep_local = t2_pairs.shape[0]
    virt_local = t2_pairs.shape[4]
    total = NIRREP * VIR_CAP * OCC_CAP
    energy, live = ph_vectors(eps_occ, eps_virt, occ_count, virt_count, window_irrep)
    row_index = lax.axis_index("row")
    col_index = lax.axis_index("col")
    zero_index = jnp.int32(0)
    source_live = lax.dynamic_slice(
        live,
        (row_index * irrep_local, col_index * virt_local, zero_index),
        (irrep_local, virt_local, OCC_CAP),
    )
    full_live = live.reshape(-1)
    ordered = jnp.transpose(t2_pairs, (0, 4, 2, 1, 5, 3)).reshape(
        irrep_local, virt_local, OCC_CAP, total
    )
    keep = source_live[:, :, :, None] & full_live[None, None, None, :]
    ordered = jnp.where(keep, ordered, jnp.zeros_like(ordered))
    moved = lax.all_to_all(ordered, "col", split_axis=3, concat_axis=1, tiled=True)
    amp_local = moved.reshape(irrep_local * VIR_CAP * OCC_CAP, moved.shape[3])
    amp_panel = lax.all_gather(amp_local, "row", axis=0, tiled=True)
    ints_panel = lax.all_gather(cycle_ints, "col", axis=1, tiled=True)
    cycle = jnp.dot(ints_panel, amp_panel, preferred_element_type=F32)
    rows_here, cols_here = cycle.shape
    flat_energy = energy.reshape(-1)
    row_start, col_start = row_index * rows_here, col_index * cols_here
    row_energy = lax.dynamic_slice_in_dim(flat_energy, row_start, rows_here, 0)
    col_energy = lax.dynamic_slice_in_dim(flat_energy, col_start, cols_here, 0)
    row_live = lax.dynamic_slice_in_dim(full_live, row_start, rows_here, 0)
    col_live = lax.dynamic_slice_in_dim(full_live, col_start, cols_here, 0)
    denom = row_energy[:, None] + col_energy[None, :]
    return jnp.where(row_live[:, None] & col_live[None, :], cycle / denom, F32(0.0))


def solution(mesh):
    nrow, ncol = mesh.shape["row"], mesh.shape["col"]
    placed = (P("row", None, None, None, "col", None), P("row", "col"), P(), P(), P(), P(), P())
    body = any_device
    if 2 * nrow == NIRREP and ncol == NIRREP:
        body = functools.partial(live_device, nrow, ncol)
    return jax.shard_map(body, mesh=mesh, in_specs=placed, out_specs=P("row", "col"), check_vma=False)
```

```python
import functools

import jax
import jax.numpy as jnp
from jax import lax
from jax.experimental import pallas as pl
from jax.experimental.pallas import tpu as pltpu
from jax.sharding import PartitionSpec as P

NIRREP = 8
OCC_CAP = 16
VIR_CAP = 64
BLOCK = VIR_CAP * OCC_CAP
SIZES = (640, 768, 896, 1024)
F32 = jnp.float32
BF16 = jnp.bfloat16
I32 = jnp.int32
VMEM_BYTES = 56 * 1024 * 1024


def iota(shape, dim):
    return lax.broadcasted_iota(I32, shape, dim)


def params():
    return pltpu.CompilerParams(vmem_limit_bytes=VMEM_BYTES)


def cost(flops, nbytes):
    return pl.CostEstimate(flops=flops, bytes_accessed=nbytes, transcendentals=0)


def pair_scalars(occ, virt, win, pair):
    first = 2 * pair
    o_a, o_b = occ[first], occ[first + 1]
    v_a, v_b = virt[first ^ win[0]], virt[(first + 1) ^ win[0]]
    return (o_a, o_b), (v_a, v_b), (o_a * ((v_a + 1) >> 1), o_a * (v_a >> 1))


def place(q, p, second, counts):
    (o_a, o_b), (v_a, v_b), (start_even, start_odd) = counts
    o = jnp.where(second, o_b, o_a)
    v = jnp.where(second, v_b, v_a)
    start = jnp.where(second, jnp.where((q & 1) == 0, start_even, start_odd), 0)
    return jnp.where((p < o) & (q < v), start + (q >> 1) * o + p, -1)


def one_hot(left, right):
    return jnp.where(left == right, 1.0, 0.0).astype(BF16)


def dot(a, b):
    return jnp.dot(a, b, preferred_element_type=F32)


def prep_kernel(size, occ, virt, win, t2_ref, even_ref, odd_ref, x_ref):
    counts = pair_scalars(occ, virt, win, pl.program_id(0))
    row = iota((256, 1), 0)
    source = (((row >> 6) & 1) << 7) | (((row >> 2) & 15) << 3) | ((row & 3) << 1) | (row >> 7)
    by_parity = one_hot(iota((256, 256), 1), source)
    targets = []
    for half in range(2):
        for group in range(4):
            parts = [
                t2_ref[:, half, :, 4 * group + i].astype(F32).reshape(256, VIR_CAP) for i in range(4)
            ]
            x = jnp.concatenate(parts, axis=1).astype(BF16)
            at = (4 * half + group) * 256
            x_ref[:, at : at + 256] = dot(by_parity, x).astype(BF16)
            r = iota((256, 1), 0)
            p, q = 4 * group + (r >> 6), r & 63
            spot = place(q, p, half == 1, counts)
            targets.append(jnp.where(spot >= 0, spot + (q & 1) * size, -1))
    for start in range(0, 2 * size, 256):
        acc = jnp.zeros((256, 256), F32)
        lane = iota((256, 256), 1) + start
        for chunk in range(8):
            acc += dot(x_ref[:, chunk * 256 : chunk * 256 + 256], one_hot(targets[chunk], lane))
        acc = acc.astype(BF16)
        for part in range(2):
            at_col = start + 128 * part
            core, col = at_col // size, at_col % size
            tile = acc[:, 128 * part : 128 * part + 128]
            even_ref[core, :, col : col + 128] = tile[:128]
            odd_ref[core, :, col : col + 128] = tile[128:]


def prep(size, scalars, t2):
    shape = jax.ShapeDtypeStruct((NIRREP, 128, size), BF16)
    block = pl.BlockSpec((2, 128, size), lambda k, *_: (k, 0, 0))
    return pl.pallas_call(
        functools.partial(prep_kernel, size),
        out_shape=(shape, shape),
        grid_spec=pltpu.PrefetchScalarGridSpec(
            num_scalar_prefetch=3,
            grid=(NIRREP // 2,),
            in_specs=[
                pl.BlockSpec((2, 2, OCC_CAP, OCC_CAP, 8, VIR_CAP), lambda k, *_: (0, k, 0, 0, 0, 0))
            ],
            out_specs=[block, block],
            scratch_shapes=[pltpu.VMEM((256, 2048), BF16)],
        ),
        compiler_params=params(),
        cost_estimate=cost(2 * 4 * 256 * 2048 * 2 * size, 12 * 2**20),
        name="prep_amplitudes",
    )(*scalars, t2)


def fill_rows(rows, spot, sel_ref):
    for first in range(0, rows, 32):
        sel_ref[first : first + 32, :] = one_hot(iota((32, BLOCK), 0) + first, spot)


def rows_kernel(rows, parity, count, occ, virt, win, at, x_ref, *refs):
    out_ref, sel_ref = refs[count], refs[-1]
    counts = pair_scalars(occ, virt, win, at[0])
    i = iota((1, BLOCK), 1)
    q = 8 * (i >> 7) + 2 * (i & 3) + parity
    spot = place(q, (i >> 2) & 15, ((i >> 6) & 1) == 1, counts)
    fill_rows(rows, spot, sel_ref)
    width = 256 if out_ref.shape[1] % 256 == 0 else 128

    @pl.loop(0, out_ref.shape[1] // width)
    def _(n):
        lanes = pl.ds(pl.multiple_of(n * width, width), width)
        out_ref[:, lanes] = dot(sel_ref[...], x_ref[:, :, lanes].reshape(BLOCK, width)).astype(BF16)


def compact_rows(rows, cols, parity, scalars, at, x, passed=(), awaited=()):
    whole = pl.BlockSpec(memory_space=pl.ANY)
    return pl.pallas_call(
        functools.partial(rows_kernel, rows, parity, len(passed) + len(awaited)),
        out_shape=[jax.ShapeDtypeStruct((rows, cols), BF16)]
        + [jax.ShapeDtypeStruct(y.shape, y.dtype) for y in passed],
        grid_spec=pltpu.PrefetchScalarGridSpec(
            num_scalar_prefetch=4,
            grid=(1,),
            in_specs=[pl.BlockSpec((NIRREP, 128, cols), lambda n, *_: (0, 0, 0))]
            + [whole] * (len(passed) + len(awaited)),
            out_specs=[pl.BlockSpec((rows, cols), lambda n, *_: (0, 0))] + [whole] * len(passed),
            scratch_shapes=[pltpu.VMEM((rows, BLOCK), BF16)],
        ),
        input_output_aliases={5 + i: 1 + i for i in range(len(passed))},
        compiler_params=params(),
        cost_estimate=cost(4 * rows * BLOCK * cols, 4 * rows * BLOCK),
        name="compact_rows",
    )(*scalars, at, x, *passed, *awaited)


def ints_kernel(rows, cols, occ, virt, win, at, mine_ref, other_ref, awaited, out_ref, sel_ref, cols_ref):
    plane, dev = at[0], at[1]
    parity = dev & 1

    @pl.when(pl.program_id(0) == 0)
    def _():
        counts = pair_scalars(occ, virt, win, plane)
        i = iota((1, BLOCK), 1)
        q = 2 * ((i >> 4) & 31) + parity
        spot = place(q, i & 15, (i >> 9) == 1, counts)
        fill_rows(rows, spot, sel_ref)

    counts = pair_scalars(occ, virt, win, dev >> 1)
    i = iota((BLOCK, 1), 0)
    q, p = i >> 4, i & 15
    lane = iota((BLOCK, 256), 1) + pl.program_id(0) * 256
    acc = None
    for ref, second in ((mine_ref, parity == 1), (other_ref, parity == 0)):
        spot = place(q, p, second, counts)
        target = jnp.where(spot >= 0, spot + (q & 1) * cols, -1)
        part = dot(ref[...].reshape(BLOCK, BLOCK), one_hot(target, lane))
        acc = part if acc is None else acc + part
    cols_ref[...] = acc.astype(BF16)
    out_ref[...] = dot(sel_ref[...], cols_ref[...]).astype(BF16)


def compact_ints(rows, cols, scalars, at, mine, other, awaited):
    mine_spec = pl.BlockSpec(
        (2, VIR_CAP // 2, 1, OCC_CAP, BLOCK), lambda n, o, v, w, a: (0, 0, a[1] & 1, 0, 0)
    )
    whole = pl.BlockSpec((BLOCK, BLOCK), lambda n, *_: (0, 0))
    return pl.pallas_call(
        functools.partial(ints_kernel, rows, cols),
        out_shape=jax.ShapeDtypeStruct((rows, 2 * cols), BF16),
        grid_spec=pltpu.PrefetchScalarGridSpec(
            num_scalar_prefetch=4,
            grid=(2 * cols // 256,),
            in_specs=[mine_spec, whole, pl.BlockSpec(memory_space=pl.ANY)],
            out_specs=pl.BlockSpec((rows, 256), lambda n, *_: (0, n)),
            scratch_shapes=[pltpu.VMEM((rows, BLOCK), BF16), pltpu.VMEM((BLOCK, 256), BF16)],
        ),
        compiler_params=params(),
        cost_estimate=cost(16 * BLOCK * BLOCK * cols, 4 * BLOCK * BLOCK + 4 * rows * cols),
        name="compact_ints",
    )(*scalars, at, mine, other, awaited)


def widen_tile(rows, cols, tile, occ, virt, win, dev, own_refs, sib_refs, wide_ref):
    parity = dev & 1
    counts = pair_scalars(occ, virt, win, dev >> 1)
    (o_a, o_b), _, (start_even, start_odd) = counts
    second = parity == 1
    o = jnp.where(second, o_b, o_a)
    i = iota((1, 256), 1) + tile * 256
    q = i >> 4
    spot = place(q, i & 15, second, counts)
    r = iota((256, 256), 0)
    picks = []
    for s in (parity, 1 - parity):
        start = jnp.where(second, jnp.where(s == 0, start_even, start_odd), 0) + 8 * tile * o
        start = jnp.minimum((start >> 7) << 7, cols - 256)
        window = pl.ds(pl.multiple_of(start, 128), 256)
        picks.append((window, one_hot(r + start, jnp.where((q & 1) == s, spot, -1))))
    for piece in range(2):
        x = dot(own_refs[piece][:, picks[0][0]], picks[0][1])
        x += dot(sib_refs[piece][:, picks[1][0]], picks[1][1])
        wide_ref[piece * cols : piece * cols + rows, :] = x.astype(BF16)
        if rows < cols:
            wide_ref[piece * cols + rows : (piece + 1) * cols, :] = jnp.zeros((cols - rows, 256), BF16)


def widen_kernel(rows, cols, slots, occ, virt, win, at, *refs):
    wide_ref = refs[-1]
    for slot in range(slots):

        @pl.when(pl.program_id(0) == slot)
        def _():
            t0, t1, s0, s1 = refs[4 * slot : 4 * slot + 4]
            tile = pl.program_id(1)
            widen_tile(rows, cols, tile, occ, virt, win, at[1], (t0, t1), (s0, s1), wide_ref.at[0])


def widen(rows, cols, scalars, at, blocks):
    slots = len(blocks) // 4
    square = pl.BlockSpec((rows, cols), lambda t, n, *_: (0, 0), pipeline_mode=pl.Buffered(1))
    return pl.pallas_call(
        functools.partial(widen_kernel, rows, cols, slots),
        out_shape=jax.ShapeDtypeStruct((slots, 2 * cols, BLOCK), BF16),
        grid_spec=pltpu.PrefetchScalarGridSpec(
            num_scalar_prefetch=4,
            grid=(slots, BLOCK // 256),
            in_specs=[square] * len(blocks),
            out_specs=pl.BlockSpec((1, 2 * cols, 256), lambda t, n, *_: (t, 0, n)),
        ),
        compiler_params=params(),
        cost_estimate=cost(slots * 8 * rows * 512 * BLOCK, slots * (8 * rows * cols + 4 * cols * BLOCK)),
        name="widen",
    )(*scalars, at, *blocks)


def ints_dot(ints_ref, wide):
    _, _, rows, width = ints_ref.shape
    return dot(ints_ref[0].reshape(2 * rows, width), wide).reshape(2, rows, 256)


def product_kernel(inner, ints_ref, wide_ref, acc_ref):
    at = pl.ds(pl.multiple_of(pl.program_id(1) * 256, 256), 256)

    @pl.when(pl.program_id(0) == 0)
    def _():
        acc_ref[:, :, at] = jnp.zeros((2, acc_ref.shape[1], 256), F32)

    @pl.loop(0, 2)
    def _(half):
        acc_ref[half, :, at] += dot(ints_ref[0, half], wide_ref[0])


def product(rows, cols, inner, ints, wide):
    slots = wide.shape[0]
    return pl.pallas_call(
        product_kernel,
        out_shape=jax.ShapeDtypeStruct((2, rows, BLOCK), F32),
        grid_spec=pltpu.PrefetchScalarGridSpec(
            num_scalar_prefetch=1,
            grid=(slots, BLOCK // 256),
            in_specs=[
                pl.BlockSpec((1, 2, rows, 2 * cols), lambda t, n, k: (k[t], 0, 0, 0)),
                pl.BlockSpec((1, 2 * cols, 256), lambda t, n, k: (t, 0, n)),
            ],
            out_specs=pl.BlockSpec((2, rows, BLOCK), lambda t, n, k: (0, 0, 0)),
        ),
        compiler_params=params(),
        cost_estimate=cost(16 * slots * rows * cols * BLOCK, slots * 4 * cols * (rows + BLOCK)),
        name="product",
    )(inner, ints, wide)


def last_kernel(
    rows, cols, occ, virt, win, at, inner,
    ints_ref, t0, t1, s0, s1, old_ref, evirt, eocc_ref, ecol_ref, out_ref, wide_ref, sum_ref,
):
    plane, dev = at[0], at[1]
    widen_tile(rows, cols, pl.program_id(0), occ, virt, win, dev, (t0, t1), (s0, s1), wide_ref)
    sum_ref[:, :rows, :] = old_ref[...] + ints_dot(ints_ref, wide_ref[...])
    i = iota((1, 256), 1) + pl.program_id(0) * 256
    col_live = ((i & 15) < occ[dev]) & ((i >> 4) < virt[dev ^ win[0]])
    col_energy = ecol_ref[...]
    _, _, starts = pair_scalars(occ, virt, win, plane)
    p = iota((OCC_CAP, 1), 0)
    irreps = [2 * plane, 2 * plane + 1]
    occs = [occ[irrep] for irrep in irreps]
    partners = [irrep ^ win[0] for irrep in irreps]
    virts = [virt[partner] for partner in partners]
    live = [(p < o) & col_live for o in occs]

    @pl.loop(0, VIR_CAP // 8)
    def _(group):
        for h in range(2):
            for i in range(8):
                half_q, s = 4 * group + i // 2, i % 2
                q = 2 * half_q + s
                start = half_q * occs[h]
                if h == 1:
                    start = start + starts[s]
                start = jnp.minimum(start, rows)
                block = sum_ref[s, pl.ds(pl.multiple_of((start >> 3) << 3, 8), OCC_CAP + 8), :]
                block = pltpu.roll(block, OCC_CAP + 8 - (start & 7), 0)[:OCC_CAP]
                denom = (eocc_ref[h] - evirt[partners[h], q]) + col_energy
                value = jnp.where(live[h] & (q < virts[h]), block / denom, 0.0)
                at_row = pl.multiple_of((h * VIR_CAP + q) * OCC_CAP, OCC_CAP)
                out_ref[pl.ds(at_row, OCC_CAP), :] = value


def last(rows, cols, scalars, at, inner, ints, own, sib, acc, energies):
    square = pl.BlockSpec((rows, cols), lambda n, *_: (0, 0))
    return pl.pallas_call(
        functools.partial(last_kernel, rows, cols),
        out_shape=jax.ShapeDtypeStruct((2 * BLOCK, BLOCK), F32),
        grid_spec=pltpu.PrefetchScalarGridSpec(
            num_scalar_prefetch=5,
            grid=(BLOCK // 256,),
            in_specs=[
                pl.BlockSpec((1, 2, rows, 2 * cols), lambda n, o, v, w, a, k: (k[0], 0, 0, 0)),
                square, square, square, square,
                pl.BlockSpec((2, rows, 256), lambda n, *_: (0, 0, n)),
                pl.BlockSpec(memory_space=pltpu.SMEM),
                pl.BlockSpec((2, OCC_CAP, 1), lambda n, *_: (0, 0, 0)),
                pl.BlockSpec((1, 256), lambda n, *_: (0, n)),
            ],
            out_specs=pl.BlockSpec((2 * BLOCK, 256), lambda n, *_: (0, n)),
            scratch_shapes=[
                pltpu.VMEM((2 * cols, 256), BF16),
                pltpu.VMEM((2, rows + OCC_CAP + 8, 256), F32),
            ],
        ),
        compiler_params=params(),
        cost_estimate=cost(16 * rows * cols * BLOCK, 8 * rows * cols + 16 * rows * BLOCK),
        name="last_product",
    )(*scalars, at, inner, ints, *own, *sib, acc, *energies)


def after_kernel(*refs):
    pass


def after(kept, awaited):
    whole = pl.BlockSpec(memory_space=pl.ANY)
    return pl.pallas_call(
        after_kernel,
        out_shape=[jax.ShapeDtypeStruct(x.shape, x.dtype) for x in kept],
        in_specs=[whole] * (len(kept) + len(awaited)),
        out_specs=[whole] * len(kept),
        input_output_aliases={i: i for i in range(len(kept))},
        name="after",
    )(*kept, *awaited)


def ring_order(n):
    return list(range(0, 1)) + list(range(1, n, 2)) + [i for i in range(n - 1, 0, -1) if i % 2 == 0]


def branch(rows, nrow, ncol, t2, ints, occ, virt, win, eps_virt, occ_rows, col_energy, at, sources):
    cols = -(-rows // 128) * 128
    scalars = (occ, virt, win)
    order = ring_order(nrow)
    ring = [(order[i], order[(i + 1) % nrow]) for i in range(nrow)]
    swap = [(c, c ^ 1) for c in range(ncol)]

    def to_sibling(x):
        return lax.ppermute(x, "col", swap)

    def around(x):
        return lax.ppermute(x, "row", ring)

    def exchange(x):
        return lax.all_to_all(x, "col", split_axis=0, concat_axis=0, tiled=True)

    even, odd = prep(cols, scalars, t2)
    even, odd = compact_rows(rows, cols, 0, scalars, at, exchange(even), passed=(odd,))
    mine = ints.reshape(2, VIR_CAP // 2, 2, OCC_CAP, BLOCK)
    other = lax.dynamic_index_in_dim(mine, 1 - (at[1] & 1), 2, keepdims=False).reshape(BLOCK, BLOCK)
    even_next = around(even)
    small = compact_ints(rows, cols, scalars, at, mine, to_sibling(other), even)
    odd, small = compact_rows(rows, cols, 1, scalars, at, exchange(odd), passed=(small,))
    odd, small = after([odd, small], [even_next])
    panel = lax.all_gather(small, "col", axis=0, tiled=False).reshape(ncol // 2, 2, rows, 2 * cols)

    held = [even, odd]
    blocks = []
    for step in range(nrow - 1):
        later = [even_next if step == 0 else around(held[0]), around(held[1])]
        blocks += held + [to_sibling(x) for x in held]
        held = later
    wide = widen(rows, cols, scalars, at, blocks)
    acc = product(rows, cols, sources[: nrow - 1], panel, wide)
    own = after(held, [acc])
    sib = [to_sibling(x) for x in own]
    energies = (eps_virt, occ_rows, col_energy)
    return last(rows, cols, scalars, at, sources[nrow - 1 :], panel, own, sib, acc, energies)


def choose_kernel(occ, virt, win, index_ref):
    index = jnp.int32(0)
    for pair in range(NIRREP // 2):
        (o_a, o_b), (v_a, v_b), _ = pair_scalars(occ, virt, win, pair)
        most = o_a * ((v_a + 1) >> 1) + o_b * ((v_b + 1) >> 1)
        need = sum((most > size).astype(I32) for size in SIZES[:-1])
        index = jnp.maximum(index, need)
    index_ref[0] = index


def choose(occ, virt, win):
    smem = pl.BlockSpec(memory_space=pltpu.SMEM)
    return pl.pallas_call(
        choose_kernel,
        out_shape=jax.ShapeDtypeStruct((1,), I32),
        in_specs=[smem] * 3,
        out_specs=smem,
        name="choose",
    )(occ, virt, win)[0]


def live_device(nrow, ncol, t2, ints, eps_occ, eps_virt, occ, virt, win):
    row, col = lax.axis_index("row"), lax.axis_index("col")
    index = choose(occ, virt, win)
    occ_rows = lax.dynamic_slice(eps_occ, (2 * row, 0), (2, OCC_CAP)).reshape(2, OCC_CAP, 1)
    col_occ = lax.dynamic_slice(eps_occ, (col, 0), (1, OCC_CAP))
    col_virt = lax.dynamic_slice(eps_virt, (col ^ win[0], 0), (1, VIR_CAP))
    col_energy = (col_occ[:, None, :] - col_virt[:, :, None]).reshape(1, BLOCK)
    at = jnp.stack([row, col]).astype(I32)
    order = ring_order(nrow)
    table = [[order[(order.index(z) - t) % nrow] for t in range(nrow)] for z in range(nrow)]
    sources = lax.dynamic_slice(jnp.array(table, I32), (row, 0), (1, nrow)).reshape(nrow)
    operands = (t2, ints, occ, virt, win, eps_virt, occ_rows, col_energy, at, sources)
    return lax.switch(index, [functools.partial(branch, size, nrow, ncol) for size in SIZES], *operands)


def ph_vectors(eps_occ, eps_virt, occ_count, virt_count, window_irrep):
    irreps = jnp.arange(NIRREP, dtype=I32)
    partner = jnp.bitwise_xor(irreps, window_irrep[0])
    onehot = partner[:, None] == irreps[None, :]
    virt_rows = jnp.dot(onehot.astype(F32), eps_virt, precision=lax.Precision.HIGHEST)
    virt_live = jnp.sum(jnp.where(onehot, virt_count[None, :], 0), axis=1)
    energy = eps_occ[:, None, :] - virt_rows[:, :, None]
    slots_occ = jnp.arange(OCC_CAP, dtype=I32)
    slots_virt = jnp.arange(VIR_CAP, dtype=I32)
    live = (slots_occ[None, None, :] < occ_count[:, None, None]) & (
        slots_virt[None, :, None] < virt_live[:, None, None]
    )
    return (energy, live)


def any_device(t2_pairs, cycle_ints, eps_occ, eps_virt, occ_count, virt_count, window_irrep):
    irrep_local = t2_pairs.shape[0]
    virt_local = t2_pairs.shape[4]
    total = NIRREP * VIR_CAP * OCC_CAP
    energy, live = ph_vectors(eps_occ, eps_virt, occ_count, virt_count, window_irrep)
    row_index = lax.axis_index("row")
    col_index = lax.axis_index("col")
    zero_index = jnp.int32(0)
    source_live = lax.dynamic_slice(
        live,
        (row_index * irrep_local, col_index * virt_local, zero_index),
        (irrep_local, virt_local, OCC_CAP),
    )
    full_live = live.reshape(-1)
    ordered = jnp.transpose(t2_pairs, (0, 4, 2, 1, 5, 3)).reshape(
        irrep_local, virt_local, OCC_CAP, total
    )
    keep = source_live[:, :, :, None] & full_live[None, None, None, :]
    ordered = jnp.where(keep, ordered, jnp.zeros_like(ordered))
    moved = lax.all_to_all(ordered, "col", split_axis=3, concat_axis=1, tiled=True)
    amp_local = moved.reshape(irrep_local * VIR_CAP * OCC_CAP, moved.shape[3])
    amp_panel = lax.all_gather(amp_local, "row", axis=0, tiled=True)
    ints_panel = lax.all_gather(cycle_ints, "col", axis=1, tiled=True)
    cycle = jnp.dot(ints_panel, amp_panel, preferred_element_type=F32)
    rows_here, cols_here = cycle.shape
    flat_energy = energy.reshape(-1)
    row_start, col_start = row_index * rows_here, col_index * cols_here
    row_energy = lax.dynamic_slice_in_dim(flat_energy, row_start, rows_here, 0)
    col_energy = lax.dynamic_slice_in_dim(flat_energy, col_start, cols_here, 0)
    row_live = lax.dynamic_slice_in_dim(full_live, row_start, rows_here, 0)
    col_live = lax.dynamic_slice_in_dim(full_live, col_start, cols_here, 0)
    denom = row_energy[:, None] + col_energy[None, :]
    return jnp.where(row_live[:, None] & col_live[None, :], cycle / denom, F32(0.0))


def solution(mesh):
    nrow, ncol = mesh.shape["row"], mesh.shape["col"]
    placed = (P("row", None, None, None, "col", None), P("row", "col"), P(), P(), P(), P(), P())
    body = any_device
    if 2 * nrow == NIRREP and ncol == NIRREP:
        body = functools.partial(live_device, nrow, ncol)
    return jax.shard_map(body, mesh=mesh, in_specs=placed, out_specs=P("row", "col"), check_vma=False)
```

```python
import functools

import jax
import jax.numpy as jnp
from jax import lax
from jax.experimental import pallas as pl
from jax.experimental.pallas import tpu as pltpu
from jax.sharding import PartitionSpec as P

NIRREP = 8
OCC_CAP = 16
VIR_CAP = 64
BLOCK = VIR_CAP * OCC_CAP
SIZES = (640, 768, 896, 1024)
F32 = jnp.float32
BF16 = jnp.bfloat16
I32 = jnp.int32
VMEM_BYTES = 56 * 1024 * 1024


def iota(shape, dim):
    return lax.broadcasted_iota(I32, shape, dim)


def params():
    return pltpu.CompilerParams(vmem_limit_bytes=VMEM_BYTES)


def cost(flops, nbytes):
    return pl.CostEstimate(flops=flops, bytes_accessed=nbytes, transcendentals=0)


def pair_scalars(occ, virt, win, pair):
    first = 2 * pair
    o_a, o_b = occ[first], occ[first + 1]
    v_a, v_b = virt[first ^ win[0]], virt[(first + 1) ^ win[0]]
    return (o_a, o_b), (v_a, v_b), (o_a * ((v_a + 1) >> 1), o_a * (v_a >> 1))


def place(q, p, second, counts):
    (o_a, o_b), (v_a, v_b), (start_even, start_odd) = counts
    o = jnp.where(second, o_b, o_a)
    v = jnp.where(second, v_b, v_a)
    start = jnp.where(second, jnp.where((q & 1) == 0, start_even, start_odd), 0)
    return jnp.where((p < o) & (q < v), start + (q >> 1) * o + p, -1)


def one_hot(left, right):
    return jnp.where(left == right, 1.0, 0.0).astype(BF16)


def dot(a, b):
    return jnp.dot(a, b, preferred_element_type=F32)


def prep_kernel(size, occ, virt, win, t2_ref, even_ref, odd_ref, x_ref):
    counts = pair_scalars(occ, virt, win, pl.program_id(0))
    row = iota((256, 1), 0)
    source = (((row >> 6) & 1) << 7) | (((row >> 2) & 15) << 3) | ((row & 3) << 1) | (row >> 7)
    by_parity = one_hot(iota((256, 256), 1), source)
    targets = []
    for half in range(2):
        for group in range(4):
            parts = [
                t2_ref[:, half, :, 4 * group + i].astype(F32).reshape(256, VIR_CAP) for i in range(4)
            ]
            x = jnp.concatenate(parts, axis=1).astype(BF16)
            at = (4 * half + group) * 256
            x_ref[:, at : at + 256] = dot(by_parity, x).astype(BF16)
            r = iota((256, 1), 0)
            p, q = 4 * group + (r >> 6), r & 63
            spot = place(q, p, half == 1, counts)
            targets.append(jnp.where(spot >= 0, spot + (q & 1) * size, -1))
    for start in range(0, 2 * size, 256):
        acc = jnp.zeros((256, 256), F32)
        lane = iota((256, 256), 1) + start
        for chunk in range(8):
            acc += dot(x_ref[:, chunk * 256 : chunk * 256 + 256], one_hot(targets[chunk], lane))
        acc = acc.astype(BF16)
        for part in range(2):
            at_col = start + 128 * part
            core, col = at_col // size, at_col % size
            tile = acc[:, 128 * part : 128 * part + 128]
            even_ref[core, :, col : col + 128] = tile[:128]
            odd_ref[core, :, col : col + 128] = tile[128:]


def prep(size, scalars, t2):
    shape = jax.ShapeDtypeStruct((NIRREP, 128, size), BF16)
    block = pl.BlockSpec((2, 128, size), lambda k, *_: (k, 0, 0))
    return pl.pallas_call(
        functools.partial(prep_kernel, size),
        out_shape=(shape, shape),
        grid_spec=pltpu.PrefetchScalarGridSpec(
            num_scalar_prefetch=3,
            grid=(NIRREP // 2,),
            in_specs=[
                pl.BlockSpec((2, 2, OCC_CAP, OCC_CAP, 8, VIR_CAP), lambda k, *_: (0, k, 0, 0, 0, 0))
            ],
            out_specs=[block, block],
            scratch_shapes=[pltpu.VMEM((256, 2048), BF16)],
        ),
        compiler_params=params(),
        cost_estimate=cost(2 * 4 * 256 * 2048 * 2 * size, 12 * 2**20),
        name="prep_amplitudes",
    )(*scalars, t2)


def fill_rows(rows, spot, sel_ref):
    for first in range(0, rows, 32):
        sel_ref[first : first + 32, :] = one_hot(iota((32, BLOCK), 0) + first, spot)


def rows_kernel(rows, parity, count, occ, virt, win, at, x_ref, *refs):
    out_ref, sel_ref = refs[count], refs[-1]
    counts = pair_scalars(occ, virt, win, at[0])
    i = iota((1, BLOCK), 1)
    q = 8 * (i >> 7) + 2 * (i & 3) + parity
    spot = place(q, (i >> 2) & 15, ((i >> 6) & 1) == 1, counts)
    fill_rows(rows, spot, sel_ref)
    cols = out_ref.shape[1]

    @pl.loop(0, -(-cols // 256))
    def _(n):
        lanes = pl.ds(pl.multiple_of(jnp.minimum(n * 256, cols - 256), 128), 256)
        out_ref[:, lanes] = dot(sel_ref[...], x_ref[:, :, lanes].reshape(BLOCK, 256)).astype(BF16)


def compact_rows(rows, cols, parity, scalars, at, x, passed=(), awaited=()):
    whole = pl.BlockSpec(memory_space=pl.ANY)
    return pl.pallas_call(
        functools.partial(rows_kernel, rows, parity, len(passed) + len(awaited)),
        out_shape=[jax.ShapeDtypeStruct((rows, cols), BF16)]
        + [jax.ShapeDtypeStruct(y.shape, y.dtype) for y in passed],
        grid_spec=pltpu.PrefetchScalarGridSpec(
            num_scalar_prefetch=4,
            grid=(1,),
            in_specs=[pl.BlockSpec((NIRREP, 128, cols), lambda n, *_: (0, 0, 0))]
            + [whole] * (len(passed) + len(awaited)),
            out_specs=[pl.BlockSpec((rows, cols), lambda n, *_: (0, 0))] + [whole] * len(passed),
            scratch_shapes=[pltpu.VMEM((rows, BLOCK), BF16)],
        ),
        input_output_aliases={5 + i: 1 + i for i in range(len(passed))},
        compiler_params=params(),
        cost_estimate=cost(4 * rows * BLOCK * cols, 4 * rows * BLOCK),
        name="compact_rows",
    )(*scalars, at, x, *passed, *awaited)


def ints_kernel(rows, cols, occ, virt, win, at, mine_ref, other_ref, awaited, out_ref, sel_ref, cols_ref):
    plane, dev = at[0], at[1]
    parity = dev & 1

    @pl.when(pl.program_id(0) == 0)
    def _():
        counts = pair_scalars(occ, virt, win, plane)
        i = iota((1, BLOCK), 1)
        q = 2 * ((i >> 4) & 31) + parity
        spot = place(q, i & 15, (i >> 9) == 1, counts)
        fill_rows(rows, spot, sel_ref)

    counts = pair_scalars(occ, virt, win, dev >> 1)
    i = iota((BLOCK, 1), 0)
    q, p = i >> 4, i & 15
    lane = iota((BLOCK, 256), 1) + pl.program_id(0) * 256
    picks = []
    for second in (parity == 1, parity == 0):
        spot = place(q, p, second, counts)
        picks.append(one_hot(jnp.where(spot >= 0, spot + (q & 1) * cols, -1), lane))

    @pl.loop(0, 2)
    def _(half):
        at_rows = pl.ds(pl.multiple_of(half * (BLOCK // 2), BLOCK // 2), BLOCK // 2)
        acc = dot(mine_ref[half].reshape(BLOCK // 2, BLOCK), picks[0])
        acc += dot(other_ref[at_rows, :], picks[1])
        cols_ref[at_rows, :] = acc.astype(BF16)

    out_ref[...] = dot(sel_ref[...], cols_ref[...]).astype(BF16)


def compact_ints(rows, cols, scalars, at, mine, other, awaited):
    mine_spec = pl.BlockSpec(
        (2, VIR_CAP // 2, 1, OCC_CAP, BLOCK), lambda n, o, v, w, a: (0, 0, a[1] & 1, 0, 0)
    )
    whole = pl.BlockSpec((BLOCK, BLOCK), lambda n, *_: (0, 0))
    return pl.pallas_call(
        functools.partial(ints_kernel, rows, cols),
        out_shape=jax.ShapeDtypeStruct((rows, 2 * cols), BF16),
        grid_spec=pltpu.PrefetchScalarGridSpec(
            num_scalar_prefetch=4,
            grid=(2 * cols // 256,),
            in_specs=[mine_spec, whole, pl.BlockSpec(memory_space=pl.ANY)],
            out_specs=pl.BlockSpec((rows, 256), lambda n, *_: (0, n)),
            scratch_shapes=[pltpu.VMEM((rows, BLOCK), BF16), pltpu.VMEM((BLOCK, 256), BF16)],
        ),
        compiler_params=params(),
        cost_estimate=cost(16 * BLOCK * BLOCK * cols, 4 * BLOCK * BLOCK + 4 * rows * cols),
        name="compact_ints",
    )(*scalars, at, mine, other, awaited)


def widen_tile(rows, cols, tile, occ, virt, win, dev, own_refs, sib_refs, wide_ref):
    parity = dev & 1
    counts = pair_scalars(occ, virt, win, dev >> 1)
    (o_a, o_b), _, (start_even, start_odd) = counts
    second = parity == 1
    o = jnp.where(second, o_b, o_a)
    i = iota((1, 256), 1) + tile * 256
    q = i >> 4
    spot = place(q, i & 15, second, counts)
    r = iota((256, 256), 0)
    picks = []
    for s in (parity, 1 - parity):
        start = jnp.where(second, jnp.where(s == 0, start_even, start_odd), 0) + 8 * tile * o
        start = jnp.minimum((start >> 7) << 7, cols - 256)
        window = pl.ds(pl.multiple_of(start, 128), 256)
        picks.append((window, one_hot(r + start, jnp.where((q & 1) == s, spot, -1))))
    for piece in range(2):
        x = dot(own_refs[piece][:, picks[0][0]], picks[0][1])
        x += dot(sib_refs[piece][:, picks[1][0]], picks[1][1])
        wide_ref[piece * cols : piece * cols + rows, :] = x.astype(BF16)
        if rows < cols:
            wide_ref[piece * cols + rows : (piece + 1) * cols, :] = jnp.zeros((cols - rows, 256), BF16)


def widen_kernel(rows, cols, slots, occ, virt, win, at, *refs):
    wide_ref = refs[-1]
    for slot in range(slots):

        @pl.when(pl.program_id(0) == slot)
        def _():
            t0, t1, s0, s1 = refs[4 * slot : 4 * slot + 4]
            tile = pl.program_id(1)
            widen_tile(rows, cols, tile, occ, virt, win, at[1], (t0, t1), (s0, s1), wide_ref.at[0])


def widen(rows, cols, scalars, at, blocks):
    slots = len(blocks) // 4
    square = pl.BlockSpec((rows, cols), lambda t, n, *_: (0, 0), pipeline_mode=pl.Buffered(1))
    return pl.pallas_call(
        functools.partial(widen_kernel, rows, cols, slots),
        out_shape=jax.ShapeDtypeStruct((slots, 2 * cols, BLOCK), BF16),
        grid_spec=pltpu.PrefetchScalarGridSpec(
            num_scalar_prefetch=4,
            grid=(slots, BLOCK // 256),
            in_specs=[square] * len(blocks),
            out_specs=pl.BlockSpec((1, 2 * cols, 256), lambda t, n, *_: (t, 0, n)),
        ),
        compiler_params=params(),
        cost_estimate=cost(slots * 8 * rows * 512 * BLOCK, slots * (8 * rows * cols + 4 * cols * BLOCK)),
        name="widen",
    )(*scalars, at, *blocks)


def product_kernel(inner, ints_ref, wide_ref, acc_ref):
    at = pl.ds(pl.multiple_of(pl.program_id(1) * 256, 256), 256)

    @pl.when(pl.program_id(0) == 0)
    def _():
        acc_ref[:, :, at] = jnp.zeros((2, acc_ref.shape[1], 256), F32)

    @pl.loop(0, 2)
    def _(half):
        acc_ref[half, :, at] += dot(ints_ref[0, half], wide_ref[0])


def product(rows, cols, inner, ints, wide):
    slots = wide.shape[0]
    return pl.pallas_call(
        product_kernel,
        out_shape=jax.ShapeDtypeStruct((2, rows, BLOCK), F32),
        grid_spec=pltpu.PrefetchScalarGridSpec(
            num_scalar_prefetch=1,
            grid=(slots, BLOCK // 256),
            in_specs=[
                pl.BlockSpec((1, 2, rows, 2 * cols), lambda t, n, k: (k[t], 0, 0, 0)),
                pl.BlockSpec((1, 2 * cols, 256), lambda t, n, k: (t, 0, n)),
            ],
            out_specs=pl.BlockSpec((2, rows, BLOCK), lambda t, n, k: (0, 0, 0)),
        ),
        compiler_params=params(),
        cost_estimate=cost(16 * slots * rows * cols * BLOCK, slots * 4 * cols * (rows + BLOCK)),
        name="product",
    )(inner, ints, wide)


def last_kernel(
    rows, cols, occ, virt, win, at, inner,
    ints_ref, t0, t1, s0, s1, old_ref, evirt, eocc_ref, ecol_ref, out_ref, wide_ref, sum_ref,
):
    plane, dev = at[0], at[1]
    widen_tile(rows, cols, pl.program_id(0), occ, virt, win, dev, (t0, t1), (s0, s1), wide_ref)

    @pl.loop(0, 2)
    def _(half):
        sum_ref[half, :rows, :] = old_ref[half] + dot(ints_ref[0, half], wide_ref[...])

    i = iota((1, 256), 1) + pl.program_id(0) * 256
    col_live = ((i & 15) < occ[dev]) & ((i >> 4) < virt[dev ^ win[0]])
    col_energy = ecol_ref[...]
    _, _, starts = pair_scalars(occ, virt, win, plane)
    p = iota((OCC_CAP, 1), 0)
    irreps = [2 * plane, 2 * plane + 1]
    occs = [occ[irrep] for irrep in irreps]
    partners = [irrep ^ win[0] for irrep in irreps]
    virts = [virt[partner] for partner in partners]
    live = [(p < o) & col_live for o in occs]

    @pl.loop(0, VIR_CAP // 8)
    def _(group):
        for h in range(2):
            for i in range(8):
                half_q, s = 4 * group + i // 2, i % 2
                q = 2 * half_q + s
                start = half_q * occs[h]
                if h == 1:
                    start = start + starts[s]
                start = jnp.minimum(start, rows)
                block = sum_ref[s, pl.ds(pl.multiple_of((start >> 3) << 3, 8), OCC_CAP + 8), :]
                block = pltpu.roll(block, OCC_CAP + 8 - (start & 7), 0)[:OCC_CAP]
                denom = (eocc_ref[h] - evirt[partners[h], q]) + col_energy
                value = jnp.where(live[h] & (q < virts[h]), block / denom, 0.0)
                at_row = pl.multiple_of((h * VIR_CAP + q) * OCC_CAP, OCC_CAP)
                out_ref[pl.ds(at_row, OCC_CAP), :] = value


def last(rows, cols, scalars, at, inner, ints, own, sib, acc, energies):
    square = pl.BlockSpec((rows, cols), lambda n, *_: (0, 0))
    return pl.pallas_call(
        functools.partial(last_kernel, rows, cols),
        out_shape=jax.ShapeDtypeStruct((2 * BLOCK, BLOCK), F32),
        grid_spec=pltpu.PrefetchScalarGridSpec(
            num_scalar_prefetch=5,
            grid=(BLOCK // 256,),
            in_specs=[
                pl.BlockSpec((1, 2, rows, 2 * cols), lambda n, o, v, w, a, k: (k[0], 0, 0, 0)),
                square, square, square, square,
                pl.BlockSpec((2, rows, 256), lambda n, *_: (0, 0, n)),
                pl.BlockSpec(memory_space=pltpu.SMEM),
                pl.BlockSpec((2, OCC_CAP, 1), lambda n, *_: (0, 0, 0)),
                pl.BlockSpec((1, 256), lambda n, *_: (0, n)),
            ],
            out_specs=pl.BlockSpec((2 * BLOCK, 256), lambda n, *_: (0, n)),
            scratch_shapes=[
                pltpu.VMEM((2 * cols, 256), BF16),
                pltpu.VMEM((2, rows + OCC_CAP + 8, 256), F32),
            ],
        ),
        compiler_params=params(),
        cost_estimate=cost(16 * rows * cols * BLOCK, 8 * rows * cols + 16 * rows * BLOCK),
        name="last_product",
    )(*scalars, at, inner, ints, *own, *sib, acc, *energies)


def after_kernel(*refs):
    pass


def after(kept, awaited):
    whole = pl.BlockSpec(memory_space=pl.ANY)
    return pl.pallas_call(
        after_kernel,
        out_shape=[jax.ShapeDtypeStruct(x.shape, x.dtype) for x in kept],
        in_specs=[whole] * (len(kept) + len(awaited)),
        out_specs=[whole] * len(kept),
        input_output_aliases={i: i for i in range(len(kept))},
        name="after",
    )(*kept, *awaited)


def ring_order(n):
    return list(range(0, 1)) + list(range(1, n, 2)) + [i for i in range(n - 1, 0, -1) if i % 2 == 0]


def branch(rows, nrow, ncol, t2, ints, occ, virt, win, eps_virt, occ_rows, col_energy, at, sources):
    cols = -(-rows // 128) * 128
    scalars = (occ, virt, win)
    order = ring_order(nrow)
    ring = [(order[i], order[(i + 1) % nrow]) for i in range(nrow)]
    swap = [(c, c ^ 1) for c in range(ncol)]

    def to_sibling(x):
        return lax.ppermute(x, "col", swap)

    def around(x):
        return lax.ppermute(x, "row", ring)

    def exchange(x):
        return lax.all_to_all(x, "col", split_axis=0, concat_axis=0, tiled=True)

    even, odd = prep(cols, scalars, t2)
    even, odd = compact_rows(rows, cols, 0, scalars, at, exchange(even), passed=(odd,))
    mine = ints.reshape(2, VIR_CAP // 2, 2, OCC_CAP, BLOCK)
    other = lax.dynamic_index_in_dim(mine, 1 - (at[1] & 1), 2, keepdims=False).reshape(BLOCK, BLOCK)
    even_next = around(even)
    small = compact_ints(rows, cols, scalars, at, mine, to_sibling(other), even)
    odd, small = compact_rows(rows, cols, 1, scalars, at, exchange(odd), passed=(small,))
    odd, small = after([odd, small], [even_next])
    panel = lax.all_gather(small, "col", axis=0, tiled=False).reshape(ncol // 2, 2, rows, 2 * cols)

    held = [even, odd]
    blocks = []
    for step in range(nrow - 1):
        later = [even_next if step == 0 else around(held[0]), around(held[1])]
        blocks += held + [to_sibling(x) for x in held]
        held = later
    wide = widen(rows, cols, scalars, at, blocks)
    acc = product(rows, cols, sources[: nrow - 1], panel, wide)
    own = after(held, [acc])
    sib = [to_sibling(x) for x in own]
    energies = (eps_virt, occ_rows, col_energy)
    return last(rows, cols, scalars, at, sources[nrow - 1 :], panel, own, sib, acc, energies)


def choose_kernel(occ, virt, win, index_ref):
    index = jnp.int32(0)
    for pair in range(NIRREP // 2):
        (o_a, o_b), (v_a, v_b), _ = pair_scalars(occ, virt, win, pair)
        most = o_a * ((v_a + 1) >> 1) + o_b * ((v_b + 1) >> 1)
        need = sum((most > size).astype(I32) for size in SIZES[:-1])
        index = jnp.maximum(index, need)
    index_ref[0] = index


def choose(occ, virt, win):
    smem = pl.BlockSpec(memory_space=pltpu.SMEM)
    return pl.pallas_call(
        choose_kernel,
        out_shape=jax.ShapeDtypeStruct((1,), I32),
        in_specs=[smem] * 3,
        out_specs=smem,
        name="choose",
    )(occ, virt, win)[0]


def live_device(nrow, ncol, t2, ints, eps_occ, eps_virt, occ, virt, win):
    row, col = lax.axis_index("row"), lax.axis_index("col")
    index = choose(occ, virt, win)
    occ_rows = lax.dynamic_slice(eps_occ, (2 * row, 0), (2, OCC_CAP)).reshape(2, OCC_CAP, 1)
    col_occ = lax.dynamic_slice(eps_occ, (col, 0), (1, OCC_CAP))
    col_virt = lax.dynamic_slice(eps_virt, (col ^ win[0], 0), (1, VIR_CAP))
    col_energy = (col_occ[:, None, :] - col_virt[:, :, None]).reshape(1, BLOCK)
    at = jnp.stack([row, col]).astype(I32)
    order = ring_order(nrow)
    table = [[order[(order.index(z) - t) % nrow] for t in range(nrow)] for z in range(nrow)]
    sources = lax.dynamic_slice(jnp.array(table, I32), (row, 0), (1, nrow)).reshape(nrow)
    operands = (t2, ints, occ, virt, win, eps_virt, occ_rows, col_energy, at, sources)
    return lax.switch(index, [functools.partial(branch, size, nrow, ncol) for size in SIZES], *operands)


def ph_vectors(eps_occ, eps_virt, occ_count, virt_count, window_irrep):
    irreps = jnp.arange(NIRREP, dtype=I32)
    partner = jnp.bitwise_xor(irreps, window_irrep[0])
    onehot = partner[:, None] == irreps[None, :]
    virt_rows = jnp.dot(onehot.astype(F32), eps_virt, precision=lax.Precision.HIGHEST)
    virt_live = jnp.sum(jnp.where(onehot, virt_count[None, :], 0), axis=1)
    energy = eps_occ[:, None, :] - virt_rows[:, :, None]
    slots_occ = jnp.arange(OCC_CAP, dtype=I32)
    slots_virt = jnp.arange(VIR_CAP, dtype=I32)
    live = (slots_occ[None, None, :] < occ_count[:, None, None]) & (
        slots_virt[None, :, None] < virt_live[:, None, None]
    )
    return (energy, live)


def any_device(t2_pairs, cycle_ints, eps_occ, eps_virt, occ_count, virt_count, window_irrep):
    irrep_local = t2_pairs.shape[0]
    virt_local = t2_pairs.shape[4]
    total = NIRREP * VIR_CAP * OCC_CAP
    energy, live = ph_vectors(eps_occ, eps_virt, occ_count, virt_count, window_irrep)
    row_index = lax.axis_index("row")
    col_index = lax.axis_index("col")
    zero_index = jnp.int32(0)
    source_live = lax.dynamic_slice(
        live,
        (row_index * irrep_local, col_index * virt_local, zero_index),
        (irrep_local, virt_local, OCC_CAP),
    )
    full_live = live.reshape(-1)
    ordered = jnp.transpose(t2_pairs, (0, 4, 2, 1, 5, 3)).reshape(
        irrep_local, virt_local, OCC_CAP, total
    )
    keep = source_live[:, :, :, None] & full_live[None, None, None, :]
    ordered = jnp.where(keep, ordered, jnp.zeros_like(ordered))
    moved = lax.all_to_all(ordered, "col", split_axis=3, concat_axis=1, tiled=True)
    amp_local = moved.reshape(irrep_local * VIR_CAP * OCC_CAP, moved.shape[3])
    amp_panel = lax.all_gather(amp_local, "row", axis=0, tiled=True)
    ints_panel = lax.all_gather(cycle_ints, "col", axis=1, tiled=True)
    cycle = jnp.dot(ints_panel, amp_panel, preferred_element_type=F32)
    rows_here, cols_here = cycle.shape
    flat_energy = energy.reshape(-1)
    row_start, col_start = row_index * rows_here, col_index * cols_here
    row_energy = lax.dynamic_slice_in_dim(flat_energy, row_start, rows_here, 0)
    col_energy = lax.dynamic_slice_in_dim(flat_energy, col_start, cols_here, 0)
    row_live = lax.dynamic_slice_in_dim(full_live, row_start, rows_here, 0)
    col_live = lax.dynamic_slice_in_dim(full_live, col_start, cols_here, 0)
    denom = row_energy[:, None] + col_energy[None, :]
    return jnp.where(row_live[:, None] & col_live[None, :], cycle / denom, F32(0.0))


def solution(mesh):
    nrow, ncol = mesh.shape["row"], mesh.shape["col"]
    placed = (P("row", None, None, None, "col", None), P("row", "col"), P(), P(), P(), P(), P())
    body = any_device
    if 2 * nrow == NIRREP and ncol == NIRREP:
        body = functools.partial(live_device, nrow, ncol)
    return jax.shard_map(body, mesh=mesh, in_specs=placed, out_specs=P("row", "col"), check_vma=False)
```

```python
import functools

import jax
import jax.numpy as jnp
from jax import lax
from jax.experimental import pallas as pl
from jax.experimental.pallas import tpu as pltpu
from jax.sharding import PartitionSpec as P

NIRREP = 8
OCC_CAP = 16
VIR_CAP = 64
BLOCK = VIR_CAP * OCC_CAP
SIZES = (1024, 896, 768, 640)
WIDE = 512
F32 = jnp.float32
BF16 = jnp.bfloat16
I32 = jnp.int32
VMEM_BYTES = 56 * 1024 * 1024


def iota(shape, dim):
    return lax.broadcasted_iota(I32, shape, dim)


def params():
    return pltpu.CompilerParams(vmem_limit_bytes=VMEM_BYTES)


def cost(flops, nbytes):
    return pl.CostEstimate(flops=flops, bytes_accessed=nbytes, transcendentals=0)


def pair_scalars(occ, virt, win, pair):
    first = 2 * pair
    o_a, o_b = occ[first], occ[first + 1]
    v_a, v_b = virt[first ^ win[0]], virt[(first + 1) ^ win[0]]
    return (o_a, o_b), (v_a, v_b), (o_a * ((v_a + 1) >> 1), o_a * (v_a >> 1))


def place(q, p, second, counts):
    (o_a, o_b), (v_a, v_b), (start_even, start_odd) = counts
    o = jnp.where(second, o_b, o_a)
    v = jnp.where(second, v_b, v_a)
    start = jnp.where(second, jnp.where((q & 1) == 0, start_even, start_odd), 0)
    return jnp.where((p < o) & (q < v), start + (q >> 1) * o + p, -1)


def one_hot(left, right):
    return jnp.where(left == right, 1.0, 0.0).astype(BF16)


def dot(a, b):
    return jnp.dot(a, b, preferred_element_type=F32)


def prep_kernel(size, occ, virt, win, t2_ref, even_ref, odd_ref, x_ref):
    counts = pair_scalars(occ, virt, win, pl.program_id(0))
    row = iota((256, 1), 0)
    source = (((row >> 6) & 1) << 7) | (((row >> 2) & 15) << 3) | ((row & 3) << 1) | (row >> 7)
    by_parity = one_hot(iota((256, 256), 1), source)
    targets = []
    for half in range(2):
        for group in range(4):
            parts = [
                t2_ref[:, half, :, 4 * group + i].astype(F32).reshape(256, VIR_CAP) for i in range(4)
            ]
            x = jnp.concatenate(parts, axis=1).astype(BF16)
            at = (4 * half + group) * 256
            x_ref[:, at : at + 256] = dot(by_parity, x).astype(BF16)
            r = iota((256, 1), 0)
            p, q = 4 * group + (r >> 6), r & 63
            spot = place(q, p, half == 1, counts)
            targets.append(jnp.where(spot >= 0, spot + (q & 1) * size, -1))
    for start in range(0, 2 * size, 256):
        acc = jnp.zeros((256, 256), F32)
        lane = iota((256, 256), 1) + start
        for chunk in range(8):
            acc += dot(x_ref[:, chunk * 256 : chunk * 256 + 256], one_hot(targets[chunk], lane))
        acc = acc.astype(BF16)
        for part in range(2):
            at_col = start + 128 * part
            core, col = at_col // size, at_col % size
            tile = acc[:, 128 * part : 128 * part + 128]
            even_ref[core, :, col : col + 128] = tile[:128]
            odd_ref[core, :, col : col + 128] = tile[128:]


def prep(size, scalars, t2):
    shape = jax.ShapeDtypeStruct((NIRREP, 128, size), BF16)
    block = pl.BlockSpec((2, 128, size), lambda k, *_: (k, 0, 0))
    return pl.pallas_call(
        functools.partial(prep_kernel, size),
        out_shape=(shape, shape),
        grid_spec=pltpu.PrefetchScalarGridSpec(
            num_scalar_prefetch=3,
            grid=(NIRREP // 2,),
            in_specs=[
                pl.BlockSpec((2, 2, OCC_CAP, OCC_CAP, 8, VIR_CAP), lambda k, *_: (0, k, 0, 0, 0, 0))
            ],
            out_specs=[block, block],
            scratch_shapes=[pltpu.VMEM((256, 2048), BF16)],
        ),
        compiler_params=params(),
        cost_estimate=cost(2 * 4 * 256 * 2048 * 2 * size, 12 * 2**20),
        name="prep_amplitudes",
    )(*scalars, t2)


def fill_rows(rows, spot, sel_ref):
    for first in range(0, rows, 32):
        sel_ref[first : first + 32, :] = one_hot(iota((32, BLOCK), 0) + first, spot)


def rows_kernel(rows, parity, count, occ, virt, win, at, x_ref, *refs):
    out_ref, sel_ref = refs[count], refs[-1]
    counts = pair_scalars(occ, virt, win, at[0])
    i = iota((1, BLOCK), 1)
    q = 8 * (i >> 7) + 2 * (i & 3) + parity
    spot = place(q, (i >> 2) & 15, ((i >> 6) & 1) == 1, counts)
    fill_rows(rows, spot, sel_ref)
    cols = out_ref.shape[1]

    @pl.loop(0, -(-cols // 256))
    def _(n):
        lanes = pl.ds(pl.multiple_of(jnp.minimum(n * 256, cols - 256), 128), 256)
        out_ref[:, lanes] = dot(sel_ref[...], x_ref[:, :, lanes].reshape(BLOCK, 256)).astype(BF16)


def compact_rows(rows, cols, parity, scalars, at, x, passed=(), awaited=()):
    whole = pl.BlockSpec(memory_space=pl.ANY)
    return pl.pallas_call(
        functools.partial(rows_kernel, rows, parity, len(passed) + len(awaited)),
        out_shape=[jax.ShapeDtypeStruct((rows, cols), BF16)]
        + [jax.ShapeDtypeStruct(y.shape, y.dtype) for y in passed],
        grid_spec=pltpu.PrefetchScalarGridSpec(
            num_scalar_prefetch=4,
            grid=(1,),
            in_specs=[pl.BlockSpec((NIRREP, 128, cols), lambda n, *_: (0, 0, 0))]
            + [whole] * (len(passed) + len(awaited)),
            out_specs=[pl.BlockSpec((rows, cols), lambda n, *_: (0, 0))] + [whole] * len(passed),
            scratch_shapes=[pltpu.VMEM((rows, BLOCK), BF16)],
        ),
        input_output_aliases={5 + i: 1 + i for i in range(len(passed))},
        compiler_params=params(),
        cost_estimate=cost(4 * rows * BLOCK * cols, 4 * rows * BLOCK),
        name="compact_rows",
    )(*scalars, at, x, *passed, *awaited)


def ints_kernel(rows, cols, occ, virt, win, at, mine_ref, other_ref, awaited, out_ref, sel_ref, cols_ref):
    plane, dev = at[0], at[1]
    parity = dev & 1

    @pl.when(pl.program_id(0) == 0)
    def _():
        counts = pair_scalars(occ, virt, win, plane)
        i = iota((1, BLOCK), 1)
        q = 2 * ((i >> 4) & 31) + parity
        spot = place(q, i & 15, (i >> 9) == 1, counts)
        fill_rows(rows, spot, sel_ref)

    counts = pair_scalars(occ, virt, win, dev >> 1)
    i = iota((BLOCK, 1), 0)
    q, p = i >> 4, i & 15
    lane = iota((BLOCK, 256), 1) + pl.program_id(0) * 256
    picks = []
    for second in (parity == 1, parity == 0):
        spot = place(q, p, second, counts)
        picks.append(one_hot(jnp.where(spot >= 0, spot + (q & 1) * cols, -1), lane))

    @pl.loop(0, 2)
    def _(half):
        at_rows = pl.ds(pl.multiple_of(half * (BLOCK // 2), BLOCK // 2), BLOCK // 2)
        acc = dot(mine_ref[half].reshape(BLOCK // 2, BLOCK), picks[0])
        acc += dot(other_ref[at_rows, :], picks[1])
        cols_ref[at_rows, :] = acc.astype(BF16)

    out_ref[...] = dot(sel_ref[...], cols_ref[...]).astype(BF16)


def compact_ints(rows, cols, scalars, at, mine, other, awaited):
    mine_spec = pl.BlockSpec(
        (2, VIR_CAP // 2, 1, OCC_CAP, BLOCK), lambda n, o, v, w, a: (0, 0, a[1] & 1, 0, 0)
    )
    whole = pl.BlockSpec((BLOCK, BLOCK), lambda n, *_: (0, 0))
    return pl.pallas_call(
        functools.partial(ints_kernel, rows, cols),
        out_shape=jax.ShapeDtypeStruct((rows, 2 * cols), BF16),
        grid_spec=pltpu.PrefetchScalarGridSpec(
            num_scalar_prefetch=4,
            grid=(2 * cols // 256,),
            in_specs=[mine_spec, whole, pl.BlockSpec(memory_space=pl.ANY)],
            out_specs=pl.BlockSpec((rows, 256), lambda n, *_: (0, n)),
            scratch_shapes=[pltpu.VMEM((rows, BLOCK), BF16), pltpu.VMEM((BLOCK, 256), BF16)],
        ),
        compiler_params=params(),
        cost_estimate=cost(16 * BLOCK * BLOCK * cols, 4 * BLOCK * BLOCK + 4 * rows * cols),
        name="compact_ints",
    )(*scalars, at, mine, other, awaited)


def widen_tile(rows, cols, tile, occ, virt, win, dev, own_refs, sib_refs, wide_ref):
    parity = dev & 1
    counts = pair_scalars(occ, virt, win, dev >> 1)
    (o_a, o_b), _, (start_even, start_odd) = counts
    second = parity == 1
    o = jnp.where(second, o_b, o_a)
    i = iota((1, 256), 1) + tile * 256
    q = i >> 4
    spot = place(q, i & 15, second, counts)
    r = iota((256, 256), 0)
    picks = []
    for s in (parity, 1 - parity):
        start = jnp.where(second, jnp.where(s == 0, start_even, start_odd), 0) + 8 * tile * o
        start = jnp.minimum((start >> 7) << 7, cols - 256)
        window = pl.ds(pl.multiple_of(start, 128), 256)
        picks.append((window, one_hot(r + start, jnp.where((q & 1) == s, spot, -1))))
    for piece in range(2):
        x = dot(own_refs[piece][:, picks[0][0]], picks[0][1])
        x += dot(sib_refs[piece][:, picks[1][0]], picks[1][1])
        wide_ref[piece * cols : piece * cols + rows, :] = x.astype(BF16)
        if rows < cols:
            wide_ref[piece * cols + rows : (piece + 1) * cols, :] = jnp.zeros((cols - rows, 256), BF16)


def widen_kernel(rows, cols, slots, occ, virt, win, at, *refs):
    wide_ref = refs[-1]
    for slot in range(slots):

        @pl.when(pl.program_id(0) == slot)
        def _():
            t0, t1, s0, s1 = refs[4 * slot : 4 * slot + 4]
            tile = pl.program_id(1)
            widen_tile(rows, cols, tile, occ, virt, win, at[1], (t0, t1), (s0, s1), wide_ref.at[0])


def widen(rows, cols, scalars, at, blocks):
    slots = len(blocks) // 4
    square = pl.BlockSpec((rows, cols), lambda t, n, *_: (0, 0), pipeline_mode=pl.Buffered(1))
    return pl.pallas_call(
        functools.partial(widen_kernel, rows, cols, slots),
        out_shape=jax.ShapeDtypeStruct((slots, 2 * cols, BLOCK), BF16),
        grid_spec=pltpu.PrefetchScalarGridSpec(
            num_scalar_prefetch=4,
            grid=(slots, BLOCK // 256),
            in_specs=[square] * len(blocks),
            out_specs=pl.BlockSpec((1, 2 * cols, 256), lambda t, n, *_: (t, 0, n)),
        ),
        compiler_params=params(),
        cost_estimate=cost(slots * 8 * rows * 512 * BLOCK, slots * (8 * rows * cols + 4 * cols * BLOCK)),
        name="widen",
    )(*scalars, at, *blocks)


def product_kernel(inner, ints_ref, wide_ref, acc_ref):
    at = pl.ds(pl.multiple_of(pl.program_id(1) * WIDE, WIDE), WIDE)

    @pl.when(pl.program_id(0) == 0)
    def _():
        acc_ref[:, :, at] = jnp.zeros((2, acc_ref.shape[1], WIDE), F32)

    @pl.loop(0, 2)
    def _(half):
        acc_ref[half, :, at] += dot(ints_ref[0, half], wide_ref[0])


def product(rows, cols, inner, ints, wide):
    slots = wide.shape[0]
    return pl.pallas_call(
        product_kernel,
        out_shape=jax.ShapeDtypeStruct((2, rows, BLOCK), F32),
        grid_spec=pltpu.PrefetchScalarGridSpec(
            num_scalar_prefetch=1,
            grid=(slots, BLOCK // WIDE),
            in_specs=[
                pl.BlockSpec((1, 2, rows, 2 * cols), lambda t, n, k: (k[t], 0, 0, 0)),
                pl.BlockSpec((1, 2 * cols, WIDE), lambda t, n, k: (t, 0, n)),
            ],
            out_specs=pl.BlockSpec((2, rows, BLOCK), lambda t, n, k: (0, 0, 0)),
        ),
        compiler_params=params(),
        cost_estimate=cost(16 * slots * rows * cols * BLOCK, slots * 4 * cols * (rows + BLOCK)),
        name="product",
    )(inner, ints, wide)


def last_kernel(
    rows, cols, occ, virt, win, at, inner,
    ints_ref, t0, t1, s0, s1, old_ref, evirt, eocc_ref, ecol_ref, out_ref, wide_ref, sum_ref,
):
    plane, dev = at[0], at[1]

    @pl.loop(0, WIDE // 256)
    def _(part):
        tile = pl.program_id(0) * (WIDE // 256) + part
        into = wide_ref.at[:, pl.ds(pl.multiple_of(part * 256, 256), 256)]
        widen_tile(rows, cols, tile, occ, virt, win, dev, (t0, t1), (s0, s1), into)

    @pl.loop(0, 2)
    def _(half):
        sum_ref[half, :rows, :] = old_ref[half] + dot(ints_ref[0, half], wide_ref[...])

    i = iota((1, WIDE), 1) + pl.program_id(0) * WIDE
    col_live = ((i & 15) < occ[dev]) & ((i >> 4) < virt[dev ^ win[0]])
    col_energy = ecol_ref[...]
    _, _, starts = pair_scalars(occ, virt, win, plane)
    p = iota((OCC_CAP, 1), 0)
    irreps = [2 * plane, 2 * plane + 1]
    occs = [occ[irrep] for irrep in irreps]
    partners = [irrep ^ win[0] for irrep in irreps]
    virts = [virt[partner] for partner in partners]
    live = [(p < o) & col_live for o in occs]

    @pl.loop(0, VIR_CAP // 4)
    def _(group):
        for h in range(2):
            for i in range(4):
                half_q, s = 2 * group + i // 2, i % 2
                q = 2 * half_q + s
                start = half_q * occs[h]
                if h == 1:
                    start = start + starts[s]
                start = jnp.minimum(start, rows)
                block = sum_ref[s, pl.ds(pl.multiple_of((start >> 3) << 3, 8), OCC_CAP + 8), :]
                block = pltpu.roll(block, OCC_CAP + 8 - (start & 7), 0)[:OCC_CAP]
                denom = (eocc_ref[h] - evirt[partners[h], q]) + col_energy
                value = jnp.where(live[h] & (q < virts[h]), block / denom, 0.0)
                at_row = pl.multiple_of((h * VIR_CAP + q) * OCC_CAP, OCC_CAP)
                out_ref[pl.ds(at_row, OCC_CAP), :] = value


def last(rows, cols, scalars, at, inner, ints, own, sib, acc, energies):
    square = pl.BlockSpec((rows, cols), lambda n, *_: (0, 0))
    return pl.pallas_call(
        functools.partial(last_kernel, rows, cols),
        out_shape=jax.ShapeDtypeStruct((2 * BLOCK, BLOCK), F32),
        grid_spec=pltpu.PrefetchScalarGridSpec(
            num_scalar_prefetch=5,
            grid=(BLOCK // WIDE,),
            in_specs=[
                pl.BlockSpec((1, 2, rows, 2 * cols), lambda n, o, v, w, a, k: (k[0], 0, 0, 0)),
                square, square, square, square,
                pl.BlockSpec((2, rows, WIDE), lambda n, *_: (0, 0, n)),
                pl.BlockSpec(memory_space=pltpu.SMEM),
                pl.BlockSpec((2, OCC_CAP, 1), lambda n, *_: (0, 0, 0)),
                pl.BlockSpec((1, WIDE), lambda n, *_: (0, n)),
            ],
            out_specs=pl.BlockSpec((2 * BLOCK, WIDE), lambda n, *_: (0, n)),
            scratch_shapes=[
                pltpu.VMEM((2 * cols, WIDE), BF16),
                pltpu.VMEM((2, rows + OCC_CAP + 8, WIDE), F32),
            ],
        ),
        compiler_params=params(),
        cost_estimate=cost(16 * rows * cols * BLOCK, 8 * rows * cols + 16 * rows * BLOCK),
        name="last_product",
    )(*scalars, at, inner, ints, *own, *sib, acc, *energies)


def after_kernel(*refs):
    pass


def after(kept, awaited):
    whole = pl.BlockSpec(memory_space=pl.ANY)
    return pl.pallas_call(
        after_kernel,
        out_shape=[jax.ShapeDtypeStruct(x.shape, x.dtype) for x in kept],
        in_specs=[whole] * (len(kept) + len(awaited)),
        out_specs=[whole] * len(kept),
        input_output_aliases={i: i for i in range(len(kept))},
        name="after",
    )(*kept, *awaited)


def ring_order(n):
    return list(range(0, 1)) + list(range(1, n, 2)) + [i for i in range(n - 1, 0, -1) if i % 2 == 0]


def branch(rows, nrow, ncol, t2, ints, occ, virt, win, eps_virt, occ_rows, col_energy, at, sources):
    cols = -(-rows // 128) * 128
    scalars = (occ, virt, win)
    order = ring_order(nrow)
    ring = [(order[i], order[(i + 1) % nrow]) for i in range(nrow)]
    swap = [(c, c ^ 1) for c in range(ncol)]

    def to_sibling(x):
        return lax.ppermute(x, "col", swap)

    def around(x):
        return lax.ppermute(x, "row", ring)

    def exchange(x):
        return lax.all_to_all(x, "col", split_axis=0, concat_axis=0, tiled=True)

    even, odd = prep(cols, scalars, t2)
    even, odd = compact_rows(rows, cols, 0, scalars, at, exchange(even), passed=(odd,))
    mine = ints.reshape(2, VIR_CAP // 2, 2, OCC_CAP, BLOCK)
    other = lax.dynamic_index_in_dim(mine, 1 - (at[1] & 1), 2, keepdims=False).reshape(BLOCK, BLOCK)
    even_next = around(even)
    small = compact_ints(rows, cols, scalars, at, mine, to_sibling(other), even)
    odd, small = compact_rows(rows, cols, 1, scalars, at, exchange(odd), passed=(small,))
    odd, small = after([odd, small], [even_next])
    panel = lax.all_gather(small, "col", axis=0, tiled=False).reshape(ncol // 2, 2, rows, 2 * cols)

    held = [even, odd]
    blocks = []
    for step in range(nrow - 1):
        later = [even_next if step == 0 else around(held[0]), around(held[1])]
        blocks += held + [to_sibling(x) for x in held]
        held = later
    wide = widen(rows, cols, scalars, at, blocks)
    acc = product(rows, cols, sources[: nrow - 1], panel, wide)
    own = after(held, [acc])
    sib = [to_sibling(x) for x in own]
    energies = (eps_virt, occ_rows, col_energy)
    return last(rows, cols, scalars, at, sources[nrow - 1 :], panel, own, sib, acc, energies)


def choose_kernel(occ, virt, win, index_ref):
    index = jnp.int32(len(SIZES) - 1)
    for pair in range(NIRREP // 2):
        (o_a, o_b), (v_a, v_b), _ = pair_scalars(occ, virt, win, pair)
        most = o_a * ((v_a + 1) >> 1) + o_b * ((v_b + 1) >> 1)
        fits = sum((most <= size).astype(I32) for size in SIZES[1:])
        index = jnp.minimum(index, fits)
    index_ref[0] = index


def choose(occ, virt, win):
    smem = pl.BlockSpec(memory_space=pltpu.SMEM)
    return pl.pallas_call(
        choose_kernel,
        out_shape=jax.ShapeDtypeStruct((1,), I32),
        in_specs=[smem] * 3,
        out_specs=smem,
        name="choose",
    )(occ, virt, win)[0]


def live_device(nrow, ncol, t2, ints, eps_occ, eps_virt, occ, virt, win):
    row, col = lax.axis_index("row"), lax.axis_index("col")
    index = choose(occ, virt, win)
    occ_rows = lax.dynamic_slice(eps_occ, (2 * row, 0), (2, OCC_CAP)).reshape(2, OCC_CAP, 1)
    col_occ = lax.dynamic_slice(eps_occ, (col, 0), (1, OCC_CAP))
    col_virt = lax.dynamic_slice(eps_virt, (col ^ win[0], 0), (1, VIR_CAP))
    col_energy = (col_occ[:, None, :] - col_virt[:, :, None]).reshape(1, BLOCK)
    at = jnp.stack([row, col]).astype(I32)
    order = ring_order(nrow)
    table = [[order[(order.index(z) - t) % nrow] for t in range(nrow)] for z in range(nrow)]
    sources = lax.dynamic_slice(jnp.array(table, I32), (row, 0), (1, nrow)).reshape(nrow)
    operands = (t2, ints, occ, virt, win, eps_virt, occ_rows, col_energy, at, sources)
    return lax.switch(index, [functools.partial(branch, size, nrow, ncol) for size in SIZES], *operands)


def ph_vectors(eps_occ, eps_virt, occ_count, virt_count, window_irrep):
    irreps = jnp.arange(NIRREP, dtype=I32)
    partner = jnp.bitwise_xor(irreps, window_irrep[0])
    onehot = partner[:, None] == irreps[None, :]
    virt_rows = jnp.dot(onehot.astype(F32), eps_virt, precision=lax.Precision.HIGHEST)
    virt_live = jnp.sum(jnp.where(onehot, virt_count[None, :], 0), axis=1)
    energy = eps_occ[:, None, :] - virt_rows[:, :, None]
    slots_occ = jnp.arange(OCC_CAP, dtype=I32)
    slots_virt = jnp.arange(VIR_CAP, dtype=I32)
    live = (slots_occ[None, None, :] < occ_count[:, None, None]) & (
        slots_virt[None, :, None] < virt_live[:, None, None]
    )
    return (energy, live)


def any_device(t2_pairs, cycle_ints, eps_occ, eps_virt, occ_count, virt_count, window_irrep):
    irrep_local = t2_pairs.shape[0]
    virt_local = t2_pairs.shape[4]
    total = NIRREP * VIR_CAP * OCC_CAP
    energy, live = ph_vectors(eps_occ, eps_virt, occ_count, virt_count, window_irrep)
    row_index = lax.axis_index("row")
    col_index = lax.axis_index("col")
    zero_index = jnp.int32(0)
    source_live = lax.dynamic_slice(
        live,
        (row_index * irrep_local, col_index * virt_local, zero_index),
        (irrep_local, virt_local, OCC_CAP),
    )
    full_live = live.reshape(-1)
    ordered = jnp.transpose(t2_pairs, (0, 4, 2, 1, 5, 3)).reshape(
        irrep_local, virt_local, OCC_CAP, total
    )
    keep = source_live[:, :, :, None] & full_live[None, None, None, :]
    ordered = jnp.where(keep, ordered, jnp.zeros_like(ordered))
    moved = lax.all_to_all(ordered, "col", split_axis=3, concat_axis=1, tiled=True)
    amp_local = moved.reshape(irrep_local * VIR_CAP * OCC_CAP, moved.shape[3])
    amp_panel = lax.all_gather(amp_local, "row", axis=0, tiled=True)
    ints_panel = lax.all_gather(cycle_ints, "col", axis=1, tiled=True)
    cycle = jnp.dot(ints_panel, amp_panel, preferred_element_type=F32)
    rows_here, cols_here = cycle.shape
    flat_energy = energy.reshape(-1)
    row_start, col_start = row_index * rows_here, col_index * cols_here
    row_energy = lax.dynamic_slice_in_dim(flat_energy, row_start, rows_here, 0)
    col_energy = lax.dynamic_slice_in_dim(flat_energy, col_start, cols_here, 0)
    row_live = lax.dynamic_slice_in_dim(full_live, row_start, rows_here, 0)
    col_live = lax.dynamic_slice_in_dim(full_live, col_start, cols_here, 0)
    denom = row_energy[:, None] + col_energy[None, :]
    return jnp.where(row_live[:, None] & col_live[None, :], cycle / denom, F32(0.0))


def solution(mesh):
    nrow, ncol = mesh.shape["row"], mesh.shape["col"]
    placed = (P("row", None, None, None, "col", None), P("row", "col"), P(), P(), P(), P(), P())
    body = any_device
    if 2 * nrow == NIRREP and ncol == NIRREP:
        body = functools.partial(live_device, nrow, ncol)
    return jax.shard_map(body, mesh=mesh, in_specs=placed, out_specs=P("row", "col"), check_vma=False)
```

```python
import functools

import jax
import jax.numpy as jnp
from jax import lax
from jax.experimental import pallas as pl
from jax.experimental.pallas import tpu as pltpu
from jax.sharding import PartitionSpec as P

NIRREP = 8
OCC_CAP = 16
VIR_CAP = 64
BLOCK = VIR_CAP * OCC_CAP
SIZES = (1024, 896, 768, 640)
WIDE = 512
F32 = jnp.float32
BF16 = jnp.bfloat16
I32 = jnp.int32
VMEM_BYTES = 56 * 1024 * 1024


def iota(shape, dim):
    return lax.broadcasted_iota(I32, shape, dim)


def params():
    return pltpu.CompilerParams(vmem_limit_bytes=VMEM_BYTES)


def cost(flops, nbytes):
    return pl.CostEstimate(flops=flops, bytes_accessed=nbytes, transcendentals=0)


def pair_scalars(occ, virt, win, pair):
    first = 2 * pair
    o_a, o_b = occ[first], occ[first + 1]
    v_a, v_b = virt[first ^ win[0]], virt[(first + 1) ^ win[0]]
    return (o_a, o_b), (v_a, v_b), (o_a * ((v_a + 1) >> 1), o_a * (v_a >> 1))


def place(q, p, second, counts):
    (o_a, o_b), (v_a, v_b), (start_even, start_odd) = counts
    o = jnp.where(second, o_b, o_a)
    v = jnp.where(second, v_b, v_a)
    start = jnp.where(second, jnp.where((q & 1) == 0, start_even, start_odd), 0)
    return jnp.where((p < o) & (q < v), start + (q >> 1) * o + p, -1)


def one_hot(left, right):
    return jnp.where(left == right, 1.0, 0.0).astype(BF16)


def dot(a, b):
    return jnp.dot(a, b, preferred_element_type=F32)


def prep_kernel(size, occ, virt, win, t2_ref, even_ref, odd_ref, x_ref):
    counts = pair_scalars(occ, virt, win, pl.program_id(0))
    row = iota((256, 1), 0)
    source = (((row >> 6) & 1) << 7) | (((row >> 2) & 15) << 3) | ((row & 3) << 1) | (row >> 7)
    by_parity = one_hot(iota((256, 256), 1), source)
    targets = []
    for half in range(2):
        for group in range(4):
            parts = [
                t2_ref[:, half, :, 4 * group + i].astype(F32).reshape(256, VIR_CAP) for i in range(4)
            ]
            x = jnp.concatenate(parts, axis=1).astype(BF16)
            at = (4 * half + group) * 256
            x_ref[:, at : at + 256] = dot(by_parity, x).astype(BF16)
            r = iota((256, 1), 0)
            p, q = 4 * group + (r >> 6), r & 63
            spot = place(q, p, half == 1, counts)
            targets.append(jnp.where(spot >= 0, spot + (q & 1) * size, -1))
    @pl.loop(0, 2)
    def _(core):
        for tile in range(-(-size // 256)):
            col = min(256 * tile, size - 256)
            lane = iota((256, 256), 1) + (col + core * size)
            acc = jnp.zeros((256, 256), F32)
            for chunk in range(8):
                acc += dot(x_ref[:, chunk * 256 : chunk * 256 + 256], one_hot(targets[chunk], lane))
            acc = acc.astype(BF16)
            even_ref[core, :, col : col + 256] = acc[:128]
            odd_ref[core, :, col : col + 256] = acc[128:]


def prep(size, scalars, t2):
    shape = jax.ShapeDtypeStruct((NIRREP, 128, size), BF16)
    block = pl.BlockSpec((2, 128, size), lambda k, *_: (k, 0, 0))
    return pl.pallas_call(
        functools.partial(prep_kernel, size),
        out_shape=(shape, shape),
        grid_spec=pltpu.PrefetchScalarGridSpec(
            num_scalar_prefetch=3,
            grid=(NIRREP // 2,),
            in_specs=[
                pl.BlockSpec((2, 2, OCC_CAP, OCC_CAP, 8, VIR_CAP), lambda k, *_: (0, k, 0, 0, 0, 0))
            ],
            out_specs=[block, block],
            scratch_shapes=[pltpu.VMEM((256, 2048), BF16)],
        ),
        compiler_params=params(),
        cost_estimate=cost(2 * 4 * 256 * 2048 * 2 * size, 12 * 2**20),
        name="prep_amplitudes",
    )(*scalars, t2)


def fill_rows(rows, spot, sel_ref):
    @pl.loop(0, rows // 128)
    def _(n):
        first = pl.multiple_of(n * 128, 128)
        sel_ref[pl.ds(first, 128), :] = one_hot(iota((128, BLOCK), 0) + first, spot)


def rows_kernel(rows, parity, count, occ, virt, win, at, x_ref, *refs):
    out_ref, sel_ref = refs[count], refs[-1]
    counts = pair_scalars(occ, virt, win, at[0])
    i = iota((1, BLOCK), 1)
    q = 8 * (i >> 7) + 2 * (i & 3) + parity
    spot = place(q, (i >> 2) & 15, ((i >> 6) & 1) == 1, counts)
    fill_rows(rows, spot, sel_ref)
    cols = out_ref.shape[1]

    @pl.loop(0, -(-cols // 256))
    def _(n):
        lanes = pl.ds(pl.multiple_of(jnp.minimum(n * 256, cols - 256), 128), 256)
        x = x_ref[:, :, lanes].reshape(BLOCK, 256)

        @pl.loop(0, 2)
        def _(half):
            at_rows = pl.ds(pl.multiple_of(half * (rows // 2), 64), rows // 2)
            out_ref[at_rows, lanes] = dot(sel_ref[at_rows, :], x).astype(BF16)


def compact_rows(rows, cols, parity, scalars, at, x, passed=(), awaited=()):
    whole = pl.BlockSpec(memory_space=pl.ANY)
    return pl.pallas_call(
        functools.partial(rows_kernel, rows, parity, len(passed) + len(awaited)),
        out_shape=[jax.ShapeDtypeStruct((rows, cols), BF16)]
        + [jax.ShapeDtypeStruct(y.shape, y.dtype) for y in passed],
        grid_spec=pltpu.PrefetchScalarGridSpec(
            num_scalar_prefetch=4,
            grid=(1,),
            in_specs=[pl.BlockSpec((NIRREP, 128, cols), lambda n, *_: (0, 0, 0))]
            + [whole] * (len(passed) + len(awaited)),
            out_specs=[pl.BlockSpec((rows, cols), lambda n, *_: (0, 0))] + [whole] * len(passed),
            scratch_shapes=[pltpu.VMEM((rows, BLOCK), BF16)],
        ),
        input_output_aliases={5 + i: 1 + i for i in range(len(passed))},
        compiler_params=params(),
        cost_estimate=cost(4 * rows * BLOCK * cols, 4 * rows * BLOCK),
        name="compact_rows",
    )(*scalars, at, x, *passed, *awaited)


def ints_kernel(rows, cols, occ, virt, win, at, mine_ref, other_ref, awaited, out_ref, sel_ref, cols_ref):
    plane, dev = at[0], at[1]
    parity = dev & 1

    @pl.when(pl.program_id(0) == 0)
    def _():
        counts = pair_scalars(occ, virt, win, plane)
        i = iota((1, BLOCK), 1)
        q = 2 * ((i >> 4) & 31) + parity
        spot = place(q, i & 15, (i >> 9) == 1, counts)
        fill_rows(rows, spot, sel_ref)

    counts = pair_scalars(occ, virt, win, dev >> 1)
    i = iota((BLOCK, 1), 0)
    q, p = i >> 4, i & 15
    lane = iota((BLOCK, 256), 1) + pl.program_id(0) * 256
    picks = []
    for second in (parity == 1, parity == 0):
        spot = place(q, p, second, counts)
        picks.append(one_hot(jnp.where(spot >= 0, spot + (q & 1) * cols, -1), lane))

    @pl.loop(0, 2)
    def _(half):
        at_rows = pl.ds(pl.multiple_of(half * (BLOCK // 2), BLOCK // 2), BLOCK // 2)
        acc = dot(mine_ref[half].reshape(BLOCK // 2, BLOCK), picks[0])
        acc += dot(other_ref[at_rows, :], picks[1])
        cols_ref[at_rows, :] = acc.astype(BF16)

    out_ref[...] = dot(sel_ref[...], cols_ref[...]).astype(BF16)


def compact_ints(rows, cols, scalars, at, mine, other, awaited):
    mine_spec = pl.BlockSpec(
        (2, VIR_CAP // 2, 1, OCC_CAP, BLOCK), lambda n, o, v, w, a: (0, 0, a[1] & 1, 0, 0)
    )
    whole = pl.BlockSpec((BLOCK, BLOCK), lambda n, *_: (0, 0))
    return pl.pallas_call(
        functools.partial(ints_kernel, rows, cols),
        out_shape=jax.ShapeDtypeStruct((rows, 2 * cols), BF16),
        grid_spec=pltpu.PrefetchScalarGridSpec(
            num_scalar_prefetch=4,
            grid=(2 * cols // 256,),
            in_specs=[mine_spec, whole, pl.BlockSpec(memory_space=pl.ANY)],
            out_specs=pl.BlockSpec((rows, 256), lambda n, *_: (0, n)),
            scratch_shapes=[pltpu.VMEM((rows, BLOCK), BF16), pltpu.VMEM((BLOCK, 256), BF16)],
        ),
        compiler_params=params(),
        cost_estimate=cost(16 * BLOCK * BLOCK * cols, 4 * BLOCK * BLOCK + 4 * rows * cols),
        name="compact_ints",
    )(*scalars, at, mine, other, awaited)


def widen_tile(rows, cols, tile, occ, virt, win, dev, own_refs, sib_refs, wide_ref):
    parity = dev & 1
    counts = pair_scalars(occ, virt, win, dev >> 1)
    (o_a, o_b), _, (start_even, start_odd) = counts
    second = parity == 1
    o = jnp.where(second, o_b, o_a)
    i = iota((1, 256), 1) + tile * 256
    q = i >> 4
    spot = place(q, i & 15, second, counts)
    r = iota((256, 256), 0)
    picks = []
    for s in (parity, 1 - parity):
        start = jnp.where(second, jnp.where(s == 0, start_even, start_odd), 0) + 8 * tile * o
        start = jnp.minimum((start >> 7) << 7, cols - 256)
        window = pl.ds(pl.multiple_of(start, 128), 256)
        picks.append((window, one_hot(r + start, jnp.where((q & 1) == s, spot, -1))))
    for piece in range(2):
        x = dot(own_refs[piece][:, picks[0][0]], picks[0][1])
        x += dot(sib_refs[piece][:, picks[1][0]], picks[1][1])
        wide_ref[piece * cols : piece * cols + rows, :] = x.astype(BF16)
        if rows < cols:
            wide_ref[piece * cols + rows : (piece + 1) * cols, :] = jnp.zeros((cols - rows, 256), BF16)


def widen_kernel(rows, cols, slots, occ, virt, win, at, *refs):
    wide_ref = refs[-1]
    for slot in range(slots):

        @pl.when(pl.program_id(0) == slot)
        def _():
            t0, t1, s0, s1 = refs[4 * slot : 4 * slot + 4]
            tile = pl.program_id(1)
            widen_tile(rows, cols, tile, occ, virt, win, at[1], (t0, t1), (s0, s1), wide_ref.at[0])


def widen(rows, cols, scalars, at, blocks):
    slots = len(blocks) // 4
    square = pl.BlockSpec((rows, cols), lambda t, n, *_: (0, 0), pipeline_mode=pl.Buffered(1))
    return pl.pallas_call(
        functools.partial(widen_kernel, rows, cols, slots),
        out_shape=jax.ShapeDtypeStruct((slots, 2 * cols, BLOCK), BF16),
        grid_spec=pltpu.PrefetchScalarGridSpec(
            num_scalar_prefetch=4,
            grid=(slots, BLOCK // 256),
            in_specs=[square] * len(blocks),
            out_specs=pl.BlockSpec((1, 2 * cols, 256), lambda t, n, *_: (t, 0, n)),
        ),
        compiler_params=params(),
        cost_estimate=cost(slots * 8 * rows * 512 * BLOCK, slots * (8 * rows * cols + 4 * cols * BLOCK)),
        name="widen",
    )(*scalars, at, *blocks)


def product_kernel(inner, ints_ref, wide_ref, acc_ref):
    at = pl.ds(pl.multiple_of(pl.program_id(1) * WIDE, WIDE), WIDE)

    @pl.when(pl.program_id(0) == 0)
    def _():
        acc_ref[:, :, at] = jnp.zeros((2, acc_ref.shape[1], WIDE), F32)

    @pl.loop(0, 2)
    def _(half):
        acc_ref[half, :, at] += dot(ints_ref[0, half], wide_ref[0])


def product(rows, cols, inner, ints, wide):
    slots = wide.shape[0]
    return pl.pallas_call(
        product_kernel,
        out_shape=jax.ShapeDtypeStruct((2, rows, BLOCK), F32),
        grid_spec=pltpu.PrefetchScalarGridSpec(
            num_scalar_prefetch=1,
            grid=(slots, BLOCK // WIDE),
            in_specs=[
                pl.BlockSpec((1, 2, rows, 2 * cols), lambda t, n, k: (k[t], 0, 0, 0)),
                pl.BlockSpec((1, 2 * cols, WIDE), lambda t, n, k: (t, 0, n)),
            ],
            out_specs=pl.BlockSpec((2, rows, BLOCK), lambda t, n, k: (0, 0, 0)),
        ),
        compiler_params=params(),
        cost_estimate=cost(16 * slots * rows * cols * BLOCK, slots * 4 * cols * (rows + BLOCK)),
        name="product",
    )(inner, ints, wide)


def last_kernel(
    rows, cols, occ, virt, win, at, inner,
    ints_ref, t0, t1, s0, s1, old_ref, evirt, eocc_ref, ecol_ref, out_ref, wide_ref, sum_ref,
):
    plane, dev = at[0], at[1]

    @pl.loop(0, WIDE // 256)
    def _(part):
        tile = pl.program_id(0) * (WIDE // 256) + part
        into = wide_ref.at[:, pl.ds(pl.multiple_of(part * 256, 256), 256)]
        widen_tile(rows, cols, tile, occ, virt, win, dev, (t0, t1), (s0, s1), into)

    @pl.loop(0, 2)
    def _(half):
        sum_ref[half, :rows, :] = old_ref[half] + dot(ints_ref[0, half], wide_ref[...])

    i = iota((1, WIDE), 1) + pl.program_id(0) * WIDE
    col_live = ((i & 15) < occ[dev]) & ((i >> 4) < virt[dev ^ win[0]])
    col_energy = ecol_ref[...]
    _, _, starts = pair_scalars(occ, virt, win, plane)
    p = iota((OCC_CAP, 1), 0)
    irreps = [2 * plane, 2 * plane + 1]
    occs = [occ[irrep] for irrep in irreps]
    partners = [irrep ^ win[0] for irrep in irreps]
    virts = [virt[partner] for partner in partners]
    live = [(p < o) & col_live for o in occs]

    @pl.loop(0, VIR_CAP // 4)
    def _(group):
        for h in range(2):
            for i in range(4):
                half_q, s = 2 * group + i // 2, i % 2
                q = 2 * half_q + s
                start = half_q * occs[h]
                if h == 1:
                    start = start + starts[s]
                start = jnp.minimum(start, rows)
                block = sum_ref[s, pl.ds(pl.multiple_of((start >> 3) << 3, 8), OCC_CAP + 8), :]
                block = pltpu.roll(block, OCC_CAP + 8 - (start & 7), 0)[:OCC_CAP]
                denom = (eocc_ref[h] - evirt[partners[h], q]) + col_energy
                value = jnp.where(live[h] & (q < virts[h]), block / denom, 0.0)
                at_row = pl.multiple_of((h * VIR_CAP + q) * OCC_CAP, OCC_CAP)
                out_ref[pl.ds(at_row, OCC_CAP), :] = value


def last(rows, cols, scalars, at, inner, ints, own, sib, acc, energies):
    square = pl.BlockSpec((rows, cols), lambda n, *_: (0, 0))
    return pl.pallas_call(
        functools.partial(last_kernel, rows, cols),
        out_shape=jax.ShapeDtypeStruct((2 * BLOCK, BLOCK), F32),
        grid_spec=pltpu.PrefetchScalarGridSpec(
            num_scalar_prefetch=5,
            grid=(BLOCK // WIDE,),
            in_specs=[
                pl.BlockSpec((1, 2, rows, 2 * cols), lambda n, o, v, w, a, k: (k[0], 0, 0, 0)),
                square, square, square, square,
                pl.BlockSpec((2, rows, WIDE), lambda n, *_: (0, 0, n)),
                pl.BlockSpec(memory_space=pltpu.SMEM),
                pl.BlockSpec((2, OCC_CAP, 1), lambda n, *_: (0, 0, 0)),
                pl.BlockSpec((1, WIDE), lambda n, *_: (0, n)),
            ],
            out_specs=pl.BlockSpec((2 * BLOCK, WIDE), lambda n, *_: (0, n)),
            scratch_shapes=[
                pltpu.VMEM((2 * cols, WIDE), BF16),
                pltpu.VMEM((2, rows + OCC_CAP + 8, WIDE), F32),
            ],
        ),
        compiler_params=params(),
        cost_estimate=cost(16 * rows * cols * BLOCK, 8 * rows * cols + 16 * rows * BLOCK),
        name="last_product",
    )(*scalars, at, inner, ints, *own, *sib, acc, *energies)


def after_kernel(*refs):
    pass


def after(kept, awaited):
    whole = pl.BlockSpec(memory_space=pl.ANY)
    return pl.pallas_call(
        after_kernel,
        out_shape=[jax.ShapeDtypeStruct(x.shape, x.dtype) for x in kept],
        in_specs=[whole] * (len(kept) + len(awaited)),
        out_specs=[whole] * len(kept),
        input_output_aliases={i: i for i in range(len(kept))},
        name="after",
    )(*kept, *awaited)


def ring_order(n):
    return list(range(0, 1)) + list(range(1, n, 2)) + [i for i in range(n - 1, 0, -1) if i % 2 == 0]


def branch(rows, nrow, ncol, t2, ints, occ, virt, win, eps_virt, occ_rows, col_energy, at, sources):
    cols = -(-rows // 128) * 128
    scalars = (occ, virt, win)
    order = ring_order(nrow)
    ring = [(order[i], order[(i + 1) % nrow]) for i in range(nrow)]
    swap = [(c, c ^ 1) for c in range(ncol)]

    def to_sibling(x):
        return lax.ppermute(x, "col", swap)

    def around(x):
        return lax.ppermute(x, "row", ring)

    def exchange(x):
        return lax.all_to_all(x, "col", split_axis=0, concat_axis=0, tiled=True)

    even, odd = prep(cols, scalars, t2)
    even, odd = compact_rows(rows, cols, 0, scalars, at, exchange(even), passed=(odd,))
    mine = ints.reshape(2, VIR_CAP // 2, 2, OCC_CAP, BLOCK)
    other = lax.dynamic_index_in_dim(mine, 1 - (at[1] & 1), 2, keepdims=False).reshape(BLOCK, BLOCK)
    even_next = around(even)
    small = compact_ints(rows, cols, scalars, at, mine, to_sibling(other), even)
    odd, small = compact_rows(rows, cols, 1, scalars, at, exchange(odd), passed=(small,))
    odd, small = after([odd, small], [even_next])
    panel = lax.all_gather(small, "col", axis=0, tiled=False).reshape(ncol // 2, 2, rows, 2 * cols)

    held = [even, odd]
    blocks = []
    for step in range(nrow - 1):
        later = [even_next if step == 0 else around(held[0]), around(held[1])]
        blocks += held + [to_sibling(x) for x in held]
        held = later
    wide = widen(rows, cols, scalars, at, blocks)
    acc = product(rows, cols, sources[: nrow - 1], panel, wide)
    own = after(held, [acc])
    sib = [to_sibling(x) for x in own]
    energies = (eps_virt, occ_rows, col_energy)
    return last(rows, cols, scalars, at, sources[nrow - 1 :], panel, own, sib, acc, energies)


def choose_kernel(occ, virt, win, index_ref):
    index = jnp.int32(len(SIZES) - 1)
    for pair in range(NIRREP // 2):
        (o_a, o_b), (v_a, v_b), _ = pair_scalars(occ, virt, win, pair)
        most = o_a * ((v_a + 1) >> 1) + o_b * ((v_b + 1) >> 1)
        fits = sum((most <= size).astype(I32) for size in SIZES[1:])
        index = jnp.minimum(index, fits)
    index_ref[0] = index


def choose(occ, virt, win):
    smem = pl.BlockSpec(memory_space=pltpu.SMEM)
    return pl.pallas_call(
        choose_kernel,
        out_shape=jax.ShapeDtypeStruct((1,), I32),
        in_specs=[smem] * 3,
        out_specs=smem,
        name="choose",
    )(occ, virt, win)[0]


def live_device(nrow, ncol, t2, ints, eps_occ, eps_virt, occ, virt, win):
    row, col = lax.axis_index("row"), lax.axis_index("col")
    index = choose(occ, virt, win)
    occ_rows = lax.dynamic_slice(eps_occ, (2 * row, 0), (2, OCC_CAP)).reshape(2, OCC_CAP, 1)
    col_occ = lax.dynamic_slice(eps_occ, (col, 0), (1, OCC_CAP))
    col_virt = lax.dynamic_slice(eps_virt, (col ^ win[0], 0), (1, VIR_CAP))
    col_energy = (col_occ[:, None, :] - col_virt[:, :, None]).reshape(1, BLOCK)
    at = jnp.stack([row, col]).astype(I32)
    order = ring_order(nrow)
    table = [[order[(order.index(z) - t) % nrow] for t in range(nrow)] for z in range(nrow)]
    sources = lax.dynamic_slice(jnp.array(table, I32), (row, 0), (1, nrow)).reshape(nrow)
    operands = (t2, ints, occ, virt, win, eps_virt, occ_rows, col_energy, at, sources)
    return lax.switch(index, [functools.partial(branch, size, nrow, ncol) for size in SIZES], *operands)


def ph_vectors(eps_occ, eps_virt, occ_count, virt_count, window_irrep):
    irreps = jnp.arange(NIRREP, dtype=I32)
    partner = jnp.bitwise_xor(irreps, window_irrep[0])
    onehot = partner[:, None] == irreps[None, :]
    virt_rows = jnp.dot(onehot.astype(F32), eps_virt, precision=lax.Precision.HIGHEST)
    virt_live = jnp.sum(jnp.where(onehot, virt_count[None, :], 0), axis=1)
    energy = eps_occ[:, None, :] - virt_rows[:, :, None]
    slots_occ = jnp.arange(OCC_CAP, dtype=I32)
    slots_virt = jnp.arange(VIR_CAP, dtype=I32)
    live = (slots_occ[None, None, :] < occ_count[:, None, None]) & (
        slots_virt[None, :, None] < virt_live[:, None, None]
    )
    return (energy, live)


def any_device(t2_pairs, cycle_ints, eps_occ, eps_virt, occ_count, virt_count, window_irrep):
    irrep_local = t2_pairs.shape[0]
    virt_local = t2_pairs.shape[4]
    total = NIRREP * VIR_CAP * OCC_CAP
    energy, live = ph_vectors(eps_occ, eps_virt, occ_count, virt_count, window_irrep)
    row_index = lax.axis_index("row")
    col_index = lax.axis_index("col")
    zero_index = jnp.int32(0)
    source_live = lax.dynamic_slice(
        live,
        (row_index * irrep_local, col_index * virt_local, zero_index),
        (irrep_local, virt_local, OCC_CAP),
    )
    full_live = live.reshape(-1)
    ordered = jnp.transpose(t2_pairs, (0, 4, 2, 1, 5, 3)).reshape(
        irrep_local, virt_local, OCC_CAP, total
    )
    keep = source_live[:, :, :, None] & full_live[None, None, None, :]
    ordered = jnp.where(keep, ordered, jnp.zeros_like(ordered))
    moved = lax.all_to_all(ordered, "col", split_axis=3, concat_axis=1, tiled=True)
    amp_local = moved.reshape(irrep_local * VIR_CAP * OCC_CAP, moved.shape[3])
    amp_panel = lax.all_gather(amp_local, "row", axis=0, tiled=True)
    ints_panel = lax.all_gather(cycle_ints, "col", axis=1, tiled=True)
    cycle = jnp.dot(ints_panel, amp_panel, preferred_element_type=F32)
    rows_here, cols_here = cycle.shape
    flat_energy = energy.reshape(-1)
    row_start, col_start = row_index * rows_here, col_index * cols_here
    row_energy = lax.dynamic_slice_in_dim(flat_energy, row_start, rows_here, 0)
    col_energy = lax.dynamic_slice_in_dim(flat_energy, col_start, cols_here, 0)
    row_live = lax.dynamic_slice_in_dim(full_live, row_start, rows_here, 0)
    col_live = lax.dynamic_slice_in_dim(full_live, col_start, cols_here, 0)
    denom = row_energy[:, None] + col_energy[None, :]
    return jnp.where(row_live[:, None] & col_live[None, :], cycle / denom, F32(0.0))


def solution(mesh):
    nrow, ncol = mesh.shape["row"], mesh.shape["col"]
    placed = (P("row", None, None, None, "col", None), P("row", "col"), P(), P(), P(), P(), P())
    body = any_device
    if 2 * nrow == NIRREP and ncol == NIRREP:
        body = functools.partial(live_device, nrow, ncol)
    return jax.shard_map(body, mesh=mesh, in_specs=placed, out_specs=P("row", "col"), check_vma=False)
```

```python
import functools

import jax
import jax.numpy as jnp
from jax import lax
from jax.experimental import pallas as pl
from jax.experimental.pallas import tpu as pltpu
from jax.sharding import PartitionSpec as P

NIRREP = 8
OCC_CAP = 16
VIR_CAP = 64
BLOCK = VIR_CAP * OCC_CAP
SIZES = (1024, 896, 768, 640)
WIDE = 512
F32 = jnp.float32
BF16 = jnp.bfloat16
I32 = jnp.int32
I16 = jnp.int16
VMEM_BYTES = 56 * 1024 * 1024


def iota(shape, dim):
    return lax.broadcasted_iota(I32, shape, dim)


def params():
    return pltpu.CompilerParams(vmem_limit_bytes=VMEM_BYTES)


def cost(flops, nbytes):
    return pl.CostEstimate(flops=flops, bytes_accessed=nbytes, transcendentals=0)


def pair_scalars(occ, virt, win, pair):
    first = 2 * pair
    o_a, o_b = occ[first], occ[first + 1]
    v_a, v_b = virt[first ^ win[0]], virt[(first + 1) ^ win[0]]
    return (o_a, o_b), (v_a, v_b), (o_a * ((v_a + 1) >> 1), o_a * (v_a >> 1))


def place(q, p, second, counts):
    (o_a, o_b), (v_a, v_b), (start_even, start_odd) = counts
    o = jnp.where(second, o_b, o_a)
    v = jnp.where(second, v_b, v_a)
    start = jnp.where(second, jnp.where((q & 1) == 0, start_even, start_odd), 0)
    return jnp.where((p < o) & (q < v), start + (q >> 1) * o + p, -1)


def one_hot(left, right):
    return jnp.where(left.astype(I16) == right.astype(I16), BF16(1.0), BF16(0.0))


def dot(a, b):
    return jnp.dot(a, b, preferred_element_type=F32)


def prep_kernel(size, occ, virt, win, t2_ref, even_ref, odd_ref, x_ref):
    counts = pair_scalars(occ, virt, win, pl.program_id(0))
    row = iota((256, 1), 0)
    source = (((row >> 6) & 1) << 7) | (((row >> 2) & 15) << 3) | ((row & 3) << 1) | (row >> 7)
    by_parity = one_hot(iota((256, 256), 1), source)
    targets = []
    for half in range(2):
        for group in range(4):
            parts = [
                t2_ref[:, half, :, 4 * group + i].astype(F32).reshape(256, VIR_CAP) for i in range(4)
            ]
            x = jnp.concatenate(parts, axis=1).astype(BF16)
            at = (4 * half + group) * 256
            x_ref[:, at : at + 256] = dot(by_parity, x).astype(BF16)
            r = iota((256, 1), 0)
            p, q = 4 * group + (r >> 6), r & 63
            spot = place(q, p, half == 1, counts)
            targets.append(jnp.where(spot >= 0, spot + (q & 1) * size, -1))
    @pl.loop(0, 2)
    def _(core):
        for tile in range(-(-size // 256)):
            col = min(256 * tile, size - 256)
            lane = iota((256, 256), 1) + (col + core * size)
            acc = jnp.zeros((256, 256), F32)
            for chunk in range(4 if col >= BLOCK // 2 else 0, 8):
                acc += dot(x_ref[:, chunk * 256 : chunk * 256 + 256], one_hot(targets[chunk], lane))
            acc = acc.astype(BF16)
            even_ref[core, :, col : col + 256] = acc[:128]
            odd_ref[core, :, col : col + 256] = acc[128:]


def prep(size, scalars, t2):
    shape = jax.ShapeDtypeStruct((NIRREP, 128, size), BF16)
    block = pl.BlockSpec((2, 128, size), lambda k, *_: (k, 0, 0))
    return pl.pallas_call(
        functools.partial(prep_kernel, size),
        out_shape=(shape, shape),
        grid_spec=pltpu.PrefetchScalarGridSpec(
            num_scalar_prefetch=3,
            grid=(NIRREP // 2,),
            in_specs=[
                pl.BlockSpec((2, 2, OCC_CAP, OCC_CAP, 8, VIR_CAP), lambda k, *_: (0, k, 0, 0, 0, 0))
            ],
            out_specs=[block, block],
            scratch_shapes=[pltpu.VMEM((256, 2048), BF16)],
        ),
        compiler_params=params(),
        cost_estimate=cost(2 * 4 * 256 * 2048 * 2 * size, 12 * 2**20),
        name="prep_amplitudes",
    )(*scalars, t2)


def fill_rows(rows, spot, sel_ref):
    @pl.loop(0, rows // 128)
    def _(n):
        first = pl.multiple_of(n * 128, 128)
        sel_ref[pl.ds(first, 128), :] = one_hot(iota((128, BLOCK), 0) + first, spot)


def rows_kernel(rows, parity, count, occ, virt, win, at, x_ref, *refs):
    out_ref, sel_ref = refs[count], refs[-1]
    counts = pair_scalars(occ, virt, win, at[0])
    i = iota((1, BLOCK), 1)
    q = 8 * (i >> 7) + 2 * (i & 3) + parity
    spot = place(q, (i >> 2) & 15, ((i >> 6) & 1) == 1, counts)
    fill_rows(rows, spot, sel_ref)
    cols = out_ref.shape[1]

    @pl.loop(0, -(-cols // 256))
    def _(n):
        lanes = pl.ds(pl.multiple_of(jnp.minimum(n * 256, cols - 256), 128), 256)
        x = x_ref[:, :, lanes].reshape(BLOCK, 256)

        @pl.loop(0, 2)
        def _(half):
            at_rows = pl.ds(pl.multiple_of(half * (rows // 2), 64), rows // 2)
            out_ref[at_rows, lanes] = dot(sel_ref[at_rows, :], x).astype(BF16)


def compact_rows(rows, cols, parity, scalars, at, x, passed=(), awaited=()):
    whole = pl.BlockSpec(memory_space=pl.ANY)
    return pl.pallas_call(
        functools.partial(rows_kernel, rows, parity, len(passed) + len(awaited)),
        out_shape=[jax.ShapeDtypeStruct((rows, cols), BF16)]
        + [jax.ShapeDtypeStruct(y.shape, y.dtype) for y in passed],
        grid_spec=pltpu.PrefetchScalarGridSpec(
            num_scalar_prefetch=4,
            grid=(1,),
            in_specs=[pl.BlockSpec((NIRREP, 128, cols), lambda n, *_: (0, 0, 0))]
            + [whole] * (len(passed) + len(awaited)),
            out_specs=[pl.BlockSpec((rows, cols), lambda n, *_: (0, 0))] + [whole] * len(passed),
            scratch_shapes=[pltpu.VMEM((rows, BLOCK), BF16)],
        ),
        input_output_aliases={5 + i: 1 + i for i in range(len(passed))},
        compiler_params=params(),
        cost_estimate=cost(4 * rows * BLOCK * cols, 4 * rows * BLOCK),
        name="compact_rows",
    )(*scalars, at, x, *passed, *awaited)


def ints_kernel(rows, cols, occ, virt, win, at, mine_ref, other_ref, awaited, out_ref, sel_ref, cols_ref):
    plane, dev = at[0], at[1]
    parity = dev & 1

    @pl.when(pl.program_id(0) == 0)
    def _():
        counts = pair_scalars(occ, virt, win, plane)
        i = iota((1, BLOCK), 1)
        q = 2 * ((i >> 4) & 31) + parity
        spot = place(q, i & 15, (i >> 9) == 1, counts)
        fill_rows(rows, spot, sel_ref)

    counts = pair_scalars(occ, virt, win, dev >> 1)
    i = iota((BLOCK, 1), 0)
    q, p = i >> 4, i & 15
    lane = iota((BLOCK, 256), 1) + pl.program_id(0) * 256
    picks = []
    for second in (parity == 1, parity == 0):
        spot = place(q, p, second, counts)
        picks.append(one_hot(jnp.where(spot >= 0, spot + (q & 1) * cols, -1), lane))

    @pl.loop(0, 2)
    def _(half):
        at_rows = pl.ds(pl.multiple_of(half * (BLOCK // 2), BLOCK // 2), BLOCK // 2)
        acc = dot(mine_ref[half].reshape(BLOCK // 2, BLOCK), picks[0])
        acc += dot(other_ref[at_rows, :], picks[1])
        cols_ref[at_rows, :] = acc.astype(BF16)

    out_ref[...] = dot(sel_ref[...], cols_ref[...]).astype(BF16)


def compact_ints(rows, cols, scalars, at, mine, other, awaited):
    mine_spec = pl.BlockSpec(
        (2, VIR_CAP // 2, 1, OCC_CAP, BLOCK), lambda n, o, v, w, a: (0, 0, a[1] & 1, 0, 0)
    )
    whole = pl.BlockSpec((BLOCK, BLOCK), lambda n, *_: (0, 0))
    return pl.pallas_call(
        functools.partial(ints_kernel, rows, cols),
        out_shape=jax.ShapeDtypeStruct((rows, 2 * cols), BF16),
        grid_spec=pltpu.PrefetchScalarGridSpec(
            num_scalar_prefetch=4,
            grid=(2 * cols // 256,),
            in_specs=[mine_spec, whole, pl.BlockSpec(memory_space=pl.ANY)],
            out_specs=pl.BlockSpec((rows, 256), lambda n, *_: (0, n)),
            scratch_shapes=[pltpu.VMEM((rows, BLOCK), BF16), pltpu.VMEM((BLOCK, 256), BF16)],
        ),
        compiler_params=params(),
        cost_estimate=cost(16 * BLOCK * BLOCK * cols, 4 * BLOCK * BLOCK + 4 * rows * cols),
        name="compact_ints",
    )(*scalars, at, mine, other, awaited)


def widen_tile(rows, cols, tile, occ, virt, win, dev, own_refs, sib_refs, wide_ref):
    parity = dev & 1
    counts = pair_scalars(occ, virt, win, dev >> 1)
    (o_a, o_b), _, (start_even, start_odd) = counts
    second = parity == 1
    o = jnp.where(second, o_b, o_a)
    i = iota((1, 256), 1) + tile * 256
    q = i >> 4
    spot = place(q, i & 15, second, counts)
    r = iota((256, 256), 0)
    picks = []
    for s in (parity, 1 - parity):
        start = jnp.where(second, jnp.where(s == 0, start_even, start_odd), 0) + 8 * tile * o
        start = jnp.minimum((start >> 7) << 7, cols - 256)
        window = pl.ds(pl.multiple_of(start, 128), 256)
        picks.append((window, one_hot(r + start, jnp.where((q & 1) == s, spot, -1))))
    for piece in range(2):
        x = dot(own_refs[piece][:, picks[0][0]], picks[0][1])
        x += dot(sib_refs[piece][:, picks[1][0]], picks[1][1])
        wide_ref[piece * cols : piece * cols + rows, :] = x.astype(BF16)
        if rows < cols:
            wide_ref[piece * cols + rows : (piece + 1) * cols, :] = jnp.zeros((cols - rows, 256), BF16)


def widen_kernel(rows, cols, slots, occ, virt, win, at, *refs):
    wide_ref = refs[-1]
    for slot in range(slots):

        @pl.when(pl.program_id(0) == slot)
        def _():
            t0, t1, s0, s1 = refs[4 * slot : 4 * slot + 4]
            tile = pl.program_id(1)
            widen_tile(rows, cols, tile, occ, virt, win, at[1], (t0, t1), (s0, s1), wide_ref.at[0])


def widen(rows, cols, scalars, at, blocks):
    slots = len(blocks) // 4
    square = pl.BlockSpec((rows, cols), lambda t, n, *_: (0, 0), pipeline_mode=pl.Buffered(1))
    return pl.pallas_call(
        functools.partial(widen_kernel, rows, cols, slots),
        out_shape=jax.ShapeDtypeStruct((slots, 2 * cols, BLOCK), BF16),
        grid_spec=pltpu.PrefetchScalarGridSpec(
            num_scalar_prefetch=4,
            grid=(slots, BLOCK // 256),
            in_specs=[square] * len(blocks),
            out_specs=pl.BlockSpec((1, 2 * cols, 256), lambda t, n, *_: (t, 0, n)),
        ),
        compiler_params=params(),
        cost_estimate=cost(slots * 8 * rows * 512 * BLOCK, slots * (8 * rows * cols + 4 * cols * BLOCK)),
        name="widen",
    )(*scalars, at, *blocks)


def product_kernel(inner, ints_ref, wide_ref, acc_ref):
    at = pl.ds(pl.multiple_of(pl.program_id(1) * WIDE, WIDE), WIDE)

    @pl.when(pl.program_id(0) == 0)
    def _():
        acc_ref[:, :, at] = jnp.zeros((2, acc_ref.shape[1], WIDE), F32)

    @pl.loop(0, 2)
    def _(half):
        acc_ref[half, :, at] += dot(ints_ref[0, half], wide_ref[0])


def product(rows, cols, inner, ints, wide):
    slots = wide.shape[0]
    return pl.pallas_call(
        product_kernel,
        out_shape=jax.ShapeDtypeStruct((2, rows, BLOCK), F32),
        grid_spec=pltpu.PrefetchScalarGridSpec(
            num_scalar_prefetch=1,
            grid=(slots, BLOCK // WIDE),
            in_specs=[
                pl.BlockSpec((1, 2, rows, 2 * cols), lambda t, n, k: (k[t], 0, 0, 0)),
                pl.BlockSpec((1, 2 * cols, WIDE), lambda t, n, k: (t, 0, n)),
            ],
            out_specs=pl.BlockSpec((2, rows, BLOCK), lambda t, n, k: (0, 0, 0)),
        ),
        compiler_params=params(),
        cost_estimate=cost(16 * slots * rows * cols * BLOCK, slots * 4 * cols * (rows + BLOCK)),
        name="product",
    )(inner, ints, wide)


def last_kernel(
    rows, cols, occ, virt, win, at, inner,
    ints_ref, t0, t1, s0, s1, old_ref, evirt, eocc_ref, ecol_ref, out_ref, wide_ref, sum_ref,
):
    plane, dev = at[0], at[1]

    @pl.loop(0, WIDE // 256)
    def _(part):
        tile = pl.program_id(0) * (WIDE // 256) + part
        into = wide_ref.at[:, pl.ds(pl.multiple_of(part * 256, 256), 256)]
        widen_tile(rows, cols, tile, occ, virt, win, dev, (t0, t1), (s0, s1), into)

    @pl.loop(0, 2)
    def _(half):
        sum_ref[half, :rows, :] = old_ref[half] + dot(ints_ref[0, half], wide_ref[...])

    i = iota((1, WIDE), 1) + pl.program_id(0) * WIDE
    col_live = ((i & 15) < occ[dev]) & ((i >> 4) < virt[dev ^ win[0]])
    col_energy = ecol_ref[...]
    _, _, starts = pair_scalars(occ, virt, win, plane)
    p = iota((OCC_CAP, 1), 0)
    irreps = [2 * plane, 2 * plane + 1]
    occs = [occ[irrep] for irrep in irreps]
    partners = [irrep ^ win[0] for irrep in irreps]
    virts = [virt[partner] for partner in partners]
    live = [(p < o) & col_live for o in occs]

    @pl.loop(0, VIR_CAP // 4)
    def _(group):
        for h in range(2):
            for i in range(4):
                half_q, s = 2 * group + i // 2, i % 2
                q = 2 * half_q + s
                start = half_q * occs[h]
                if h == 1:
                    start = start + starts[s]
                start = jnp.minimum(start, rows)
                block = sum_ref[s, pl.ds(pl.multiple_of((start >> 3) << 3, 8), OCC_CAP + 8), :]
                block = pltpu.roll(block, OCC_CAP + 8 - (start & 7), 0)[:OCC_CAP]
                denom = (eocc_ref[h] - evirt[partners[h], q]) + col_energy
                value = jnp.where(live[h] & (q < virts[h]), block / denom, 0.0)
                at_row = pl.multiple_of((h * VIR_CAP + q) * OCC_CAP, OCC_CAP)
                out_ref[pl.ds(at_row, OCC_CAP), :] = value


def last(rows, cols, scalars, at, inner, ints, own, sib, acc, energies):
    square = pl.BlockSpec((rows, cols), lambda n, *_: (0, 0))
    return pl.pallas_call(
        functools.partial(last_kernel, rows, cols),
        out_shape=jax.ShapeDtypeStruct((2 * BLOCK, BLOCK), F32),
        grid_spec=pltpu.PrefetchScalarGridSpec(
            num_scalar_prefetch=5,
            grid=(BLOCK // WIDE,),
            in_specs=[
                pl.BlockSpec((1, 2, rows, 2 * cols), lambda n, o, v, w, a, k: (k[0], 0, 0, 0)),
                square, square, square, square,
                pl.BlockSpec((2, rows, WIDE), lambda n, *_: (0, 0, n)),
                pl.BlockSpec(memory_space=pltpu.SMEM),
                pl.BlockSpec((2, OCC_CAP, 1), lambda n, *_: (0, 0, 0)),
                pl.BlockSpec((1, WIDE), lambda n, *_: (0, n)),
            ],
            out_specs=pl.BlockSpec((2 * BLOCK, WIDE), lambda n, *_: (0, n)),
            scratch_shapes=[
                pltpu.VMEM((2 * cols, WIDE), BF16),
                pltpu.VMEM((2, rows + OCC_CAP + 8, WIDE), F32),
            ],
        ),
        compiler_params=params(),
        cost_estimate=cost(16 * rows * cols * BLOCK, 8 * rows * cols + 16 * rows * BLOCK),
        name="last_product",
    )(*scalars, at, inner, ints, *own, *sib, acc, *energies)


def after_kernel(*refs):
    pass


def after(kept, awaited):
    whole = pl.BlockSpec(memory_space=pl.ANY)
    return pl.pallas_call(
        after_kernel,
        out_shape=[jax.ShapeDtypeStruct(x.shape, x.dtype) for x in kept],
        in_specs=[whole] * (len(kept) + len(awaited)),
        out_specs=[whole] * len(kept),
        input_output_aliases={i: i for i in range(len(kept))},
        name="after",
    )(*kept, *awaited)


def ring_order(n):
    return list(range(0, 1)) + list(range(1, n, 2)) + [i for i in range(n - 1, 0, -1) if i % 2 == 0]


def branch(rows, nrow, ncol, t2, ints, occ, virt, win, eps_virt, occ_rows, col_energy, at, sources):
    cols = -(-rows // 128) * 128
    scalars = (occ, virt, win)
    order = ring_order(nrow)
    ring = [(order[i], order[(i + 1) % nrow]) for i in range(nrow)]
    swap = [(c, c ^ 1) for c in range(ncol)]

    def to_sibling(x):
        return lax.ppermute(x, "col", swap)

    def around(x):
        return lax.ppermute(x, "row", ring)

    def exchange(x):
        return lax.all_to_all(x, "col", split_axis=0, concat_axis=0, tiled=True)

    even, odd = prep(cols, scalars, t2)
    even, odd = compact_rows(rows, cols, 0, scalars, at, exchange(even), passed=(odd,))
    mine = ints.reshape(2, VIR_CAP // 2, 2, OCC_CAP, BLOCK)
    other = lax.dynamic_index_in_dim(mine, 1 - (at[1] & 1), 2, keepdims=False).reshape(BLOCK, BLOCK)
    even_next = around(even)
    small = compact_ints(rows, cols, scalars, at, mine, to_sibling(other), even)
    odd, small = compact_rows(rows, cols, 1, scalars, at, exchange(odd), passed=(small,))
    odd, small = after([odd, small], [even_next])
    panel = lax.all_gather(small, "col", axis=0, tiled=False).reshape(ncol // 2, 2, rows, 2 * cols)

    held = [even, odd]
    blocks = []
    for step in range(nrow - 1):
        later = [even_next if step == 0 else around(held[0]), around(held[1])]
        blocks += held + [to_sibling(x) for x in held]
        held = later
    wide = widen(rows, cols, scalars, at, blocks)
    acc = product(rows, cols, sources[: nrow - 1], panel, wide)
    own = after(held, [acc])
    sib = [to_sibling(x) for x in own]
    energies = (eps_virt, occ_rows, col_energy)
    return last(rows, cols, scalars, at, sources[nrow - 1 :], panel, own, sib, acc, energies)


def choose_kernel(occ, virt, win, index_ref):
    index = jnp.int32(len(SIZES) - 1)
    for pair in range(NIRREP // 2):
        (o_a, o_b), (v_a, v_b), _ = pair_scalars(occ, virt, win, pair)
        most = o_a * ((v_a + 1) >> 1) + o_b * ((v_b + 1) >> 1)
        fits = sum((most <= size).astype(I32) for size in SIZES[1:])
        index = jnp.minimum(index, fits)
    index_ref[0] = index


def choose(occ, virt, win):
    smem = pl.BlockSpec(memory_space=pltpu.SMEM)
    return pl.pallas_call(
        choose_kernel,
        out_shape=jax.ShapeDtypeStruct((1,), I32),
        in_specs=[smem] * 3,
        out_specs=smem,
        name="choose",
    )(occ, virt, win)[0]


def live_device(nrow, ncol, t2, ints, eps_occ, eps_virt, occ, virt, win):
    row, col = lax.axis_index("row"), lax.axis_index("col")
    index = choose(occ, virt, win)
    occ_rows = lax.dynamic_slice(eps_occ, (2 * row, 0), (2, OCC_CAP)).reshape(2, OCC_CAP, 1)
    col_occ = lax.dynamic_slice(eps_occ, (col, 0), (1, OCC_CAP))
    col_virt = lax.dynamic_slice(eps_virt, (col ^ win[0], 0), (1, VIR_CAP))
    col_energy = (col_occ[:, None, :] - col_virt[:, :, None]).reshape(1, BLOCK)
    at = jnp.stack([row, col]).astype(I32)
    order = ring_order(nrow)
    table = [[order[(order.index(z) - t) % nrow] for t in range(nrow)] for z in range(nrow)]
    sources = lax.dynamic_slice(jnp.array(table, I32), (row, 0), (1, nrow)).reshape(nrow)
    operands = (t2, ints, occ, virt, win, eps_virt, occ_rows, col_energy, at, sources)
    return lax.switch(index, [functools.partial(branch, size, nrow, ncol) for size in SIZES], *operands)


def ph_vectors(eps_occ, eps_virt, occ_count, virt_count, window_irrep):
    irreps = jnp.arange(NIRREP, dtype=I32)
    partner = jnp.bitwise_xor(irreps, window_irrep[0])
    onehot = partner[:, None] == irreps[None, :]
    virt_rows = jnp.dot(onehot.astype(F32), eps_virt, precision=lax.Precision.HIGHEST)
    virt_live = jnp.sum(jnp.where(onehot, virt_count[None, :], 0), axis=1)
    energy = eps_occ[:, None, :] - virt_rows[:, :, None]
    slots_occ = jnp.arange(OCC_CAP, dtype=I32)
    slots_virt = jnp.arange(VIR_CAP, dtype=I32)
    live = (slots_occ[None, None, :] < occ_count[:, None, None]) & (
        slots_virt[None, :, None] < virt_live[:, None, None]
    )
    return (energy, live)


def any_device(t2_pairs, cycle_ints, eps_occ, eps_virt, occ_count, virt_count, window_irrep):
    irrep_local = t2_pairs.shape[0]
    virt_local = t2_pairs.shape[4]
    total = NIRREP * VIR_CAP * OCC_CAP
    energy, live = ph_vectors(eps_occ, eps_virt, occ_count, virt_count, window_irrep)
    row_index = lax.axis_index("row")
    col_index = lax.axis_index("col")
    zero_index = jnp.int32(0)
    source_live = lax.dynamic_slice(
        live,
        (row_index * irrep_local, col_index * virt_local, zero_index),
        (irrep_local, virt_local, OCC_CAP),
    )
    full_live = live.reshape(-1)
    ordered = jnp.transpose(t2_pairs, (0, 4, 2, 1, 5, 3)).reshape(
        irrep_local, virt_local, OCC_CAP, total
    )
    keep = source_live[:, :, :, None] & full_live[None, None, None, :]
    ordered = jnp.where(keep, ordered, jnp.zeros_like(ordered))
    moved = lax.all_to_all(ordered, "col", split_axis=3, concat_axis=1, tiled=True)
    amp_local = moved.reshape(irrep_local * VIR_CAP * OCC_CAP, moved.shape[3])
    amp_panel = lax.all_gather(amp_local, "row", axis=0, tiled=True)
    ints_panel = lax.all_gather(cycle_ints, "col", axis=1, tiled=True)
    cycle = jnp.dot(ints_panel, amp_panel, preferred_element_type=F32)
    rows_here, cols_here = cycle.shape
    flat_energy = energy.reshape(-1)
    row_start, col_start = row_index * rows_here, col_index * cols_here
    row_energy = lax.dynamic_slice_in_dim(flat_energy, row_start, rows_here, 0)
    col_energy = lax.dynamic_slice_in_dim(flat_energy, col_start, cols_here, 0)
    row_live = lax.dynamic_slice_in_dim(full_live, row_start, rows_here, 0)
    col_live = lax.dynamic_slice_in_dim(full_live, col_start, cols_here, 0)
    denom = row_energy[:, None] + col_energy[None, :]
    return jnp.where(row_live[:, None] & col_live[None, :], cycle / denom, F32(0.0))


def solution(mesh):
    nrow, ncol = mesh.shape["row"], mesh.shape["col"]
    placed = (P("row", None, None, None, "col", None), P("row", "col"), P(), P(), P(), P(), P())
    body = any_device
    if 2 * nrow == NIRREP and ncol == NIRREP:
        body = functools.partial(live_device, nrow, ncol)
    return jax.shard_map(body, mesh=mesh, in_specs=placed, out_specs=P("row", "col"), check_vma=False)
```

```python
import functools

import jax
import jax.numpy as jnp
from jax import lax
from jax.experimental import pallas as pl
from jax.experimental.pallas import tpu as pltpu
from jax.sharding import PartitionSpec as P

NIRREP = 8
OCC_CAP = 16
VIR_CAP = 64
BLOCK = VIR_CAP * OCC_CAP
SIZES = (1024, 640, 896, 768)
WIDE = 512
F32 = jnp.float32
BF16 = jnp.bfloat16
I32 = jnp.int32
I16 = jnp.int16
VMEM_BYTES = 56 * 1024 * 1024


def iota(shape, dim):
    return lax.broadcasted_iota(I32, shape, dim)


def params():
    return pltpu.CompilerParams(vmem_limit_bytes=VMEM_BYTES)


def cost(flops, nbytes):
    return pl.CostEstimate(flops=flops, bytes_accessed=nbytes, transcendentals=0)


def pair_scalars(occ, virt, win, pair):
    first = 2 * pair
    o_a, o_b = occ[first], occ[first + 1]
    v_a, v_b = virt[first ^ win[0]], virt[(first + 1) ^ win[0]]
    return (o_a, o_b), (v_a, v_b), (o_a * ((v_a + 1) >> 1), o_a * (v_a >> 1))


def place(q, p, second, counts):
    (o_a, o_b), (v_a, v_b), (start_even, start_odd) = counts
    o = jnp.where(second, o_b, o_a)
    v = jnp.where(second, v_b, v_a)
    start = jnp.where(second, jnp.where((q & 1) == 0, start_even, start_odd), 0)
    return jnp.where((p < o) & (q < v), start + (q >> 1) * o + p, -1)


def one_hot(left, right):
    return jnp.where(left.astype(I16) == right.astype(I16), BF16(1.0), BF16(0.0))


def dot(a, b):
    return jnp.dot(a, b, preferred_element_type=F32)


def prep_kernel(size, occ, virt, win, t2_ref, even_ref, odd_ref, x_ref):
    counts = pair_scalars(occ, virt, win, pl.program_id(0))
    row = iota((256, 1), 0)
    source = (((row >> 6) & 1) << 7) | (((row >> 2) & 15) << 3) | ((row & 3) << 1) | (row >> 7)
    by_parity = one_hot(iota((256, 256), 1), source)
    targets = []
    for half in range(2):
        for group in range(4):
            parts = [
                t2_ref[:, half, :, 4 * group + i].astype(F32).reshape(256, VIR_CAP) for i in range(4)
            ]
            x = jnp.concatenate(parts, axis=1).astype(BF16)
            at = (4 * half + group) * 256
            x_ref[:, at : at + 256] = dot(by_parity, x).astype(BF16)
            r = iota((256, 1), 0)
            p, q = 4 * group + (r >> 6), r & 63
            spot = place(q, p, half == 1, counts)
            targets.append(jnp.where(spot >= 0, spot + (q & 1) * size, -1))
    @pl.loop(0, 2)
    def _(core):
        for tile in range(-(-size // 256)):
            col = min(256 * tile, size - 256)
            lane = iota((256, 256), 1) + (col + core * size)
            acc = jnp.zeros((256, 256), F32)
            for chunk in range(4 if col >= BLOCK // 2 else 0, 8):
                acc += dot(x_ref[:, chunk * 256 : chunk * 256 + 256], one_hot(targets[chunk], lane))
            acc = acc.astype(BF16)
            even_ref[core, :, col : col + 256] = acc[:128]
            odd_ref[core, :, col : col + 256] = acc[128:]


def prep(size, scalars, t2):
    shape = jax.ShapeDtypeStruct((NIRREP, 128, size), BF16)
    block = pl.BlockSpec((2, 128, size), lambda k, *_: (k, 0, 0))
    return pl.pallas_call(
        functools.partial(prep_kernel, size),
        out_shape=(shape, shape),
        grid_spec=pltpu.PrefetchScalarGridSpec(
            num_scalar_prefetch=3,
            grid=(NIRREP // 2,),
            in_specs=[
                pl.BlockSpec((2, 2, OCC_CAP, OCC_CAP, 8, VIR_CAP), lambda k, *_: (0, k, 0, 0, 0, 0))
            ],
            out_specs=[block, block],
            scratch_shapes=[pltpu.VMEM((256, 2048), BF16)],
        ),
        compiler_params=params(),
        cost_estimate=cost(2 * 4 * 256 * 2048 * 2 * size, 12 * 2**20),
        name="prep_amplitudes",
    )(*scalars, t2)


def fill_rows(rows, spot, sel_ref):
    @pl.loop(0, rows // 128)
    def _(n):
        first = pl.multiple_of(n * 128, 128)
        sel_ref[pl.ds(first, 128), :] = one_hot(iota((128, BLOCK), 0) + first, spot)


def rows_kernel(rows, parity, count, occ, virt, win, at, x_ref, *refs):
    out_ref, sel_ref = refs[count], refs[-1]
    counts = pair_scalars(occ, virt, win, at[0])
    i = iota((1, BLOCK), 1)
    q = 8 * (i >> 7) + 2 * (i & 3) + parity
    spot = place(q, (i >> 2) & 15, ((i >> 6) & 1) == 1, counts)
    fill_rows(rows, spot, sel_ref)
    cols = out_ref.shape[1]

    @pl.loop(0, -(-cols // 256))
    def _(n):
        lanes = pl.ds(pl.multiple_of(jnp.minimum(n * 256, cols - 256), 128), 256)
        x = x_ref[:, :, lanes].reshape(BLOCK, 256)

        @pl.loop(0, 2)
        def _(half):
            at_rows = pl.ds(pl.multiple_of(half * (rows // 2), 64), rows // 2)
            out_ref[at_rows, lanes] = dot(sel_ref[at_rows, :], x).astype(BF16)


def compact_rows(rows, cols, parity, scalars, at, x, passed=(), awaited=()):
    whole = pl.BlockSpec(memory_space=pl.ANY)
    return pl.pallas_call(
        functools.partial(rows_kernel, rows, parity, len(passed) + len(awaited)),
        out_shape=[jax.ShapeDtypeStruct((rows, cols), BF16)]
        + [jax.ShapeDtypeStruct(y.shape, y.dtype) for y in passed],
        grid_spec=pltpu.PrefetchScalarGridSpec(
            num_scalar_prefetch=4,
            grid=(1,),
            in_specs=[pl.BlockSpec((NIRREP, 128, cols), lambda n, *_: (0, 0, 0))]
            + [whole] * (len(passed) + len(awaited)),
            out_specs=[pl.BlockSpec((rows, cols), lambda n, *_: (0, 0))] + [whole] * len(passed),
            scratch_shapes=[pltpu.VMEM((rows, BLOCK), BF16)],
        ),
        input_output_aliases={5 + i: 1 + i for i in range(len(passed))},
        compiler_params=params(),
        cost_estimate=cost(4 * rows * BLOCK * cols, 4 * rows * BLOCK),
        name="compact_rows",
    )(*scalars, at, x, *passed, *awaited)


def ints_kernel(rows, cols, occ, virt, win, at, mine_ref, other_ref, awaited, out_ref, sel_ref, cols_ref):
    plane, dev = at[0], at[1]
    parity = dev & 1

    @pl.when(pl.program_id(0) == 0)
    def _():
        counts = pair_scalars(occ, virt, win, plane)
        i = iota((1, BLOCK), 1)
        q = 2 * ((i >> 4) & 31) + parity
        spot = place(q, i & 15, (i >> 9) == 1, counts)
        fill_rows(rows, spot, sel_ref)

    counts = pair_scalars(occ, virt, win, dev >> 1)
    i = iota((BLOCK, 1), 0)
    q, p = i >> 4, i & 15
    lane = iota((BLOCK, 256), 1) + pl.program_id(0) * 256
    picks = []
    for second in (parity == 1, parity == 0):
        spot = place(q, p, second, counts)
        picks.append(one_hot(jnp.where(spot >= 0, spot + (q & 1) * cols, -1), lane))

    @pl.loop(0, 2)
    def _(half):
        at_rows = pl.ds(pl.multiple_of(half * (BLOCK // 2), BLOCK // 2), BLOCK // 2)
        acc = dot(mine_ref[half].reshape(BLOCK // 2, BLOCK), picks[0])
        acc += dot(other_ref[at_rows, :], picks[1])
        cols_ref[at_rows, :] = acc.astype(BF16)

    out_ref[...] = dot(sel_ref[...], cols_ref[...]).astype(BF16)


def compact_ints(rows, cols, scalars, at, mine, other, awaited):
    mine_spec = pl.BlockSpec(
        (2, VIR_CAP // 2, 1, OCC_CAP, BLOCK), lambda n, o, v, w, a: (0, 0, a[1] & 1, 0, 0)
    )
    whole = pl.BlockSpec((BLOCK, BLOCK), lambda n, *_: (0, 0))
    return pl.pallas_call(
        functools.partial(ints_kernel, rows, cols),
        out_shape=jax.ShapeDtypeStruct((rows, 2 * cols), BF16),
        grid_spec=pltpu.PrefetchScalarGridSpec(
            num_scalar_prefetch=4,
            grid=(2 * cols // 256,),
            in_specs=[mine_spec, whole, pl.BlockSpec(memory_space=pl.ANY)],
            out_specs=pl.BlockSpec((rows, 256), lambda n, *_: (0, n)),
            scratch_shapes=[pltpu.VMEM((rows, BLOCK), BF16), pltpu.VMEM((BLOCK, 256), BF16)],
        ),
        compiler_params=params(),
        cost_estimate=cost(16 * BLOCK * BLOCK * cols, 4 * BLOCK * BLOCK + 4 * rows * cols),
        name="compact_ints",
    )(*scalars, at, mine, other, awaited)


def widen_tile(rows, cols, tile, occ, virt, win, dev, pieces, wide_ref):
    parity = dev & 1
    counts = pair_scalars(occ, virt, win, dev >> 1)
    (o_a, o_b), _, (start_even, start_odd) = counts
    second = parity == 1
    o = jnp.where(second, o_b, o_a)
    i = iota((1, 256), 1) + tile * 256
    q = i >> 4
    spot = place(q, i & 15, second, counts)
    r = iota((256, 256), 0)
    picks = []
    for s in (parity, 1 - parity):
        start = jnp.where(second, jnp.where(s == 0, start_even, start_odd), 0) + 8 * tile * o
        start = jnp.minimum((start >> 7) << 7, cols - 256)
        window = pl.ds(pl.multiple_of(start, 128), 256)
        picks.append((window, one_hot(r + start, jnp.where((q & 1) == s, spot, -1))))
    for piece, (own_ref, sib_ref) in enumerate(pieces):
        x = dot(own_ref[:, picks[0][0]], picks[0][1]) + dot(sib_ref[:, picks[1][0]], picks[1][1])
        wide_ref[piece * cols : piece * cols + rows, :] = x.astype(BF16)
        if rows < cols:
            wide_ref[piece * cols + rows : (piece + 1) * cols, :] = jnp.zeros((cols - rows, 256), BF16)


def widen_kernel(rows, cols, slots, occ, virt, win, at, *refs):
    wide_ref = refs[-1]
    for slot in range(slots):

        @pl.when(pl.program_id(0) == slot)
        def _():
            t0, t1, s0, s1 = refs[4 * slot : 4 * slot + 4]
            tile = pl.program_id(1)
            widen_tile(rows, cols, tile, occ, virt, win, at[1], ((t0, s0), (t1, s1)), wide_ref.at[0])


def widen(rows, cols, scalars, at, blocks):
    slots = len(blocks) // 4
    square = pl.BlockSpec((rows, cols), lambda t, n, *_: (0, 0), pipeline_mode=pl.Buffered(1))
    return pl.pallas_call(
        functools.partial(widen_kernel, rows, cols, slots),
        out_shape=jax.ShapeDtypeStruct((slots, 2 * cols, BLOCK), BF16),
        grid_spec=pltpu.PrefetchScalarGridSpec(
            num_scalar_prefetch=4,
            grid=(slots, BLOCK // 256),
            in_specs=[square] * len(blocks),
            out_specs=pl.BlockSpec((1, 2 * cols, 256), lambda t, n, *_: (t, 0, n)),
        ),
        compiler_params=params(),
        cost_estimate=cost(slots * 8 * rows * 512 * BLOCK, slots * (8 * rows * cols + 4 * cols * BLOCK)),
        name="widen",
    )(*scalars, at, *blocks)


def widen_wide(rows, cols, n, occ, virt, win, dev, own_ref, sib_ref, wide_ref):
    @pl.loop(0, WIDE // 256)
    def _(part):
        into = wide_ref.at[:, pl.ds(pl.multiple_of(part * 256, 256), 256)]
        tile = n * (WIDE // 256) + part
        widen_tile(rows, cols, tile, occ, virt, win, dev, ((own_ref, sib_ref),), into)


def product_kernel(
    rows, cols, slots, occ, virt, win, at, inner, ints_ref, wide_ref, own_ref, sib_ref, acc_ref, part_ref
):
    step = pl.program_id(0)
    lanes = pl.ds(pl.multiple_of(pl.program_id(1) * WIDE, WIDE), WIDE)

    @pl.when(step == 0)
    def _():
        acc_ref[:, :, lanes] = jnp.zeros((2, rows, WIDE), F32)

    @pl.when(step < slots)
    def _():
        @pl.loop(0, 2)
        def _(half):
            acc_ref[half, :, lanes] += dot(ints_ref[0, half], wide_ref[0])

    @pl.when(step == slots)
    def _():
        widen_wide(rows, cols, pl.program_id(1), occ, virt, win, at[1], own_ref, sib_ref, part_ref)

        @pl.loop(0, 2)
        def _(half):
            acc_ref[half, :, lanes] += dot(ints_ref[0, half, :, :cols], part_ref[...])


def product(rows, cols, scalars, at, inner, ints, wide, own, sib):
    slots = wide.shape[0]
    square = pl.BlockSpec((rows, cols), lambda t, n, *_: (0, 0), pipeline_mode=pl.Buffered(1))
    return pl.pallas_call(
        functools.partial(product_kernel, rows, cols, slots),
        out_shape=jax.ShapeDtypeStruct((2, rows, BLOCK), F32),
        grid_spec=pltpu.PrefetchScalarGridSpec(
            num_scalar_prefetch=5,
            grid=(slots + 1, BLOCK // WIDE),
            in_specs=[
                pl.BlockSpec((1, 2, rows, 2 * cols), lambda t, n, o, v, w, a, k: (k[t], 0, 0, 0)),
                pl.BlockSpec((1, 2 * cols, WIDE), lambda t, n, *_: (jnp.minimum(t, slots - 1), 0, n)),
                square,
                square,
            ],
            out_specs=pl.BlockSpec((2, rows, BLOCK), lambda t, n, *_: (0, 0, 0)),
            scratch_shapes=[pltpu.VMEM((cols, WIDE), BF16)],
        ),
        compiler_params=params(),
        cost_estimate=cost(16 * slots * rows * cols * BLOCK, slots * 4 * cols * (rows + BLOCK)),
        name="product",
    )(*scalars, at, inner, ints, wide, own, sib)


def last_kernel(
    rows, cols, occ, virt, win, at, inner,
    ints_ref, own_ref, sib_ref, old_ref, evirt, eocc_ref, ecol_ref, out_ref, wide_ref, sum_ref,
):
    plane, dev = at[0], at[1]

    widen_wide(rows, cols, pl.program_id(0), occ, virt, win, dev, own_ref, sib_ref, wide_ref)

    @pl.loop(0, 2)
    def _(half):
        sum_ref[half, :rows, :] = old_ref[half] + dot(ints_ref[0, half], wide_ref[...])

    i = iota((1, WIDE), 1) + pl.program_id(0) * WIDE
    col_live = ((i & 15) < occ[dev]) & ((i >> 4) < virt[dev ^ win[0]])
    col_energy = ecol_ref[...]
    _, _, starts = pair_scalars(occ, virt, win, plane)
    p = iota((OCC_CAP, 1), 0)
    irreps = [2 * plane, 2 * plane + 1]
    occs = [occ[irrep] for irrep in irreps]
    partners = [irrep ^ win[0] for irrep in irreps]
    virts = [virt[partner] for partner in partners]
    live = [(p < o) & col_live for o in occs]

    @pl.loop(0, VIR_CAP // 4)
    def _(group):
        for h in range(2):
            for i in range(4):
                half_q, s = 2 * group + i // 2, i % 2
                q = 2 * half_q + s
                start = half_q * occs[h]
                if h == 1:
                    start = start + starts[s]
                start = jnp.minimum(start, rows)
                block = sum_ref[s, pl.ds(pl.multiple_of((start >> 3) << 3, 8), OCC_CAP + 8), :]
                block = pltpu.roll(block, OCC_CAP + 8 - (start & 7), 0)[:OCC_CAP]
                denom = (eocc_ref[h] - evirt[partners[h], q]) + col_energy
                value = jnp.where(live[h] & (q < virts[h]), block / denom, 0.0)
                at_row = pl.multiple_of((h * VIR_CAP + q) * OCC_CAP, OCC_CAP)
                out_ref[pl.ds(at_row, OCC_CAP), :] = value


def last(rows, cols, scalars, at, inner, ints, own, sib, acc, energies):
    square = pl.BlockSpec((rows, cols), lambda n, *_: (0, 0))
    return pl.pallas_call(
        functools.partial(last_kernel, rows, cols),
        out_shape=jax.ShapeDtypeStruct((2 * BLOCK, BLOCK), F32),
        grid_spec=pltpu.PrefetchScalarGridSpec(
            num_scalar_prefetch=5,
            grid=(BLOCK // WIDE,),
            in_specs=[
                pl.BlockSpec((1, 2, rows, cols), lambda n, o, v, w, a, k: (k[0], 0, 0, 1)),
                square,
                square,
                pl.BlockSpec((2, rows, WIDE), lambda n, *_: (0, 0, n)),
                pl.BlockSpec(memory_space=pltpu.SMEM),
                pl.BlockSpec((2, OCC_CAP, 1), lambda n, *_: (0, 0, 0)),
                pl.BlockSpec((1, WIDE), lambda n, *_: (0, n)),
            ],
            out_specs=pl.BlockSpec((2 * BLOCK, WIDE), lambda n, *_: (0, n)),
            scratch_shapes=[
                pltpu.VMEM((cols, WIDE), BF16),
                pltpu.VMEM((2, rows + OCC_CAP + 8, WIDE), F32),
            ],
        ),
        compiler_params=params(),
        cost_estimate=cost(16 * rows * cols * BLOCK, 8 * rows * cols + 16 * rows * BLOCK),
        name="last_product",
    )(*scalars, at, inner, ints, own, sib, acc, *energies)


def after_kernel(*refs):
    pass


def after(kept, awaited):
    whole = pl.BlockSpec(memory_space=pl.ANY)
    return pl.pallas_call(
        after_kernel,
        out_shape=[jax.ShapeDtypeStruct(x.shape, x.dtype) for x in kept],
        in_specs=[whole] * (len(kept) + len(awaited)),
        out_specs=[whole] * len(kept),
        input_output_aliases={i: i for i in range(len(kept))},
        name="after",
    )(*kept, *awaited)


def ring_order(n):
    return list(range(0, 1)) + list(range(1, n, 2)) + [i for i in range(n - 1, 0, -1) if i % 2 == 0]


def branch(rows, nrow, ncol, t2, ints, occ, virt, win, eps_virt, occ_rows, col_energy, at, sources):
    cols = -(-rows // 128) * 128
    scalars = (occ, virt, win)
    order = ring_order(nrow)
    ring = [(order[i], order[(i + 1) % nrow]) for i in range(nrow)]
    swap = [(c, c ^ 1) for c in range(ncol)]

    def to_sibling(x):
        return lax.ppermute(x, "col", swap)

    def around(x):
        return lax.ppermute(x, "row", ring)

    def exchange(x):
        return lax.all_to_all(x, "col", split_axis=0, concat_axis=0, tiled=True)

    even, odd = prep(cols, scalars, t2)
    even, odd = compact_rows(rows, cols, 0, scalars, at, exchange(even), passed=(odd,))
    mine = ints.reshape(2, VIR_CAP // 2, 2, OCC_CAP, BLOCK)
    other = lax.dynamic_index_in_dim(mine, 1 - (at[1] & 1), 2, keepdims=False).reshape(BLOCK, BLOCK)
    even_next = around(even)
    small = compact_ints(rows, cols, scalars, at, mine, to_sibling(other), even)
    odd, small = compact_rows(rows, cols, 1, scalars, at, exchange(odd), passed=(small,))
    odd, small = after([odd, small], [even_next])
    panel = lax.all_gather(small, "col", axis=0, tiled=False).reshape(ncol // 2, 2, rows, 2 * cols)

    held = [even, odd]
    blocks = []
    for step in range(nrow - 1):
        later = [even_next if step == 0 else around(held[0]), around(held[1])]
        blocks += held + [to_sibling(x) for x in held]
        held = later
    wide = widen(rows, cols, scalars, at, blocks)
    (even,) = after([held[0]], [wide])
    acc = product(rows, cols, scalars, at, sources, panel, wide, even, to_sibling(even))
    (odd,) = after([held[1]], [acc])
    energies = (eps_virt, occ_rows, col_energy)
    inner = sources[nrow - 1 :]
    return last(rows, cols, scalars, at, inner, panel, odd, to_sibling(odd), acc, energies)


def choose_kernel(occ, virt, win, index_ref):
    most = jnp.int32(0)
    for pair in range(NIRREP // 2):
        (o_a, o_b), (v_a, v_b), _ = pair_scalars(occ, virt, win, pair)
        most = jnp.maximum(most, o_a * ((v_a + 1) >> 1) + o_b * ((v_b + 1) >> 1))
    index = jnp.int32(SIZES.index(max(SIZES)))
    for size in sorted(SIZES, reverse=True):
        index = jnp.where(most <= size, SIZES.index(size), index)
    index_ref[0] = index


def choose(occ, virt, win):
    smem = pl.BlockSpec(memory_space=pltpu.SMEM)
    return pl.pallas_call(
        choose_kernel,
        out_shape=jax.ShapeDtypeStruct((1,), I32),
        in_specs=[smem] * 3,
        out_specs=smem,
        name="choose",
    )(occ, virt, win)[0]


def live_device(nrow, ncol, t2, ints, eps_occ, eps_virt, occ, virt, win):
    row, col = lax.axis_index("row"), lax.axis_index("col")
    index = choose(occ, virt, win)
    occ_rows = lax.dynamic_slice(eps_occ, (2 * row, 0), (2, OCC_CAP)).reshape(2, OCC_CAP, 1)
    col_occ = lax.dynamic_slice(eps_occ, (col, 0), (1, OCC_CAP))
    col_virt = lax.dynamic_slice(eps_virt, (col ^ win[0], 0), (1, VIR_CAP))
    col_energy = (col_occ[:, None, :] - col_virt[:, :, None]).reshape(1, BLOCK)
    at = jnp.stack([row, col]).astype(I32)
    order = ring_order(nrow)
    table = [[order[(order.index(z) - t) % nrow] for t in range(nrow)] for z in range(nrow)]
    sources = lax.dynamic_slice(jnp.array(table, I32), (row, 0), (1, nrow)).reshape(nrow)
    operands = (t2, ints, occ, virt, win, eps_virt, occ_rows, col_energy, at, sources)
    return lax.switch(index, [functools.partial(branch, size, nrow, ncol) for size in SIZES], *operands)


def ph_vectors(eps_occ, eps_virt, occ_count, virt_count, window_irrep):
    irreps = jnp.arange(NIRREP, dtype=I32)
    partner = jnp.bitwise_xor(irreps, window_irrep[0])
    onehot = partner[:, None] == irreps[None, :]
    virt_rows = jnp.dot(onehot.astype(F32), eps_virt, precision=lax.Precision.HIGHEST)
    virt_live = jnp.sum(jnp.where(onehot, virt_count[None, :], 0), axis=1)
    energy = eps_occ[:, None, :] - virt_rows[:, :, None]
    slots_occ = jnp.arange(OCC_CAP, dtype=I32)
    slots_virt = jnp.arange(VIR_CAP, dtype=I32)
    live = (slots_occ[None, None, :] < occ_count[:, None, None]) & (
        slots_virt[None, :, None] < virt_live[:, None, None]
    )
    return (energy, live)


def any_device(t2_pairs, cycle_ints, eps_occ, eps_virt, occ_count, virt_count, window_irrep):
    irrep_local = t2_pairs.shape[0]
    virt_local = t2_pairs.shape[4]
    total = NIRREP * VIR_CAP * OCC_CAP
    energy, live = ph_vectors(eps_occ, eps_virt, occ_count, virt_count, window_irrep)
    row_index = lax.axis_index("row")
    col_index = lax.axis_index("col")
    zero_index = jnp.int32(0)
    source_live = lax.dynamic_slice(
        live,
        (row_index * irrep_local, col_index * virt_local, zero_index),
        (irrep_local, virt_local, OCC_CAP),
    )
    full_live = live.reshape(-1)
    ordered = jnp.transpose(t2_pairs, (0, 4, 2, 1, 5, 3)).reshape(
        irrep_local, virt_local, OCC_CAP, total
    )
    keep = source_live[:, :, :, None] & full_live[None, None, None, :]
    ordered = jnp.where(keep, ordered, jnp.zeros_like(ordered))
    moved = lax.all_to_all(ordered, "col", split_axis=3, concat_axis=1, tiled=True)
    amp_local = moved.reshape(irrep_local * VIR_CAP * OCC_CAP, moved.shape[3])
    amp_panel = lax.all_gather(amp_local, "row", axis=0, tiled=True)
    ints_panel = lax.all_gather(cycle_ints, "col", axis=1, tiled=True)
    cycle = jnp.dot(ints_panel, amp_panel, preferred_element_type=F32)
    rows_here, cols_here = cycle.shape
    flat_energy = energy.reshape(-1)
    row_start, col_start = row_index * rows_here, col_index * cols_here
    row_energy = lax.dynamic_slice_in_dim(flat_energy, row_start, rows_here, 0)
    col_energy = lax.dynamic_slice_in_dim(flat_energy, col_start, cols_here, 0)
    row_live = lax.dynamic_slice_in_dim(full_live, row_start, rows_here, 0)
    col_live = lax.dynamic_slice_in_dim(full_live, col_start, cols_here, 0)
    denom = row_energy[:, None] + col_energy[None, :]
    return jnp.where(row_live[:, None] & col_live[None, :], cycle / denom, F32(0.0))


def solution(mesh):
    nrow, ncol = mesh.shape["row"], mesh.shape["col"]
    placed = (P("row", None, None, None, "col", None), P("row", "col"), P(), P(), P(), P(), P())
    body = any_device
    if 2 * nrow == NIRREP and ncol == NIRREP:
        body = functools.partial(live_device, nrow, ncol)
    return jax.shard_map(body, mesh=mesh, in_specs=placed, out_specs=P("row", "col"), check_vma=False)
```

```python
import functools

import jax
import jax.numpy as jnp
from jax import lax
from jax.experimental import pallas as pl
from jax.experimental.pallas import tpu as pltpu
from jax.sharding import PartitionSpec as P

NIRREP = 8
OCC_CAP = 16
VIR_CAP = 64
BLOCK = VIR_CAP * OCC_CAP
SIZES = (1024, 896, 768, 640)
WIDE = 512
F32 = jnp.float32
BF16 = jnp.bfloat16
I32 = jnp.int32
I16 = jnp.int16
VMEM_BYTES = 56 * 1024 * 1024


def iota(shape, dim):
    return lax.broadcasted_iota(I32, shape, dim)


def params():
    return pltpu.CompilerParams(vmem_limit_bytes=VMEM_BYTES)


def cost(flops, nbytes):
    return pl.CostEstimate(flops=flops, bytes_accessed=nbytes, transcendentals=0)


def pair_scalars(occ, virt, win, pair):
    first = 2 * pair
    o_a, o_b = occ[first], occ[first + 1]
    v_a, v_b = virt[first ^ win[0]], virt[(first + 1) ^ win[0]]
    return (o_a, o_b), (v_a, v_b), (o_a * ((v_a + 1) >> 1), o_a * (v_a >> 1))


def place(q, p, second, counts):
    (o_a, o_b), (v_a, v_b), (start_even, start_odd) = counts
    o = jnp.where(second, o_b, o_a)
    v = jnp.where(second, v_b, v_a)
    start = jnp.where(second, jnp.where((q & 1) == 0, start_even, start_odd), 0)
    return jnp.where((p < o) & (q < v), start + (q >> 1) * o + p, -1)


def one_hot(left, right):
    return jnp.where(left.astype(I16) == right.astype(I16), BF16(1.0), BF16(0.0))


def dot(a, b):
    return jnp.dot(a, b, preferred_element_type=F32)


def prep_kernel(size, occ, virt, win, t2_ref, even_ref, odd_ref, x_ref, acc_ref):
    counts = pair_scalars(occ, virt, win, pl.program_id(0))
    row = iota((256, 1), 0)
    source = (((row >> 6) & 1) << 7) | (((row >> 2) & 15) << 3) | ((row & 3) << 1) | (row >> 7)
    by_parity = one_hot(iota((256, 256), 1), source)
    targets = []
    for half in range(2):
        for group in range(4):
            parts = [
                t2_ref[:, half, :, 4 * group + i].astype(F32).reshape(256, VIR_CAP) for i in range(4)
            ]
            x = jnp.concatenate(parts, axis=1).astype(BF16)
            at = (4 * half + group) * 256
            x_ref[:, at : at + 256] = dot(by_parity, x).astype(BF16)
            r = iota((256, 1), 0)
            p, q = 4 * group + (r >> 6), r & 63
            spot = place(q, p, half == 1, counts)
            targets.append(jnp.where(spot >= 0, spot + (q & 1) * size, -1))
    (o_a, o_b), (v_a, v_b), (start_even, start_odd) = counts

    @pl.loop(0, 2)
    def _(core):
        start = jnp.where(core == 0, start_even, start_odd)
        end = start + o_b * ((v_b + 1 - core) >> 1)
        for tile in range(-(-size // 256)):
            col = min(256 * tile, size - 256)
            lane = iota((256, 256), 1) + (col + core * size)

            def part(half):
                chunks = range(4 * half, 4 * half + 4)
                return sum(
                    dot(x_ref[:, c * 256 : c * 256 + 256], one_hot(targets[c], lane)) for c in chunks
                )

            acc_ref[...] = jnp.zeros((256, 256), F32)
            if col < BLOCK // 2:

                @pl.when(start > col)
                def _():
                    acc_ref[...] += part(0)

            @pl.when((start < col + 256) & (end > col))
            def _():
                acc_ref[...] += part(1)

            acc = acc_ref[...].astype(BF16)
            even_ref[core, :, col : col + 256] = acc[:128]
            odd_ref[core, :, col : col + 256] = acc[128:]


def prep(size, scalars, t2):
    shape = jax.ShapeDtypeStruct((NIRREP, 128, size), BF16)
    block = pl.BlockSpec((2, 128, size), lambda k, *_: (k, 0, 0))
    return pl.pallas_call(
        functools.partial(prep_kernel, size),
        out_shape=(shape, shape),
        grid_spec=pltpu.PrefetchScalarGridSpec(
            num_scalar_prefetch=3,
            grid=(NIRREP // 2,),
            in_specs=[
                pl.BlockSpec((2, 2, OCC_CAP, OCC_CAP, 8, VIR_CAP), lambda k, *_: (0, k, 0, 0, 0, 0))
            ],
            out_specs=[block, block],
            scratch_shapes=[pltpu.VMEM((256, 2048), BF16), pltpu.VMEM((256, 256), F32)],
        ),
        compiler_params=params(),
        cost_estimate=cost(2 * 4 * 256 * 2048 * 2 * size, 12 * 2**20),
        name="prep_amplitudes",
    )(*scalars, t2)


def fill_rows(rows, spot, sel_ref):
    @pl.loop(0, rows // 128)
    def _(n):
        first = pl.multiple_of(n * 128, 128)
        sel_ref[pl.ds(first, 128), :] = one_hot(iota((128, BLOCK), 0) + first, spot)


def rows_kernel(rows, parity, count, occ, virt, win, at, x_ref, *refs):
    out_ref, sel_ref = refs[count], refs[-1]
    counts = pair_scalars(occ, virt, win, at[0])
    i = iota((1, BLOCK), 1)
    q = 8 * (i >> 7) + 2 * (i & 3) + parity
    spot = place(q, (i >> 2) & 15, ((i >> 6) & 1) == 1, counts)
    fill_rows(rows, spot, sel_ref)
    cols = out_ref.shape[1]

    @pl.loop(0, -(-cols // 256))
    def _(n):
        lanes = pl.ds(pl.multiple_of(jnp.minimum(n * 256, cols - 256), 128), 256)
        x = x_ref[:, :, lanes].reshape(BLOCK, 256)

        @pl.loop(0, 2)
        def _(half):
            at_rows = pl.ds(pl.multiple_of(half * (rows // 2), 64), rows // 2)
            out_ref[at_rows, lanes] = dot(sel_ref[at_rows, :], x).astype(BF16)


def compact_rows(rows, cols, parity, scalars, at, x, passed=(), awaited=()):
    whole = pl.BlockSpec(memory_space=pl.ANY)
    return pl.pallas_call(
        functools.partial(rows_kernel, rows, parity, len(passed) + len(awaited)),
        out_shape=[jax.ShapeDtypeStruct((rows, cols), BF16)]
        + [jax.ShapeDtypeStruct(y.shape, y.dtype) for y in passed],
        grid_spec=pltpu.PrefetchScalarGridSpec(
            num_scalar_prefetch=4,
            grid=(1,),
            in_specs=[pl.BlockSpec((NIRREP, 128, cols), lambda n, *_: (0, 0, 0))]
            + [whole] * (len(passed) + len(awaited)),
            out_specs=[pl.BlockSpec((rows, cols), lambda n, *_: (0, 0))] + [whole] * len(passed),
            scratch_shapes=[pltpu.VMEM((rows, BLOCK), BF16)],
        ),
        input_output_aliases={5 + i: 1 + i for i in range(len(passed))},
        compiler_params=params(),
        cost_estimate=cost(4 * rows * BLOCK * cols, 4 * rows * BLOCK),
        name="compact_rows",
    )(*scalars, at, x, *passed, *awaited)


def ints_kernel(rows, cols, occ, virt, win, at, mine_ref, other_ref, awaited, out_ref, sel_ref, cols_ref):
    plane, dev = at[0], at[1]
    parity = dev & 1

    @pl.when(pl.program_id(0) == 0)
    def _():
        counts = pair_scalars(occ, virt, win, plane)
        i = iota((1, BLOCK), 1)
        q = 2 * ((i >> 4) & 31) + parity
        spot = place(q, i & 15, (i >> 9) == 1, counts)
        fill_rows(rows, spot, sel_ref)

    counts = pair_scalars(occ, virt, win, dev >> 1)
    i = iota((BLOCK, 1), 0)
    q, p = i >> 4, i & 15
    lane = iota((BLOCK, 256), 1) + pl.program_id(0) * 256
    picks = []
    for second in (parity == 1, parity == 0):
        spot = place(q, p, second, counts)
        picks.append(one_hot(jnp.where(spot >= 0, spot + (q & 1) * cols, -1), lane))

    @pl.loop(0, 2)
    def _(half):
        at_rows = pl.ds(pl.multiple_of(half * (BLOCK // 2), BLOCK // 2), BLOCK // 2)
        acc = dot(mine_ref[half].reshape(BLOCK // 2, BLOCK), picks[0])
        acc += dot(other_ref[at_rows, :], picks[1])
        cols_ref[at_rows, :] = acc.astype(BF16)

    out_ref[...] = dot(sel_ref[...], cols_ref[...]).astype(BF16)


def compact_ints(rows, cols, scalars, at, mine, other, awaited):
    mine_spec = pl.BlockSpec(
        (2, VIR_CAP // 2, 1, OCC_CAP, BLOCK), lambda n, o, v, w, a: (0, 0, a[1] & 1, 0, 0)
    )
    whole = pl.BlockSpec((BLOCK, BLOCK), lambda n, *_: (0, 0))
    return pl.pallas_call(
        functools.partial(ints_kernel, rows, cols),
        out_shape=jax.ShapeDtypeStruct((rows, 2 * cols), BF16),
        grid_spec=pltpu.PrefetchScalarGridSpec(
            num_scalar_prefetch=4,
            grid=(2 * cols // 256,),
            in_specs=[mine_spec, whole, pl.BlockSpec(memory_space=pl.ANY)],
            out_specs=pl.BlockSpec((rows, 256), lambda n, *_: (0, n)),
            scratch_shapes=[pltpu.VMEM((rows, BLOCK), BF16), pltpu.VMEM((BLOCK, 256), BF16)],
        ),
        compiler_params=params(),
        cost_estimate=cost(16 * BLOCK * BLOCK * cols, 4 * BLOCK * BLOCK + 4 * rows * cols),
        name="compact_ints",
    )(*scalars, at, mine, other, awaited)


def widen_tile(rows, cols, tile, occ, virt, win, dev, own_refs, sib_refs, wide_ref):
    parity = dev & 1
    counts = pair_scalars(occ, virt, win, dev >> 1)
    (o_a, o_b), _, (start_even, start_odd) = counts
    second = parity == 1
    o = jnp.where(second, o_b, o_a)
    i = iota((1, 256), 1) + tile * 256
    q = i >> 4
    spot = place(q, i & 15, second, counts)
    r = iota((256, 256), 0)
    picks = []
    for s in (parity, 1 - parity):
        start = jnp.where(second, jnp.where(s == 0, start_even, start_odd), 0) + 8 * tile * o
        start = jnp.minimum((start >> 7) << 7, cols - 256)
        window = pl.ds(pl.multiple_of(start, 128), 256)
        picks.append((window, one_hot(r + start, jnp.where((q & 1) == s, spot, -1))))
    for piece in range(2):
        x = dot(own_refs[piece][:, picks[0][0]], picks[0][1])
        x += dot(sib_refs[piece][:, picks[1][0]], picks[1][1])
        wide_ref[piece * cols : piece * cols + rows, :] = x.astype(BF16)
        if rows < cols:
            wide_ref[piece * cols + rows : (piece + 1) * cols, :] = jnp.zeros((cols - rows, 256), BF16)


def widen_kernel(rows, cols, slots, occ, virt, win, at, *refs):
    wide_ref = refs[-1]
    for slot in range(slots):

        @pl.when(pl.program_id(0) == slot)
        def _():
            t0, t1, s0, s1 = refs[4 * slot : 4 * slot + 4]
            tile = pl.program_id(1)
            widen_tile(rows, cols, tile, occ, virt, win, at[1], (t0, t1), (s0, s1), wide_ref.at[0])


def widen(rows, cols, scalars, at, blocks):
    slots = len(blocks) // 4
    square = pl.BlockSpec((rows, cols), lambda t, n, *_: (0, 0), pipeline_mode=pl.Buffered(1))
    return pl.pallas_call(
        functools.partial(widen_kernel, rows, cols, slots),
        out_shape=jax.ShapeDtypeStruct((slots, 2 * cols, BLOCK), BF16),
        grid_spec=pltpu.PrefetchScalarGridSpec(
            num_scalar_prefetch=4,
            grid=(slots, BLOCK // 256),
            in_specs=[square] * len(blocks),
            out_specs=pl.BlockSpec((1, 2 * cols, 256), lambda t, n, *_: (t, 0, n)),
        ),
        compiler_params=params(),
        cost_estimate=cost(slots * 8 * rows * 512 * BLOCK, slots * (8 * rows * cols + 4 * cols * BLOCK)),
        name="widen",
    )(*scalars, at, *blocks)


def product_kernel(inner, ints_ref, wide_ref, acc_ref):
    at = pl.ds(pl.multiple_of(pl.program_id(1) * WIDE, WIDE), WIDE)

    @pl.when(pl.program_id(0) == 0)
    def _():
        acc_ref[:, :, at] = jnp.zeros((2, acc_ref.shape[1], WIDE), F32)

    @pl.loop(0, 2)
    def _(half):
        acc_ref[half, :, at] += dot(ints_ref[0, half], wide_ref[0])


def product(rows, cols, inner, ints, wide):
    slots = wide.shape[0]
    return pl.pallas_call(
        product_kernel,
        out_shape=jax.ShapeDtypeStruct((2, rows, BLOCK), F32),
        grid_spec=pltpu.PrefetchScalarGridSpec(
            num_scalar_prefetch=1,
            grid=(slots, BLOCK // WIDE),
            in_specs=[
                pl.BlockSpec((1, 2, rows, 2 * cols), lambda t, n, k: (k[t], 0, 0, 0)),
                pl.BlockSpec((1, 2 * cols, WIDE), lambda t, n, k: (t, 0, n)),
            ],
            out_specs=pl.BlockSpec((2, rows, BLOCK), lambda t, n, k: (0, 0, 0)),
        ),
        compiler_params=params(),
        cost_estimate=cost(16 * slots * rows * cols * BLOCK, slots * 4 * cols * (rows + BLOCK)),
        name="product",
    )(inner, ints, wide)


def last_kernel(
    rows, cols, occ, virt, win, at, inner,
    ints_ref, t0, t1, s0, s1, old_ref, evirt, eocc_ref, ecol_ref, out_ref, wide_ref, sum_ref,
):
    plane, dev = at[0], at[1]

    @pl.loop(0, WIDE // 256)
    def _(part):
        tile = pl.program_id(0) * (WIDE // 256) + part
        into = wide_ref.at[:, pl.ds(pl.multiple_of(part * 256, 256), 256)]
        widen_tile(rows, cols, tile, occ, virt, win, dev, (t0, t1), (s0, s1), into)

    @pl.loop(0, 2)
    def _(half):
        sum_ref[half, :rows, :] = old_ref[half] + dot(ints_ref[0, half], wide_ref[...])

    i = iota((1, WIDE), 1) + pl.program_id(0) * WIDE
    col_live = ((i & 15) < occ[dev]) & ((i >> 4) < virt[dev ^ win[0]])
    col_energy = ecol_ref[...]
    _, _, starts = pair_scalars(occ, virt, win, plane)
    p = iota((OCC_CAP, 1), 0)
    irreps = [2 * plane, 2 * plane + 1]
    occs = [occ[irrep] for irrep in irreps]
    partners = [irrep ^ win[0] for irrep in irreps]
    virts = [virt[partner] for partner in partners]
    live = [(p < o) & col_live for o in occs]

    @pl.loop(0, VIR_CAP // 4)
    def _(group):
        for h in range(2):
            for i in range(4):
                half_q, s = 2 * group + i // 2, i % 2
                q = 2 * half_q + s
                start = half_q * occs[h]
                if h == 1:
                    start = start + starts[s]
                start = jnp.minimum(start, rows)
                block = sum_ref[s, pl.ds(pl.multiple_of((start >> 3) << 3, 8), OCC_CAP + 8), :]
                block = pltpu.roll(block, OCC_CAP + 8 - (start & 7), 0)[:OCC_CAP]
                denom = (eocc_ref[h] - evirt[partners[h], q]) + col_energy
                value = jnp.where(live[h] & (q < virts[h]), block / denom, 0.0)
                at_row = pl.multiple_of((h * VIR_CAP + q) * OCC_CAP, OCC_CAP)
                out_ref[pl.ds(at_row, OCC_CAP), :] = value


def last(rows, cols, scalars, at, inner, ints, own, sib, acc, energies):
    square = pl.BlockSpec((rows, cols), lambda n, *_: (0, 0))
    return pl.pallas_call(
        functools.partial(last_kernel, rows, cols),
        out_shape=jax.ShapeDtypeStruct((2 * BLOCK, BLOCK), F32),
        grid_spec=pltpu.PrefetchScalarGridSpec(
            num_scalar_prefetch=5,
            grid=(BLOCK // WIDE,),
            in_specs=[
                pl.BlockSpec((1, 2, rows, 2 * cols), lambda n, o, v, w, a, k: (k[0], 0, 0, 0)),
                square, square, square, square,
                pl.BlockSpec((2, rows, WIDE), lambda n, *_: (0, 0, n)),
                pl.BlockSpec(memory_space=pltpu.SMEM),
                pl.BlockSpec((2, OCC_CAP, 1), lambda n, *_: (0, 0, 0)),
                pl.BlockSpec((1, WIDE), lambda n, *_: (0, n)),
            ],
            out_specs=pl.BlockSpec((2 * BLOCK, WIDE), lambda n, *_: (0, n)),
            scratch_shapes=[
                pltpu.VMEM((2 * cols, WIDE), BF16),
                pltpu.VMEM((2, rows + OCC_CAP + 8, WIDE), F32),
            ],
        ),
        compiler_params=params(),
        cost_estimate=cost(16 * rows * cols * BLOCK, 8 * rows * cols + 16 * rows * BLOCK),
        name="last_product",
    )(*scalars, at, inner, ints, *own, *sib, acc, *energies)


def after_kernel(*refs):
    pass


def after(kept, awaited):
    whole = pl.BlockSpec(memory_space=pl.ANY)
    return pl.pallas_call(
        after_kernel,
        out_shape=[jax.ShapeDtypeStruct(x.shape, x.dtype) for x in kept],
        in_specs=[whole] * (len(kept) + len(awaited)),
        out_specs=[whole] * len(kept),
        input_output_aliases={i: i for i in range(len(kept))},
        name="after",
    )(*kept, *awaited)


def ring_order(n):
    return list(range(0, 1)) + list(range(1, n, 2)) + [i for i in range(n - 1, 0, -1) if i % 2 == 0]


def branch(rows, nrow, ncol, t2, ints, occ, virt, win, eps_virt, occ_rows, col_energy, at, sources):
    cols = -(-rows // 128) * 128
    scalars = (occ, virt, win)
    order = ring_order(nrow)
    ring = [(order[i], order[(i + 1) % nrow]) for i in range(nrow)]
    swap = [(c, c ^ 1) for c in range(ncol)]

    def to_sibling(x):
        return lax.ppermute(x, "col", swap)

    def around(x):
        return lax.ppermute(x, "row", ring)

    def exchange(x):
        return lax.all_to_all(x, "col", split_axis=0, concat_axis=0, tiled=True)

    even, odd = prep(cols, scalars, t2)
    even, odd = compact_rows(rows, cols, 0, scalars, at, exchange(even), passed=(odd,))
    mine = ints.reshape(2, VIR_CAP // 2, 2, OCC_CAP, BLOCK)
    other = lax.dynamic_index_in_dim(mine, 1 - (at[1] & 1), 2, keepdims=False).reshape(BLOCK, BLOCK)
    even_next = around(even)
    small = compact_ints(rows, cols, scalars, at, mine, to_sibling(other), even)
    odd, small = compact_rows(rows, cols, 1, scalars, at, exchange(odd), passed=(small,))
    odd, small = after([odd, small], [even_next])
    panel = lax.all_gather(small, "col", axis=0, tiled=False).reshape(ncol // 2, 2, rows, 2 * cols)

    held = [even, odd]
    blocks = []
    for step in range(nrow - 1):
        later = [even_next if step == 0 else around(held[0]), around(held[1])]
        blocks += held + [to_sibling(x) for x in held]
        held = later
    wide = widen(rows, cols, scalars, at, blocks)
    acc = product(rows, cols, sources[: nrow - 1], panel, wide)
    own = after(held, [acc])
    sib = [to_sibling(x) for x in own]
    energies = (eps_virt, occ_rows, col_energy)
    return last(rows, cols, scalars, at, sources[nrow - 1 :], panel, own, sib, acc, energies)


def choose_kernel(occ, virt, win, index_ref):
    index = jnp.int32(len(SIZES) - 1)
    for pair in range(NIRREP // 2):
        (o_a, o_b), (v_a, v_b), _ = pair_scalars(occ, virt, win, pair)
        most = o_a * ((v_a + 1) >> 1) + o_b * ((v_b + 1) >> 1)
        fits = sum((most <= size).astype(I32) for size in SIZES[1:])
        index = jnp.minimum(index, fits)
    index_ref[0] = index


def choose(occ, virt, win):
    smem = pl.BlockSpec(memory_space=pltpu.SMEM)
    return pl.pallas_call(
        choose_kernel,
        out_shape=jax.ShapeDtypeStruct((1,), I32),
        in_specs=[smem] * 3,
        out_specs=smem,
        name="choose",
    )(occ, virt, win)[0]


def live_device(nrow, ncol, t2, ints, eps_occ, eps_virt, occ, virt, win):
    row, col = lax.axis_index("row"), lax.axis_index("col")
    index = choose(occ, virt, win)
    occ_rows = lax.dynamic_slice(eps_occ, (2 * row, 0), (2, OCC_CAP)).reshape(2, OCC_CAP, 1)
    col_occ = lax.dynamic_slice(eps_occ, (col, 0), (1, OCC_CAP))
    col_virt = lax.dynamic_slice(eps_virt, (col ^ win[0], 0), (1, VIR_CAP))
    col_energy = (col_occ[:, None, :] - col_virt[:, :, None]).reshape(1, BLOCK)
    at = jnp.stack([row, col]).astype(I32)
    order = ring_order(nrow)
    table = [[order[(order.index(z) - t) % nrow] for t in range(nrow)] for z in range(nrow)]
    sources = lax.dynamic_slice(jnp.array(table, I32), (row, 0), (1, nrow)).reshape(nrow)
    operands = (t2, ints, occ, virt, win, eps_virt, occ_rows, col_energy, at, sources)
    return lax.switch(index, [functools.partial(branch, size, nrow, ncol) for size in SIZES], *operands)


def ph_vectors(eps_occ, eps_virt, occ_count, virt_count, window_irrep):
    irreps = jnp.arange(NIRREP, dtype=I32)
    partner = jnp.bitwise_xor(irreps, window_irrep[0])
    onehot = partner[:, None] == irreps[None, :]
    virt_rows = jnp.dot(onehot.astype(F32), eps_virt, precision=lax.Precision.HIGHEST)
    virt_live = jnp.sum(jnp.where(onehot, virt_count[None, :], 0), axis=1)
    energy = eps_occ[:, None, :] - virt_rows[:, :, None]
    slots_occ = jnp.arange(OCC_CAP, dtype=I32)
    slots_virt = jnp.arange(VIR_CAP, dtype=I32)
    live = (slots_occ[None, None, :] < occ_count[:, None, None]) & (
        slots_virt[None, :, None] < virt_live[:, None, None]
    )
    return (energy, live)


def any_device(t2_pairs, cycle_ints, eps_occ, eps_virt, occ_count, virt_count, window_irrep):
    irrep_local = t2_pairs.shape[0]
    virt_local = t2_pairs.shape[4]
    total = NIRREP * VIR_CAP * OCC_CAP
    energy, live = ph_vectors(eps_occ, eps_virt, occ_count, virt_count, window_irrep)
    row_index = lax.axis_index("row")
    col_index = lax.axis_index("col")
    zero_index = jnp.int32(0)
    source_live = lax.dynamic_slice(
        live,
        (row_index * irrep_local, col_index * virt_local, zero_index),
        (irrep_local, virt_local, OCC_CAP),
    )
    full_live = live.reshape(-1)
    ordered = jnp.transpose(t2_pairs, (0, 4, 2, 1, 5, 3)).reshape(
        irrep_local, virt_local, OCC_CAP, total
    )
    keep = source_live[:, :, :, None] & full_live[None, None, None, :]
    ordered = jnp.where(keep, ordered, jnp.zeros_like(ordered))
    moved = lax.all_to_all(ordered, "col", split_axis=3, concat_axis=1, tiled=True)
    amp_local = moved.reshape(irrep_local * VIR_CAP * OCC_CAP, moved.shape[3])
    amp_panel = lax.all_gather(amp_local, "row", axis=0, tiled=True)
    ints_panel = lax.all_gather(cycle_ints, "col", axis=1, tiled=True)
    cycle = jnp.dot(ints_panel, amp_panel, preferred_element_type=F32)
    rows_here, cols_here = cycle.shape
    flat_energy = energy.reshape(-1)
    row_start, col_start = row_index * rows_here, col_index * cols_here
    row_energy = lax.dynamic_slice_in_dim(flat_energy, row_start, rows_here, 0)
    col_energy = lax.dynamic_slice_in_dim(flat_energy, col_start, cols_here, 0)
    row_live = lax.dynamic_slice_in_dim(full_live, row_start, rows_here, 0)
    col_live = lax.dynamic_slice_in_dim(full_live, col_start, cols_here, 0)
    denom = row_energy[:, None] + col_energy[None, :]
    return jnp.where(row_live[:, None] & col_live[None, :], cycle / denom, F32(0.0))


def solution(mesh):
    nrow, ncol = mesh.shape["row"], mesh.shape["col"]
    placed = (P("row", None, None, None, "col", None), P("row", "col"), P(), P(), P(), P(), P())
    body = any_device
    if 2 * nrow == NIRREP and ncol == NIRREP:
        body = functools.partial(live_device, nrow, ncol)
    return jax.shard_map(body, mesh=mesh, in_specs=placed, out_specs=P("row", "col"), check_vma=False)
```

```python
import functools

import jax
import jax.numpy as jnp
from jax import lax
from jax.experimental import pallas as pl
from jax.experimental.pallas import tpu as pltpu
from jax.sharding import PartitionSpec as P

NIRREP = 8
OCC_CAP = 16
VIR_CAP = 64
BLOCK = VIR_CAP * OCC_CAP
SIZES = (1024, 896, 768, 640)
WIDE = 512
F32 = jnp.float32
BF16 = jnp.bfloat16
I32 = jnp.int32
I16 = jnp.int16
VMEM_BYTES = 56 * 1024 * 1024


def iota(shape, dim):
    return lax.broadcasted_iota(I32, shape, dim)


def params():
    return pltpu.CompilerParams(vmem_limit_bytes=VMEM_BYTES)


def cost(flops, nbytes):
    return pl.CostEstimate(flops=flops, bytes_accessed=nbytes, transcendentals=0)


def pair_scalars(occ, virt, win, pair):
    first = 2 * pair
    o_a, o_b = occ[first], occ[first + 1]
    v_a, v_b = virt[first ^ win[0]], virt[(first + 1) ^ win[0]]
    return (o_a, o_b), (v_a, v_b), (o_a * ((v_a + 1) >> 1), o_a * (v_a >> 1))


def place(q, p, second, counts):
    (o_a, o_b), (v_a, v_b), (start_even, start_odd) = counts
    o = jnp.where(second, o_b, o_a)
    v = jnp.where(second, v_b, v_a)
    start = jnp.where(second, jnp.where((q & 1) == 0, start_even, start_odd), 0)
    return jnp.where((p < o) & (q < v), start + (q >> 1) * o + p, -1)


def one_hot(left, right):
    return jnp.where(left.astype(I16) == right.astype(I16), BF16(1.0), BF16(0.0))


def dot(a, b):
    return jnp.dot(a, b, preferred_element_type=F32)


def prep_kernel(size, occ, virt, win, t2_ref, even_ref, odd_ref, x_ref):
    counts = pair_scalars(occ, virt, win, pl.program_id(0))
    row = iota((256, 1), 0)
    source = (((row >> 6) & 1) << 7) | (((row >> 2) & 15) << 3) | ((row & 3) << 1) | (row >> 7)
    by_parity = one_hot(iota((256, 256), 1), source)
    targets = []
    for half in range(2):
        for group in range(4):
            parts = [
                t2_ref[:, half, :, 4 * group + i].astype(F32).reshape(256, VIR_CAP) for i in range(4)
            ]
            x = jnp.concatenate(parts, axis=1).astype(BF16)
            at = (4 * half + group) * 256
            x_ref[:, at : at + 256] = dot(by_parity, x).astype(BF16)
            r = iota((256, 1), 0)
            p, q = 4 * group + (r >> 6), r & 63
            spot = place(q, p, half == 1, counts)
            targets.append(jnp.where(spot >= 0, spot + (q & 1) * size, -1))
    @pl.loop(0, 2)
    def _(core):
        for tile in range(-(-size // 256)):
            col = min(256 * tile, size - 256)
            lane = iota((256, 256), 1) + (col + core * size)
            acc = jnp.zeros((256, 256), F32)
            for chunk in range(4 if col >= BLOCK // 2 else 0, 8):
                acc += dot(x_ref[:, chunk * 256 : chunk * 256 + 256], one_hot(targets[chunk], lane))
            acc = acc.astype(BF16)
            even_ref[core, :, col : col + 256] = acc[:128]
            odd_ref[core, :, col : col + 256] = acc[128:]


def prep(size, scalars, t2):
    shape = jax.ShapeDtypeStruct((NIRREP, 128, size), BF16)
    block = pl.BlockSpec((2, 128, size), lambda k, *_: (k, 0, 0))
    return pl.pallas_call(
        functools.partial(prep_kernel, size),
        out_shape=(shape, shape),
        grid_spec=pltpu.PrefetchScalarGridSpec(
            num_scalar_prefetch=3,
            grid=(NIRREP // 2,),
            in_specs=[
                pl.BlockSpec((2, 2, OCC_CAP, OCC_CAP, 8, VIR_CAP), lambda k, *_: (0, k, 0, 0, 0, 0))
            ],
            out_specs=[block, block],
            scratch_shapes=[pltpu.VMEM((256, 2048), BF16)],
        ),
        compiler_params=params(),
        cost_estimate=cost(2 * 4 * 256 * 2048 * 2 * size, 12 * 2**20),
        name="prep_amplitudes",
    )(*scalars, t2)


def fill_rows(rows, spot, sel_ref):
    @pl.loop(0, rows // 128)
    def _(n):
        first = pl.multiple_of(n * 128, 128)
        sel_ref[pl.ds(first, 128), :] = one_hot(iota((128, BLOCK), 0) + first, spot)


def rows_kernel(rows, parity, count, occ, virt, win, at, x_ref, *refs):
    out_ref, sel_ref = refs[count], refs[-1]
    counts = pair_scalars(occ, virt, win, at[0])
    i = iota((1, BLOCK), 1)
    q = 8 * (i >> 7) + 2 * (i & 3) + parity
    spot = place(q, (i >> 2) & 15, ((i >> 6) & 1) == 1, counts)
    fill_rows(rows, spot, sel_ref)
    cols = out_ref.shape[1]

    @pl.loop(0, -(-cols // 256))
    def _(n):
        lanes = pl.ds(pl.multiple_of(jnp.minimum(n * 256, cols - 256), 128), 256)
        x = x_ref[:, :, lanes].reshape(BLOCK, 256)

        @pl.loop(0, 2)
        def _(half):
            at_rows = pl.ds(pl.multiple_of(half * (rows // 2), 64), rows // 2)
            out_ref[at_rows, lanes] = dot(sel_ref[at_rows, :], x).astype(BF16)


def compact_rows(rows, cols, parity, scalars, at, x, passed=(), awaited=()):
    whole = pl.BlockSpec(memory_space=pl.ANY)
    return pl.pallas_call(
        functools.partial(rows_kernel, rows, parity, len(passed) + len(awaited)),
        out_shape=[jax.ShapeDtypeStruct((rows, cols), BF16)]
        + [jax.ShapeDtypeStruct(y.shape, y.dtype) for y in passed],
        grid_spec=pltpu.PrefetchScalarGridSpec(
            num_scalar_prefetch=4,
            grid=(1,),
            in_specs=[pl.BlockSpec((NIRREP, 128, cols), lambda n, *_: (0, 0, 0))]
            + [whole] * (len(passed) + len(awaited)),
            out_specs=[pl.BlockSpec((rows, cols), lambda n, *_: (0, 0))] + [whole] * len(passed),
            scratch_shapes=[pltpu.VMEM((rows, BLOCK), BF16)],
        ),
        input_output_aliases={5 + i: 1 + i for i in range(len(passed))},
        compiler_params=params(),
        cost_estimate=cost(4 * rows * BLOCK * cols, 4 * rows * BLOCK),
        name="compact_rows",
    )(*scalars, at, x, *passed, *awaited)


def ints_kernel(rows, cols, occ, virt, win, at, mine_ref, other_ref, awaited, out_ref, sel_ref, cols_ref):
    plane, dev = at[0], at[1]
    parity = dev & 1

    @pl.when(pl.program_id(0) == 0)
    def _():
        counts = pair_scalars(occ, virt, win, plane)
        i = iota((1, BLOCK), 1)
        q = 2 * ((i >> 4) & 31) + parity
        spot = place(q, i & 15, (i >> 9) == 1, counts)
        fill_rows(rows, spot, sel_ref)

    counts = pair_scalars(occ, virt, win, dev >> 1)
    i = iota((BLOCK, 1), 0)
    q, p = i >> 4, i & 15
    lane = iota((BLOCK, 256), 1) + pl.program_id(0) * 256
    picks = []
    for second in (parity == 1, parity == 0):
        spot = place(q, p, second, counts)
        picks.append(one_hot(jnp.where(spot >= 0, spot + (q & 1) * cols, -1), lane))

    @pl.loop(0, 2)
    def _(half):
        at_rows = pl.ds(pl.multiple_of(half * (BLOCK // 2), BLOCK // 2), BLOCK // 2)
        acc = dot(mine_ref[half].reshape(BLOCK // 2, BLOCK), picks[0])
        acc += dot(other_ref[at_rows, :], picks[1])
        cols_ref[at_rows, :] = acc.astype(BF16)

    out_ref[...] = dot(sel_ref[...], cols_ref[...]).astype(BF16)


def compact_ints(rows, cols, scalars, at, mine, other, awaited):
    mine_spec = pl.BlockSpec(
        (2, VIR_CAP // 2, 1, OCC_CAP, BLOCK), lambda n, o, v, w, a: (0, 0, a[1] & 1, 0, 0)
    )
    whole = pl.BlockSpec((BLOCK, BLOCK), lambda n, *_: (0, 0))
    return pl.pallas_call(
        functools.partial(ints_kernel, rows, cols),
        out_shape=jax.ShapeDtypeStruct((rows, 2 * cols), BF16),
        grid_spec=pltpu.PrefetchScalarGridSpec(
            num_scalar_prefetch=4,
            grid=(2 * cols // 256,),
            in_specs=[mine_spec, whole, pl.BlockSpec(memory_space=pl.ANY)],
            out_specs=pl.BlockSpec((rows, 256), lambda n, *_: (0, n)),
            scratch_shapes=[pltpu.VMEM((rows, BLOCK), BF16), pltpu.VMEM((BLOCK, 256), BF16)],
        ),
        compiler_params=params(),
        cost_estimate=cost(16 * BLOCK * BLOCK * cols, 4 * BLOCK * BLOCK + 4 * rows * cols),
        name="compact_ints",
    )(*scalars, at, mine, other, awaited)


def widen_tile(rows, cols, tile, occ, virt, win, dev, own_refs, sib_refs, wide_ref):
    parity = dev & 1
    counts = pair_scalars(occ, virt, win, dev >> 1)
    (o_a, o_b), _, (start_even, start_odd) = counts
    second = parity == 1
    o = jnp.where(second, o_b, o_a)
    i = iota((1, 256), 1) + tile * 256
    q = i >> 4
    spot = place(q, i & 15, second, counts)
    r = iota((256, 256), 0)
    picks = []
    for s in (parity, 1 - parity):
        start = jnp.where(second, jnp.where(s == 0, start_even, start_odd), 0) + 8 * tile * o
        start = jnp.minimum((start >> 7) << 7, cols - 256)
        window = pl.ds(pl.multiple_of(start, 128), 256)
        picks.append((window, one_hot(r + start, jnp.where((q & 1) == s, spot, -1))))
    for piece in range(2):

        @pl.loop(0, 2)
        def _(half):
            first = pl.multiple_of(half * (rows // 2), 64)
            at_rows = pl.ds(first, rows // 2)
            x = dot(own_refs[piece][at_rows, picks[0][0]], picks[0][1])
            x += dot(sib_refs[piece][at_rows, picks[1][0]], picks[1][1])
            into = pl.ds(pl.multiple_of(piece * cols + first, 64), rows // 2)
            wide_ref[into, :] = x.astype(BF16)

        if rows < cols:
            wide_ref[piece * cols + rows : (piece + 1) * cols, :] = jnp.zeros((cols - rows, 256), BF16)


def widen_kernel(rows, cols, slots, occ, virt, win, at, *refs):
    wide_ref = refs[-1]
    for slot in range(slots):

        @pl.when(pl.program_id(0) == slot)
        def _():
            t0, t1, s0, s1 = refs[4 * slot : 4 * slot + 4]
            tile = pl.program_id(1)
            widen_tile(rows, cols, tile, occ, virt, win, at[1], (t0, t1), (s0, s1), wide_ref.at[0])


def widen(rows, cols, scalars, at, blocks):
    slots = len(blocks) // 4
    square = pl.BlockSpec((rows, cols), lambda t, n, *_: (0, 0), pipeline_mode=pl.Buffered(1))
    return pl.pallas_call(
        functools.partial(widen_kernel, rows, cols, slots),
        out_shape=jax.ShapeDtypeStruct((slots, 2 * cols, BLOCK), BF16),
        grid_spec=pltpu.PrefetchScalarGridSpec(
            num_scalar_prefetch=4,
            grid=(slots, BLOCK // 256),
            in_specs=[square] * len(blocks),
            out_specs=pl.BlockSpec((1, 2 * cols, 256), lambda t, n, *_: (t, 0, n)),
        ),
        compiler_params=params(),
        cost_estimate=cost(slots * 8 * rows * 512 * BLOCK, slots * (8 * rows * cols + 4 * cols * BLOCK)),
        name="widen",
    )(*scalars, at, *blocks)


def product_kernel(inner, ints_ref, wide_ref, acc_ref):
    at = pl.ds(pl.multiple_of(pl.program_id(1) * WIDE, WIDE), WIDE)

    @pl.when(pl.program_id(0) == 0)
    def _():
        acc_ref[:, :, at] = jnp.zeros((2, acc_ref.shape[1], WIDE), F32)

    rows = acc_ref.shape[1]

    @pl.loop(0, 4)
    def _(quarter):
        at_rows = pl.ds(pl.multiple_of((quarter & 1) * (rows // 2), 64), rows // 2)
        acc_ref[quarter >> 1, at_rows, at] += dot(ints_ref[0, quarter >> 1, at_rows, :], wide_ref[0])


def product(rows, cols, inner, ints, wide):
    slots = wide.shape[0]
    return pl.pallas_call(
        product_kernel,
        out_shape=jax.ShapeDtypeStruct((2, rows, BLOCK), F32),
        grid_spec=pltpu.PrefetchScalarGridSpec(
            num_scalar_prefetch=1,
            grid=(slots, BLOCK // WIDE),
            in_specs=[
                pl.BlockSpec((1, 2, rows, 2 * cols), lambda t, n, k: (k[t], 0, 0, 0)),
                pl.BlockSpec((1, 2 * cols, WIDE), lambda t, n, k: (t, 0, n)),
            ],
            out_specs=pl.BlockSpec((2, rows, BLOCK), lambda t, n, k: (0, 0, 0)),
        ),
        compiler_params=params(),
        cost_estimate=cost(16 * slots * rows * cols * BLOCK, slots * 4 * cols * (rows + BLOCK)),
        name="product",
    )(inner, ints, wide)


def last_kernel(
    rows, cols, occ, virt, win, at, inner,
    ints_ref, t0, t1, s0, s1, old_ref, evirt, eocc_ref, ecol_ref, out_ref, wide_ref, sum_ref,
):
    plane, dev = at[0], at[1]

    @pl.loop(0, WIDE // 256)
    def _(part):
        tile = pl.program_id(0) * (WIDE // 256) + part
        into = wide_ref.at[:, pl.ds(pl.multiple_of(part * 256, 256), 256)]
        widen_tile(rows, cols, tile, occ, virt, win, dev, (t0, t1), (s0, s1), into)

    @pl.loop(0, 2)
    def _(half):
        sum_ref[half, :rows, :] = old_ref[half] + dot(ints_ref[0, half], wide_ref[...])

    i = iota((1, WIDE), 1) + pl.program_id(0) * WIDE
    col_live = ((i & 15) < occ[dev]) & ((i >> 4) < virt[dev ^ win[0]])
    col_energy = ecol_ref[...]
    _, _, starts = pair_scalars(occ, virt, win, plane)
    p = iota((OCC_CAP, 1), 0)
    irreps = [2 * plane, 2 * plane + 1]
    occs = [occ[irrep] for irrep in irreps]
    partners = [irrep ^ win[0] for irrep in irreps]
    virts = [virt[partner] for partner in partners]
    live = [(p < o) & col_live for o in occs]

    @pl.loop(0, VIR_CAP // 8)
    def _(group):
        for h in range(2):
            for i in range(8):
                half_q, s = 4 * group + i // 2, i % 2
                q = 2 * half_q + s
                start = half_q * occs[h]
                if h == 1:
                    start = start + starts[s]
                start = jnp.minimum(start, rows)
                block = sum_ref[s, pl.ds(pl.multiple_of((start >> 3) << 3, 8), OCC_CAP + 8), :]
                block = pltpu.roll(block, OCC_CAP + 8 - (start & 7), 0)[:OCC_CAP]
                denom = (eocc_ref[h] - evirt[partners[h], q]) + col_energy
                value = jnp.where(live[h] & (q < virts[h]), block / denom, 0.0)
                at_row = pl.multiple_of((h * VIR_CAP + q) * OCC_CAP, OCC_CAP)
                out_ref[pl.ds(at_row, OCC_CAP), :] = value


def last(rows, cols, scalars, at, inner, ints, own, sib, acc, energies):
    square = pl.BlockSpec((rows, cols), lambda n, *_: (0, 0))
    return pl.pallas_call(
        functools.partial(last_kernel, rows, cols),
        out_shape=jax.ShapeDtypeStruct((2 * BLOCK, BLOCK), F32),
        grid_spec=pltpu.PrefetchScalarGridSpec(
            num_scalar_prefetch=5,
            grid=(BLOCK // WIDE,),
            in_specs=[
                pl.BlockSpec((1, 2, rows, 2 * cols), lambda n, o, v, w, a, k: (k[0], 0, 0, 0)),
                square, square, square, square,
                pl.BlockSpec((2, rows, WIDE), lambda n, *_: (0, 0, n)),
                pl.BlockSpec(memory_space=pltpu.SMEM),
                pl.BlockSpec((2, OCC_CAP, 1), lambda n, *_: (0, 0, 0)),
                pl.BlockSpec((1, WIDE), lambda n, *_: (0, n)),
            ],
            out_specs=pl.BlockSpec((2 * BLOCK, WIDE), lambda n, *_: (0, n)),
            scratch_shapes=[
                pltpu.VMEM((2 * cols, WIDE), BF16),
                pltpu.VMEM((2, rows + OCC_CAP + 8, WIDE), F32),
            ],
        ),
        compiler_params=params(),
        cost_estimate=cost(16 * rows * cols * BLOCK, 8 * rows * cols + 16 * rows * BLOCK),
        name="last_product",
    )(*scalars, at, inner, ints, *own, *sib, acc, *energies)


def after_kernel(*refs):
    pass


def after(kept, awaited):
    whole = pl.BlockSpec(memory_space=pl.ANY)
    return pl.pallas_call(
        after_kernel,
        out_shape=[jax.ShapeDtypeStruct(x.shape, x.dtype) for x in kept],
        in_specs=[whole] * (len(kept) + len(awaited)),
        out_specs=[whole] * len(kept),
        input_output_aliases={i: i for i in range(len(kept))},
        name="after",
    )(*kept, *awaited)


def ring_order(n):
    return list(range(0, 1)) + list(range(1, n, 2)) + [i for i in range(n - 1, 0, -1) if i % 2 == 0]


def branch(rows, nrow, ncol, t2, ints, occ, virt, win, eps_virt, occ_rows, col_energy, at, sources):
    cols = -(-rows // 128) * 128
    scalars = (occ, virt, win)
    order = ring_order(nrow)
    ring = [(order[i], order[(i + 1) % nrow]) for i in range(nrow)]
    swap = [(c, c ^ 1) for c in range(ncol)]

    def to_sibling(x):
        return lax.ppermute(x, "col", swap)

    def around(x):
        return lax.ppermute(x, "row", ring)

    def exchange(x):
        return lax.all_to_all(x, "col", split_axis=0, concat_axis=0, tiled=True)

    even, odd = prep(cols, scalars, t2)
    even, odd = compact_rows(rows, cols, 0, scalars, at, exchange(even), passed=(odd,))
    mine = ints.reshape(2, VIR_CAP // 2, 2, OCC_CAP, BLOCK)
    other = lax.dynamic_index_in_dim(mine, 1 - (at[1] & 1), 2, keepdims=False).reshape(BLOCK, BLOCK)
    even_next = around(even)
    small = compact_ints(rows, cols, scalars, at, mine, to_sibling(other), even)
    odd, small = compact_rows(rows, cols, 1, scalars, at, exchange(odd), passed=(small,))
    (small,) = after([small], [even_next])
    panel = lax.all_gather(small, "col", axis=0, tiled=False).reshape(ncol // 2, 2, rows, 2 * cols)

    held = [even, odd]
    blocks = []
    for step in range(nrow - 1):
        later = [even_next if step == 0 else around(held[0]), around(held[1])]
        blocks += held + [to_sibling(x) for x in held]
        held = later
    wide = widen(rows, cols, scalars, at, blocks)
    acc = product(rows, cols, sources[: nrow - 1], panel, wide)
    own = after(held, [acc])
    sib = [to_sibling(x) for x in own]
    energies = (eps_virt, occ_rows, col_energy)
    return last(rows, cols, scalars, at, sources[nrow - 1 :], panel, own, sib, acc, energies)


def choose_kernel(occ, virt, win, index_ref):
    index = jnp.int32(len(SIZES) - 1)
    for pair in range(NIRREP // 2):
        (o_a, o_b), (v_a, v_b), _ = pair_scalars(occ, virt, win, pair)
        most = o_a * ((v_a + 1) >> 1) + o_b * ((v_b + 1) >> 1)
        fits = sum((most <= size).astype(I32) for size in SIZES[1:])
        index = jnp.minimum(index, fits)
    index_ref[0] = index


def choose(occ, virt, win):
    smem = pl.BlockSpec(memory_space=pltpu.SMEM)
    return pl.pallas_call(
        choose_kernel,
        out_shape=jax.ShapeDtypeStruct((1,), I32),
        in_specs=[smem] * 3,
        out_specs=smem,
        name="choose",
    )(occ, virt, win)[0]


def live_device(nrow, ncol, t2, ints, eps_occ, eps_virt, occ, virt, win):
    row, col = lax.axis_index("row"), lax.axis_index("col")
    index = choose(occ, virt, win)
    occ_rows = lax.dynamic_slice(eps_occ, (2 * row, 0), (2, OCC_CAP)).reshape(2, OCC_CAP, 1)
    col_occ = lax.dynamic_slice(eps_occ, (col, 0), (1, OCC_CAP))
    col_virt = lax.dynamic_slice(eps_virt, (col ^ win[0], 0), (1, VIR_CAP))
    col_energy = (col_occ[:, None, :] - col_virt[:, :, None]).reshape(1, BLOCK)
    at = jnp.stack([row, col]).astype(I32)
    order = ring_order(nrow)
    table = [[order[(order.index(z) - t) % nrow] for t in range(nrow)] for z in range(nrow)]
    sources = lax.dynamic_slice(jnp.array(table, I32), (row, 0), (1, nrow)).reshape(nrow)
    operands = (t2, ints, occ, virt, win, eps_virt, occ_rows, col_energy, at, sources)
    return lax.switch(index, [functools.partial(branch, size, nrow, ncol) for size in SIZES], *operands)


def ph_vectors(eps_occ, eps_virt, occ_count, virt_count, window_irrep):
    irreps = jnp.arange(NIRREP, dtype=I32)
    partner = jnp.bitwise_xor(irreps, window_irrep[0])
    onehot = partner[:, None] == irreps[None, :]
    virt_rows = jnp.dot(onehot.astype(F32), eps_virt, precision=lax.Precision.HIGHEST)
    virt_live = jnp.sum(jnp.where(onehot, virt_count[None, :], 0), axis=1)
    energy = eps_occ[:, None, :] - virt_rows[:, :, None]
    slots_occ = jnp.arange(OCC_CAP, dtype=I32)
    slots_virt = jnp.arange(VIR_CAP, dtype=I32)
    live = (slots_occ[None, None, :] < occ_count[:, None, None]) & (
        slots_virt[None, :, None] < virt_live[:, None, None]
    )
    return (energy, live)


def any_device(t2_pairs, cycle_ints, eps_occ, eps_virt, occ_count, virt_count, window_irrep):
    irrep_local = t2_pairs.shape[0]
    virt_local = t2_pairs.shape[4]
    total = NIRREP * VIR_CAP * OCC_CAP
    energy, live = ph_vectors(eps_occ, eps_virt, occ_count, virt_count, window_irrep)
    row_index = lax.axis_index("row")
    col_index = lax.axis_index("col")
    zero_index = jnp.int32(0)
    source_live = lax.dynamic_slice(
        live,
        (row_index * irrep_local, col_index * virt_local, zero_index),
        (irrep_local, virt_local, OCC_CAP),
    )
    full_live = live.reshape(-1)
    ordered = jnp.transpose(t2_pairs, (0, 4, 2, 1, 5, 3)).reshape(
        irrep_local, virt_local, OCC_CAP, total
    )
    keep = source_live[:, :, :, None] & full_live[None, None, None, :]
    ordered = jnp.where(keep, ordered, jnp.zeros_like(ordered))
    moved = lax.all_to_all(ordered, "col", split_axis=3, concat_axis=1, tiled=True)
    amp_local = moved.reshape(irrep_local * VIR_CAP * OCC_CAP, moved.shape[3])
    amp_panel = lax.all_gather(amp_local, "row", axis=0, tiled=True)
    ints_panel = lax.all_gather(cycle_ints, "col", axis=1, tiled=True)
    cycle = jnp.dot(ints_panel, amp_panel, preferred_element_type=F32)
    rows_here, cols_here = cycle.shape
    flat_energy = energy.reshape(-1)
    row_start, col_start = row_index * rows_here, col_index * cols_here
    row_energy = lax.dynamic_slice_in_dim(flat_energy, row_start, rows_here, 0)
    col_energy = lax.dynamic_slice_in_dim(flat_energy, col_start, cols_here, 0)
    row_live = lax.dynamic_slice_in_dim(full_live, row_start, rows_here, 0)
    col_live = lax.dynamic_slice_in_dim(full_live, col_start, cols_here, 0)
    denom = row_energy[:, None] + col_energy[None, :]
    return jnp.where(row_live[:, None] & col_live[None, :], cycle / denom, F32(0.0))


def solution(mesh):
    nrow, ncol = mesh.shape["row"], mesh.shape["col"]
    placed = (P("row", None, None, None, "col", None), P("row", "col"), P(), P(), P(), P(), P())
    body = any_device
    if 2 * nrow == NIRREP and ncol == NIRREP:
        body = functools.partial(live_device, nrow, ncol)
    return jax.shard_map(body, mesh=mesh, in_specs=placed, out_specs=P("row", "col"), check_vma=False)
```

```python
import functools

import jax
import jax.numpy as jnp
from jax import lax
from jax.experimental import pallas as pl
from jax.experimental.pallas import tpu as pltpu
from jax.sharding import PartitionSpec as P

NIRREP = 8
OCC_CAP = 16
VIR_CAP = 64
BLOCK = VIR_CAP * OCC_CAP
SIZES = (1024, 896, 768, 640)
WIDE = 512
F32 = jnp.float32
BF16 = jnp.bfloat16
I32 = jnp.int32
I16 = jnp.int16
VMEM_BYTES = 56 * 1024 * 1024


def iota(shape, dim):
    return lax.broadcasted_iota(I32, shape, dim)


def params():
    return pltpu.CompilerParams(vmem_limit_bytes=VMEM_BYTES)


def cost(flops, nbytes):
    return pl.CostEstimate(flops=flops, bytes_accessed=nbytes, transcendentals=0)


def pair_scalars(occ, virt, win, pair):
    first = 2 * pair
    o_a, o_b = occ[first], occ[first + 1]
    v_a, v_b = virt[first ^ win[0]], virt[(first + 1) ^ win[0]]
    return (o_a, o_b), (v_a, v_b), (o_a * ((v_a + 1) >> 1), o_a * (v_a >> 1))


def place(q, p, second, counts):
    (o_a, o_b), (v_a, v_b), (start_even, start_odd) = counts
    o = jnp.where(second, o_b, o_a)
    v = jnp.where(second, v_b, v_a)
    start = jnp.where(second, jnp.where((q & 1) == 0, start_even, start_odd), 0)
    return jnp.where((p < o) & (q < v), start + (q >> 1) * o + p, -1)


def one_hot(left, right):
    return jnp.where(left.astype(I16) == right.astype(I16), BF16(1.0), BF16(0.0))


def dot(a, b):
    return jnp.dot(a, b, preferred_element_type=F32)


def prep_kernel(size, occ, virt, win, t2_ref, even_ref, odd_ref, x_ref):
    counts = pair_scalars(occ, virt, win, pl.program_id(0))
    row = iota((256, 1), 0)
    source = (((row >> 6) & 1) << 7) | (((row >> 2) & 15) << 3) | ((row & 3) << 1) | (row >> 7)
    by_parity = one_hot(iota((256, 256), 1), source)
    targets = []
    for half in range(2):
        for group in range(4):
            parts = [
                t2_ref[:, half, :, 4 * group + i].astype(F32).reshape(256, VIR_CAP) for i in range(4)
            ]
            x = jnp.concatenate(parts, axis=1).astype(BF16)
            at = (4 * half + group) * 256
            x_ref[:, at : at + 256] = dot(by_parity, x).astype(BF16)
            r = iota((256, 1), 0)
            p, q = 4 * group + (r >> 6), r & 63
            spot = place(q, p, half == 1, counts)
            targets.append(jnp.where(spot >= 0, spot + (q & 1) * size, -1))
    @pl.loop(0, 2)
    def _(core):
        for tile in range(-(-size // 256)):
            col = min(256 * tile, size - 256)
            lane = iota((256, 256), 1) + (col + core * size)
            acc = jnp.zeros((256, 256), F32)
            for chunk in range(4 if col >= BLOCK // 2 else 0, 8):
                acc += dot(x_ref[:, chunk * 256 : chunk * 256 + 256], one_hot(targets[chunk], lane))
            acc = acc.astype(BF16)
            even_ref[core, :, col : col + 256] = acc[:128]
            odd_ref[core, :, col : col + 256] = acc[128:]


def prep(size, scalars, t2):
    shape = jax.ShapeDtypeStruct((NIRREP, 128, size), BF16)
    block = pl.BlockSpec((2, 128, size), lambda k, *_: (k, 0, 0))
    return pl.pallas_call(
        functools.partial(prep_kernel, size),
        out_shape=(shape, shape),
        grid_spec=pltpu.PrefetchScalarGridSpec(
            num_scalar_prefetch=3,
            grid=(NIRREP // 2,),
            in_specs=[
                pl.BlockSpec((2, 2, OCC_CAP, OCC_CAP, 8, VIR_CAP), lambda k, *_: (0, k, 0, 0, 0, 0))
            ],
            out_specs=[block, block],
            scratch_shapes=[pltpu.VMEM((256, 2048), BF16)],
        ),
        compiler_params=params(),
        cost_estimate=cost(2 * 4 * 256 * 2048 * 2 * size, 12 * 2**20),
        name="prep_amplitudes",
    )(*scalars, t2)


def fill_rows(rows, spot, sel_ref):
    @pl.loop(0, rows // 128)
    def _(n):
        first = pl.multiple_of(n * 128, 128)
        sel_ref[pl.ds(first, 128), :] = one_hot(iota((128, BLOCK), 0) + first, spot)


def rows_kernel(rows, parity, count, occ, virt, win, at, x_ref, *refs):
    out_ref, sel_ref = refs[count], refs[-1]
    counts = pair_scalars(occ, virt, win, at[0])
    i = iota((1, BLOCK), 1)
    q = 8 * (i >> 7) + 2 * (i & 3) + parity
    spot = place(q, (i >> 2) & 15, ((i >> 6) & 1) == 1, counts)
    fill_rows(rows, spot, sel_ref)
    cols = out_ref.shape[1]

    @pl.loop(0, -(-cols // 256))
    def _(n):
        lanes = pl.ds(pl.multiple_of(jnp.minimum(n * 256, cols - 256), 128), 256)
        out_ref[:, lanes] = dot(sel_ref[...], x_ref[:, :, lanes].reshape(BLOCK, 256)).astype(BF16)


def compact_rows(rows, cols, parity, scalars, at, x, passed=(), awaited=()):
    whole = pl.BlockSpec(memory_space=pl.ANY)
    return pl.pallas_call(
        functools.partial(rows_kernel, rows, parity, len(passed) + len(awaited)),
        out_shape=[jax.ShapeDtypeStruct((rows, cols), BF16)]
        + [jax.ShapeDtypeStruct(y.shape, y.dtype) for y in passed],
        grid_spec=pltpu.PrefetchScalarGridSpec(
            num_scalar_prefetch=4,
            grid=(1,),
            in_specs=[pl.BlockSpec((NIRREP, 128, cols), lambda n, *_: (0, 0, 0))]
            + [whole] * (len(passed) + len(awaited)),
            out_specs=[pl.BlockSpec((rows, cols), lambda n, *_: (0, 0))] + [whole] * len(passed),
            scratch_shapes=[pltpu.VMEM((rows, BLOCK), BF16)],
        ),
        input_output_aliases={5 + i: 1 + i for i in range(len(passed))},
        compiler_params=params(),
        cost_estimate=cost(4 * rows * BLOCK * cols, 4 * rows * BLOCK),
        name="compact_rows",
    )(*scalars, at, x, *passed, *awaited)


def ints_kernel(rows, cols, occ, virt, win, at, mine_ref, other_ref, awaited, out_ref, sel_ref, cols_ref):
    plane, dev = at[0], at[1]
    parity = dev & 1

    @pl.when(pl.program_id(0) == 0)
    def _():
        counts = pair_scalars(occ, virt, win, plane)
        i = iota((1, BLOCK), 1)
        q = 2 * ((i >> 4) & 31) + parity
        spot = place(q, i & 15, (i >> 9) == 1, counts)
        fill_rows(rows, spot, sel_ref)

    counts = pair_scalars(occ, virt, win, dev >> 1)
    i = iota((BLOCK, 1), 0)
    q, p = i >> 4, i & 15
    lane = iota((BLOCK, 256), 1) + pl.program_id(0) * 256
    picks = []
    for second in (parity == 1, parity == 0):
        spot = place(q, p, second, counts)
        picks.append(one_hot(jnp.where(spot >= 0, spot + (q & 1) * cols, -1), lane))

    @pl.loop(0, 2)
    def _(half):
        at_rows = pl.ds(pl.multiple_of(half * (BLOCK // 2), BLOCK // 2), BLOCK // 2)
        acc = dot(mine_ref[half].reshape(BLOCK // 2, BLOCK), picks[0])
        acc += dot(other_ref[at_rows, :], picks[1])
        cols_ref[at_rows, :] = acc.astype(BF16)

    out_ref[...] = dot(sel_ref[...], cols_ref[...]).astype(BF16)


def compact_ints(rows, cols, scalars, at, mine, other, awaited):
    mine_spec = pl.BlockSpec(
        (2, VIR_CAP // 2, 1, OCC_CAP, BLOCK), lambda n, o, v, w, a: (0, 0, a[1] & 1, 0, 0)
    )
    whole = pl.BlockSpec((BLOCK, BLOCK), lambda n, *_: (0, 0))
    return pl.pallas_call(
        functools.partial(ints_kernel, rows, cols),
        out_shape=jax.ShapeDtypeStruct((rows, 2 * cols), BF16),
        grid_spec=pltpu.PrefetchScalarGridSpec(
            num_scalar_prefetch=4,
            grid=(2 * cols // 256,),
            in_specs=[mine_spec, whole, pl.BlockSpec(memory_space=pl.ANY)],
            out_specs=pl.BlockSpec((rows, 256), lambda n, *_: (0, n)),
            scratch_shapes=[pltpu.VMEM((rows, BLOCK), BF16), pltpu.VMEM((BLOCK, 256), BF16)],
        ),
        compiler_params=params(),
        cost_estimate=cost(16 * BLOCK * BLOCK * cols, 4 * BLOCK * BLOCK + 4 * rows * cols),
        name="compact_ints",
    )(*scalars, at, mine, other, awaited)


def widen_tile(rows, cols, tile, occ, virt, win, dev, own_refs, sib_refs, wide_ref):
    parity = dev & 1
    counts = pair_scalars(occ, virt, win, dev >> 1)
    (o_a, o_b), _, (start_even, start_odd) = counts
    second = parity == 1
    o = jnp.where(second, o_b, o_a)
    i = iota((1, 256), 1) + tile * 256
    q = i >> 4
    spot = place(q, i & 15, second, counts)
    r = iota((256, 256), 0)
    picks = []
    for s in (parity, 1 - parity):
        start = jnp.where(second, jnp.where(s == 0, start_even, start_odd), 0) + 8 * tile * o
        start = jnp.minimum((start >> 7) << 7, cols - 256)
        window = pl.ds(pl.multiple_of(start, 128), 256)
        picks.append((window, one_hot(r + start, jnp.where((q & 1) == s, spot, -1))))
    for piece in range(2):
        x = dot(own_refs[piece][:, picks[0][0]], picks[0][1])
        x += dot(sib_refs[piece][:, picks[1][0]], picks[1][1])
        wide_ref[piece * cols : piece * cols + rows, :] = x.astype(BF16)
        if rows < cols:
            wide_ref[piece * cols + rows : (piece + 1) * cols, :] = jnp.zeros((cols - rows, 256), BF16)


def widen_kernel(rows, cols, slots, occ, virt, win, at, *refs):
    wide_ref = refs[-1]
    for slot in range(slots):

        @pl.when(pl.program_id(0) == slot)
        def _():
            t0, t1, s0, s1 = refs[4 * slot : 4 * slot + 4]
            tile = pl.program_id(1)
            widen_tile(rows, cols, tile, occ, virt, win, at[1], (t0, t1), (s0, s1), wide_ref.at[0])


def widen(rows, cols, scalars, at, blocks):
    slots = len(blocks) // 4
    square = pl.BlockSpec((rows, cols), lambda t, n, *_: (0, 0), pipeline_mode=pl.Buffered(1))
    return pl.pallas_call(
        functools.partial(widen_kernel, rows, cols, slots),
        out_shape=jax.ShapeDtypeStruct((slots, 2 * cols, BLOCK), BF16),
        grid_spec=pltpu.PrefetchScalarGridSpec(
            num_scalar_prefetch=4,
            grid=(slots, BLOCK // 256),
            in_specs=[square] * len(blocks),
            out_specs=pl.BlockSpec((1, 2 * cols, 256), lambda t, n, *_: (t, 0, n)),
        ),
        compiler_params=params(),
        cost_estimate=cost(slots * 8 * rows * 512 * BLOCK, slots * (8 * rows * cols + 4 * cols * BLOCK)),
        name="widen",
    )(*scalars, at, *blocks)


def product_kernel(inner, ints_ref, wide_ref, acc_ref):
    at = pl.ds(pl.multiple_of(pl.program_id(1) * WIDE, WIDE), WIDE)

    @pl.when(pl.program_id(0) == 0)
    def _():
        acc_ref[:, :, at] = jnp.zeros((2, acc_ref.shape[1], WIDE), F32)

    @pl.loop(0, 2)
    def _(half):
        acc_ref[half, :, at] += dot(ints_ref[0, half], wide_ref[0])


def product(rows, cols, inner, ints, wide):
    slots = wide.shape[0]
    return pl.pallas_call(
        product_kernel,
        out_shape=jax.ShapeDtypeStruct((2, rows, BLOCK), F32),
        grid_spec=pltpu.PrefetchScalarGridSpec(
            num_scalar_prefetch=1,
            grid=(slots, BLOCK // WIDE),
            in_specs=[
                pl.BlockSpec((1, 2, rows, 2 * cols), lambda t, n, k: (k[t], 0, 0, 0)),
                pl.BlockSpec((1, 2 * cols, WIDE), lambda t, n, k: (t, 0, n)),
            ],
            out_specs=pl.BlockSpec((2, rows, BLOCK), lambda t, n, k: (0, 0, 0)),
        ),
        compiler_params=params(),
        cost_estimate=cost(16 * slots * rows * cols * BLOCK, slots * 4 * cols * (rows + BLOCK)),
        name="product",
    )(inner, ints, wide)


def last_kernel(
    rows, cols, occ, virt, win, at, inner,
    ints_ref, t0, t1, s0, s1, old_ref, evirt, eocc_ref, ecol_ref, out_ref, wide_ref, sum_ref,
):
    plane, dev = at[0], at[1]

    @pl.loop(0, WIDE // 256)
    def _(part):
        tile = pl.program_id(0) * (WIDE // 256) + part
        into = wide_ref.at[:, pl.ds(pl.multiple_of(part * 256, 256), 256)]
        widen_tile(rows, cols, tile, occ, virt, win, dev, (t0, t1), (s0, s1), into)

    @pl.loop(0, 2)
    def _(half):
        sum_ref[half, :rows, :] = old_ref[half] + dot(ints_ref[0, half], wide_ref[...])

    i = iota((1, WIDE), 1) + pl.program_id(0) * WIDE
    col_live = ((i & 15) < occ[dev]) & ((i >> 4) < virt[dev ^ win[0]])
    col_energy = ecol_ref[...]
    _, _, starts = pair_scalars(occ, virt, win, plane)
    p = iota((OCC_CAP, 1), 0)
    irreps = [2 * plane, 2 * plane + 1]
    occs = [occ[irrep] for irrep in irreps]
    partners = [irrep ^ win[0] for irrep in irreps]
    virts = [virt[partner] for partner in partners]
    live = [(p < o) & col_live for o in occs]

    @pl.loop(0, VIR_CAP // 4)
    def _(group):
        for h in range(2):
            for i in range(4):
                half_q, s = 2 * group + i // 2, i % 2
                q = 2 * half_q + s
                start = half_q * occs[h]
                if h == 1:
                    start = start + starts[s]
                start = jnp.minimum(start, rows)
                block = sum_ref[s, pl.ds(pl.multiple_of((start >> 3) << 3, 8), OCC_CAP + 8), :]
                block = pltpu.roll(block, OCC_CAP + 8 - (start & 7), 0)[:OCC_CAP]
                denom = (eocc_ref[h] - evirt[partners[h], q]) + col_energy
                value = jnp.where(live[h] & (q < virts[h]), block / denom, 0.0)
                at_row = pl.multiple_of((h * VIR_CAP + q) * OCC_CAP, OCC_CAP)
                out_ref[pl.ds(at_row, OCC_CAP), :] = value


def last(rows, cols, scalars, at, inner, ints, own, sib, acc, energies):
    square = pl.BlockSpec((rows, cols), lambda n, *_: (0, 0))
    return pl.pallas_call(
        functools.partial(last_kernel, rows, cols),
        out_shape=jax.ShapeDtypeStruct((2 * BLOCK, BLOCK), F32),
        grid_spec=pltpu.PrefetchScalarGridSpec(
            num_scalar_prefetch=5,
            grid=(BLOCK // WIDE,),
            in_specs=[
                pl.BlockSpec((1, 2, rows, 2 * cols), lambda n, o, v, w, a, k: (k[0], 0, 0, 0)),
                square, square, square, square,
                pl.BlockSpec((2, rows, WIDE), lambda n, *_: (0, 0, n)),
                pl.BlockSpec(memory_space=pltpu.SMEM),
                pl.BlockSpec((2, OCC_CAP, 1), lambda n, *_: (0, 0, 0)),
                pl.BlockSpec((1, WIDE), lambda n, *_: (0, n)),
            ],
            out_specs=pl.BlockSpec((2 * BLOCK, WIDE), lambda n, *_: (0, n)),
            scratch_shapes=[
                pltpu.VMEM((2 * cols, WIDE), BF16),
                pltpu.VMEM((2, rows + OCC_CAP + 8, WIDE), F32),
            ],
        ),
        compiler_params=params(),
        cost_estimate=cost(16 * rows * cols * BLOCK, 8 * rows * cols + 16 * rows * BLOCK),
        name="last_product",
    )(*scalars, at, inner, ints, *own, *sib, acc, *energies)


def after_kernel(*refs):
    pass


def after(kept, awaited):
    whole = pl.BlockSpec(memory_space=pl.ANY)
    return pl.pallas_call(
        after_kernel,
        out_shape=[jax.ShapeDtypeStruct(x.shape, x.dtype) for x in kept],
        in_specs=[whole] * (len(kept) + len(awaited)),
        out_specs=[whole] * len(kept),
        input_output_aliases={i: i for i in range(len(kept))},
        name="after",
    )(*kept, *awaited)


def ring_order(n):
    return list(range(0, 1)) + list(range(1, n, 2)) + [i for i in range(n - 1, 0, -1) if i % 2 == 0]


def branch(rows, nrow, ncol, t2, ints, occ, virt, win, eps_virt, occ_rows, col_energy, at, sources):
    cols = -(-rows // 128) * 128
    scalars = (occ, virt, win)
    order = ring_order(nrow)
    ring = [(order[i], order[(i + 1) % nrow]) for i in range(nrow)]
    swap = [(c, c ^ 1) for c in range(ncol)]

    def to_sibling(x):
        return lax.ppermute(x, "col", swap)

    def around(x):
        return lax.ppermute(x, "row", ring)

    def exchange(x):
        return lax.all_to_all(x, "col", split_axis=0, concat_axis=0, tiled=True)

    even, odd = prep(cols, scalars, t2)
    even, odd = compact_rows(rows, cols, 0, scalars, at, exchange(even), passed=(odd,))
    mine = ints.reshape(2, VIR_CAP // 2, 2, OCC_CAP, BLOCK)
    other = lax.dynamic_index_in_dim(mine, 1 - (at[1] & 1), 2, keepdims=False).reshape(BLOCK, BLOCK)
    even_next = around(even)
    small = compact_ints(rows, cols, scalars, at, mine, to_sibling(other), even)
    odd, small = compact_rows(rows, cols, 1, scalars, at, exchange(odd), passed=(small,))
    odd, small = after([odd, small], [even_next])
    panel = lax.all_gather(small, "col", axis=0, tiled=False).reshape(ncol // 2, 2, rows, 2 * cols)

    held = [even, odd]
    blocks = []
    for step in range(nrow - 1):
        later = [even_next if step == 0 else around(held[0]), around(held[1])]
        blocks += held + [to_sibling(x) for x in held]
        held = later
    wide = widen(rows, cols, scalars, at, blocks)
    acc = product(rows, cols, sources[: nrow - 1], panel, wide)
    (even,) = after(held[:1], [acc])
    sib_even = to_sibling(even)
    (odd,) = after(held[1:], [acc, sib_even])
    own, sib = [even, odd], [sib_even, to_sibling(odd)]
    energies = (eps_virt, occ_rows, col_energy)
    return last(rows, cols, scalars, at, sources[nrow - 1 :], panel, own, sib, acc, energies)


def choose_kernel(occ, virt, win, index_ref):
    index = jnp.int32(len(SIZES) - 1)
    for pair in range(NIRREP // 2):
        (o_a, o_b), (v_a, v_b), _ = pair_scalars(occ, virt, win, pair)
        most = o_a * ((v_a + 1) >> 1) + o_b * ((v_b + 1) >> 1)
        fits = sum((most <= size).astype(I32) for size in SIZES[1:])
        index = jnp.minimum(index, fits)
    index_ref[0] = index


def choose(occ, virt, win):
    smem = pl.BlockSpec(memory_space=pltpu.SMEM)
    return pl.pallas_call(
        choose_kernel,
        out_shape=jax.ShapeDtypeStruct((1,), I32),
        in_specs=[smem] * 3,
        out_specs=smem,
        name="choose",
    )(occ, virt, win)[0]


def live_device(nrow, ncol, t2, ints, eps_occ, eps_virt, occ, virt, win):
    row, col = lax.axis_index("row"), lax.axis_index("col")
    index = choose(occ, virt, win)
    occ_rows = lax.dynamic_slice(eps_occ, (2 * row, 0), (2, OCC_CAP)).reshape(2, OCC_CAP, 1)
    col_occ = lax.dynamic_slice(eps_occ, (col, 0), (1, OCC_CAP))
    col_virt = lax.dynamic_slice(eps_virt, (col ^ win[0], 0), (1, VIR_CAP))
    col_energy = (col_occ[:, None, :] - col_virt[:, :, None]).reshape(1, BLOCK)
    at = jnp.stack([row, col]).astype(I32)
    order = ring_order(nrow)
    table = [[order[(order.index(z) - t) % nrow] for t in range(nrow)] for z in range(nrow)]
    sources = lax.dynamic_slice(jnp.array(table, I32), (row, 0), (1, nrow)).reshape(nrow)
    operands = (t2, ints, occ, virt, win, eps_virt, occ_rows, col_energy, at, sources)
    return lax.switch(index, [functools.partial(branch, size, nrow, ncol) for size in SIZES], *operands)


def ph_vectors(eps_occ, eps_virt, occ_count, virt_count, window_irrep):
    irreps = jnp.arange(NIRREP, dtype=I32)
    partner = jnp.bitwise_xor(irreps, window_irrep[0])
    onehot = partner[:, None] == irreps[None, :]
    virt_rows = jnp.dot(onehot.astype(F32), eps_virt, precision=lax.Precision.HIGHEST)
    virt_live = jnp.sum(jnp.where(onehot, virt_count[None, :], 0), axis=1)
    energy = eps_occ[:, None, :] - virt_rows[:, :, None]
    slots_occ = jnp.arange(OCC_CAP, dtype=I32)
    slots_virt = jnp.arange(VIR_CAP, dtype=I32)
    live = (slots_occ[None, None, :] < occ_count[:, None, None]) & (
        slots_virt[None, :, None] < virt_live[:, None, None]
    )
    return (energy, live)


def any_device(t2_pairs, cycle_ints, eps_occ, eps_virt, occ_count, virt_count, window_irrep):
    irrep_local = t2_pairs.shape[0]
    virt_local = t2_pairs.shape[4]
    total = NIRREP * VIR_CAP * OCC_CAP
    energy, live = ph_vectors(eps_occ, eps_virt, occ_count, virt_count, window_irrep)
    row_index = lax.axis_index("row")
    col_index = lax.axis_index("col")
    zero_index = jnp.int32(0)
    source_live = lax.dynamic_slice(
        live,
        (row_index * irrep_local, col_index * virt_local, zero_index),
        (irrep_local, virt_local, OCC_CAP),
    )
    full_live = live.reshape(-1)
    ordered = jnp.transpose(t2_pairs, (0, 4, 2, 1, 5, 3)).reshape(
        irrep_local, virt_local, OCC_CAP, total
    )
    keep = source_live[:, :, :, None] & full_live[None, None, None, :]
    ordered = jnp.where(keep, ordered, jnp.zeros_like(ordered))
    moved = lax.all_to_all(ordered, "col", split_axis=3, concat_axis=1, tiled=True)
    amp_local = moved.reshape(irrep_local * VIR_CAP * OCC_CAP, moved.shape[3])
    amp_panel = lax.all_gather(amp_local, "row", axis=0, tiled=True)
    ints_panel = lax.all_gather(cycle_ints, "col", axis=1, tiled=True)
    cycle = jnp.dot(ints_panel, amp_panel, preferred_element_type=F32)
    rows_here, cols_here = cycle.shape
    flat_energy = energy.reshape(-1)
    row_start, col_start = row_index * rows_here, col_index * cols_here
    row_energy = lax.dynamic_slice_in_dim(flat_energy, row_start, rows_here, 0)
    col_energy = lax.dynamic_slice_in_dim(flat_energy, col_start, cols_here, 0)
    row_live = lax.dynamic_slice_in_dim(full_live, row_start, rows_here, 0)
    col_live = lax.dynamic_slice_in_dim(full_live, col_start, cols_here, 0)
    denom = row_energy[:, None] + col_energy[None, :]
    return jnp.where(row_live[:, None] & col_live[None, :], cycle / denom, F32(0.0))


def solution(mesh):
    nrow, ncol = mesh.shape["row"], mesh.shape["col"]
    placed = (P("row", None, None, None, "col", None), P("row", "col"), P(), P(), P(), P(), P())
    body = any_device
    if 2 * nrow == NIRREP and ncol == NIRREP:
        body = functools.partial(live_device, nrow, ncol)
    return jax.shard_map(body, mesh=mesh, in_specs=placed, out_specs=P("row", "col"), check_vma=False)
```

```python
import functools

import jax
import jax.numpy as jnp
from jax import lax
from jax.experimental import pallas as pl
from jax.experimental.pallas import tpu as pltpu
from jax.sharding import PartitionSpec as P

NIRREP = 8
OCC_CAP = 16
VIR_CAP = 64
BLOCK = VIR_CAP * OCC_CAP
SIZES = (1024, 896, 768, 640)
WIDE = 512
F32 = jnp.float32
BF16 = jnp.bfloat16
I32 = jnp.int32
I16 = jnp.int16
VMEM_BYTES = 56 * 1024 * 1024


def iota(shape, dim):
    return lax.broadcasted_iota(I32, shape, dim)


def params():
    return pltpu.CompilerParams(vmem_limit_bytes=VMEM_BYTES)


def cost(flops, nbytes):
    return pl.CostEstimate(flops=flops, bytes_accessed=nbytes, transcendentals=0)


def pair_scalars(occ, virt, win, pair):
    first = 2 * pair
    o_a, o_b = occ[first], occ[first + 1]
    v_a, v_b = virt[first ^ win[0]], virt[(first + 1) ^ win[0]]
    return (o_a, o_b), (v_a, v_b), (o_a * ((v_a + 1) >> 1), o_a * (v_a >> 1))


def place(q, p, second, counts):
    (o_a, o_b), (v_a, v_b), (start_even, start_odd) = counts
    o = jnp.where(second, o_b, o_a)
    v = jnp.where(second, v_b, v_a)
    start = jnp.where(second, jnp.where((q & 1) == 0, start_even, start_odd), 0)
    return jnp.where((p < o) & (q < v), start + (q >> 1) * o + p, -1)


def one_hot(left, right):
    return jnp.where(left.astype(I16) == right.astype(I16), BF16(1.0), BF16(0.0))


def dot(a, b):
    return jnp.dot(a, b, preferred_element_type=F32)


def prep_kernel(size, occ, virt, win, t2_ref, even_ref, odd_ref, x_ref):
    counts = pair_scalars(occ, virt, win, pl.program_id(0))
    row = iota((256, 1), 0)
    source = (((row >> 6) & 1) << 7) | (((row >> 2) & 15) << 3) | ((row & 3) << 1) | (row >> 7)
    by_parity = one_hot(iota((256, 256), 1), source)
    targets = []
    for half in range(2):
        for group in range(4):
            parts = [
                t2_ref[:, half, :, 4 * group + i].astype(F32).reshape(256, VIR_CAP) for i in range(4)
            ]
            x = jnp.concatenate(parts, axis=1).astype(BF16)
            at = (4 * half + group) * 256
            x_ref[:, at : at + 256] = dot(by_parity, x).astype(BF16)
            r = iota((256, 1), 0)
            p, q = 4 * group + (r >> 6), r & 63
            spot = place(q, p, half == 1, counts)
            targets.append(jnp.where(spot >= 0, spot + (q & 1) * size, -1))
    @pl.loop(0, 2)
    def _(core):
        for tile in range(-(-size // 256)):
            col = min(256 * tile, size - 256)
            lane = iota((256, 256), 1) + (col + core * size)
            acc = jnp.zeros((256, 256), F32)
            for chunk in range(4 if col >= BLOCK // 2 else 0, 8):
                acc += dot(x_ref[:, chunk * 256 : chunk * 256 + 256], one_hot(targets[chunk], lane))
            acc = acc.astype(BF16)
            even_ref[core, :, col : col + 256] = acc[:128]
            odd_ref[core, :, col : col + 256] = acc[128:]


def prep(size, scalars, t2):
    shape = jax.ShapeDtypeStruct((NIRREP, 128, size), BF16)
    block = pl.BlockSpec((2, 128, size), lambda k, *_: (k, 0, 0))
    return pl.pallas_call(
        functools.partial(prep_kernel, size),
        out_shape=(shape, shape),
        grid_spec=pltpu.PrefetchScalarGridSpec(
            num_scalar_prefetch=3,
            grid=(NIRREP // 2,),
            in_specs=[
                pl.BlockSpec((2, 2, OCC_CAP, OCC_CAP, 8, VIR_CAP), lambda k, *_: (0, k, 0, 0, 0, 0))
            ],
            out_specs=[block, block],
            scratch_shapes=[pltpu.VMEM((256, 2048), BF16)],
        ),
        compiler_params=params(),
        cost_estimate=cost(2 * 4 * 256 * 2048 * 2 * size, 12 * 2**20),
        name="prep_amplitudes",
    )(*scalars, t2)


def fill_rows(rows, spot, sel_ref):
    @pl.loop(0, rows // 128)
    def _(n):
        first = pl.multiple_of(n * 128, 128)
        sel_ref[pl.ds(first, 128), :] = one_hot(iota((128, BLOCK), 0) + first, spot)


def rows_kernel(rows, parity, count, occ, virt, win, at, x_ref, *refs):
    out_ref, sel_ref = refs[count], refs[-1]
    counts = pair_scalars(occ, virt, win, at[0])
    i = iota((1, BLOCK), 1)
    q = 8 * (i >> 7) + 2 * (i & 3) + parity
    spot = place(q, (i >> 2) & 15, ((i >> 6) & 1) == 1, counts)
    fill_rows(rows, spot, sel_ref)
    cols = out_ref.shape[1]

    @pl.loop(0, -(-cols // 256))
    def _(n):
        lanes = pl.ds(pl.multiple_of(jnp.minimum(n * 256, cols - 256), 128), 256)
        out_ref[:, lanes] = dot(sel_ref[...], x_ref[:, :, lanes].reshape(BLOCK, 256)).astype(BF16)


def compact_rows(rows, cols, parity, scalars, at, x, passed=(), awaited=()):
    whole = pl.BlockSpec(memory_space=pl.ANY)
    return pl.pallas_call(
        functools.partial(rows_kernel, rows, parity, len(passed) + len(awaited)),
        out_shape=[jax.ShapeDtypeStruct((rows, cols), BF16)]
        + [jax.ShapeDtypeStruct(y.shape, y.dtype) for y in passed],
        grid_spec=pltpu.PrefetchScalarGridSpec(
            num_scalar_prefetch=4,
            grid=(1,),
            in_specs=[pl.BlockSpec((NIRREP, 128, cols), lambda n, *_: (0, 0, 0))]
            + [whole] * (len(passed) + len(awaited)),
            out_specs=[pl.BlockSpec((rows, cols), lambda n, *_: (0, 0))] + [whole] * len(passed),
            scratch_shapes=[pltpu.VMEM((rows, BLOCK), BF16)],
        ),
        input_output_aliases={5 + i: 1 + i for i in range(len(passed))},
        compiler_params=params(),
        cost_estimate=cost(4 * rows * BLOCK * cols, 4 * rows * BLOCK),
        name="compact_rows",
    )(*scalars, at, x, *passed, *awaited)


def ints_kernel(rows, cols, occ, virt, win, at, mine_ref, other_ref, awaited, out_ref, sel_ref, cols_ref):
    plane, dev = at[0], at[1]
    parity = dev & 1

    @pl.when(pl.program_id(0) == 0)
    def _():
        counts = pair_scalars(occ, virt, win, plane)
        i = iota((1, BLOCK), 1)
        q = 2 * ((i >> 4) & 31) + parity
        spot = place(q, i & 15, (i >> 9) == 1, counts)
        fill_rows(rows, spot, sel_ref)

    counts = pair_scalars(occ, virt, win, dev >> 1)
    i = iota((BLOCK, 1), 0)
    q, p = i >> 4, i & 15
    lane = iota((BLOCK, 256), 1) + pl.program_id(0) * 256
    picks = []
    for second in (parity == 1, parity == 0):
        spot = place(q, p, second, counts)
        picks.append(one_hot(jnp.where(spot >= 0, spot + (q & 1) * cols, -1), lane))

    @pl.loop(0, 2)
    def _(half):
        at_rows = pl.ds(pl.multiple_of(half * (BLOCK // 2), BLOCK // 2), BLOCK // 2)
        acc = dot(mine_ref[half].reshape(BLOCK // 2, BLOCK), picks[0])
        acc += dot(other_ref[half].reshape(BLOCK // 2, BLOCK), picks[1])
        cols_ref[at_rows, :] = acc.astype(BF16)

    out_ref[...] = dot(sel_ref[...], cols_ref[...]).astype(BF16)


def compact_ints(rows, cols, scalars, at, mine, other, awaited):
    by_parity = pl.BlockSpec(
        (2, VIR_CAP // 2, 1, OCC_CAP, BLOCK), lambda n, o, v, w, a: (0, 0, a[1] & 1, 0, 0)
    )
    return pl.pallas_call(
        functools.partial(ints_kernel, rows, cols),
        out_shape=jax.ShapeDtypeStruct((rows, 2 * cols), BF16),
        grid_spec=pltpu.PrefetchScalarGridSpec(
            num_scalar_prefetch=4,
            grid=(2 * cols // 256,),
            in_specs=[by_parity, by_parity, pl.BlockSpec(memory_space=pl.ANY)],
            out_specs=pl.BlockSpec((rows, 256), lambda n, *_: (0, n)),
            scratch_shapes=[pltpu.VMEM((rows, BLOCK), BF16), pltpu.VMEM((BLOCK, 256), BF16)],
        ),
        compiler_params=params(),
        cost_estimate=cost(16 * BLOCK * BLOCK * cols, 4 * BLOCK * BLOCK + 4 * rows * cols),
        name="compact_ints",
    )(*scalars, at, mine, other, awaited)


def widen_tile(rows, cols, tile, occ, virt, win, dev, own_refs, sib_refs, wide_ref):
    parity = dev & 1
    counts = pair_scalars(occ, virt, win, dev >> 1)
    (o_a, o_b), _, (start_even, start_odd) = counts
    second = parity == 1
    o = jnp.where(second, o_b, o_a)
    i = iota((1, 256), 1) + tile * 256
    q = i >> 4
    spot = place(q, i & 15, second, counts)
    r = iota((256, 256), 0)
    picks = []
    for s in (parity, 1 - parity):
        start = jnp.where(second, jnp.where(s == 0, start_even, start_odd), 0) + 8 * tile * o
        start = jnp.minimum((start >> 7) << 7, cols - 256)
        window = pl.ds(pl.multiple_of(start, 128), 256)
        picks.append((window, one_hot(r + start, jnp.where((q & 1) == s, spot, -1))))
    for piece in range(2):
        x = dot(own_refs[piece][:, picks[0][0]], picks[0][1])
        x += dot(sib_refs[piece][:, picks[1][0]], picks[1][1])
        wide_ref[piece * cols : piece * cols + rows, :] = x.astype(BF16)
        if rows < cols:
            wide_ref[piece * cols + rows : (piece + 1) * cols, :] = jnp.zeros((cols - rows, 256), BF16)


def widen_kernel(rows, cols, slots, occ, virt, win, at, *refs):
    wide_ref = refs[-1]
    for slot in range(slots):

        @pl.when(pl.program_id(0) == slot)
        def _():
            t0, t1, s0, s1 = refs[4 * slot : 4 * slot + 4]
            tile = pl.program_id(1)
            widen_tile(rows, cols, tile, occ, virt, win, at[1], (t0, t1), (s0, s1), wide_ref.at[0])


def widen(rows, cols, scalars, at, blocks):
    slots = len(blocks) // 4
    square = pl.BlockSpec((rows, cols), lambda t, n, *_: (0, 0), pipeline_mode=pl.Buffered(1))
    return pl.pallas_call(
        functools.partial(widen_kernel, rows, cols, slots),
        out_shape=jax.ShapeDtypeStruct((slots, 2 * cols, BLOCK), BF16),
        grid_spec=pltpu.PrefetchScalarGridSpec(
            num_scalar_prefetch=4,
            grid=(slots, BLOCK // 256),
            in_specs=[square] * len(blocks),
            out_specs=pl.BlockSpec((1, 2 * cols, 256), lambda t, n, *_: (t, 0, n)),
        ),
        compiler_params=params(),
        cost_estimate=cost(slots * 8 * rows * 512 * BLOCK, slots * (8 * rows * cols + 4 * cols * BLOCK)),
        name="widen",
    )(*scalars, at, *blocks)


def product_kernel(inner, ints_ref, wide_ref, acc_ref):
    at = pl.ds(pl.multiple_of(pl.program_id(1) * WIDE, WIDE), WIDE)

    @pl.when(pl.program_id(0) == 0)
    def _():
        acc_ref[:, :, at] = jnp.zeros((2, acc_ref.shape[1], WIDE), F32)

    @pl.loop(0, 2)
    def _(half):
        acc_ref[half, :, at] += dot(ints_ref[0, half], wide_ref[0])


def product(rows, cols, inner, ints, wide):
    slots = wide.shape[0]
    return pl.pallas_call(
        product_kernel,
        out_shape=jax.ShapeDtypeStruct((2, rows, BLOCK), F32),
        grid_spec=pltpu.PrefetchScalarGridSpec(
            num_scalar_prefetch=1,
            grid=(slots, BLOCK // WIDE),
            in_specs=[
                pl.BlockSpec((1, 2, rows, 2 * cols), lambda t, n, k: (k[t], 0, 0, 0)),
                pl.BlockSpec((1, 2 * cols, WIDE), lambda t, n, k: (t, 0, n)),
            ],
            out_specs=pl.BlockSpec((2, rows, BLOCK), lambda t, n, k: (0, 0, 0)),
        ),
        compiler_params=params(),
        cost_estimate=cost(16 * slots * rows * cols * BLOCK, slots * 4 * cols * (rows + BLOCK)),
        name="product",
    )(inner, ints, wide)


def last_kernel(
    rows, cols, occ, virt, win, at, inner,
    ints_ref, t0, t1, s0, s1, old_ref, evirt, eocc_ref, ecol_ref, out_ref, wide_ref, sum_ref,
):
    plane, dev = at[0], at[1]

    @pl.loop(0, WIDE // 256)
    def _(part):
        tile = pl.program_id(0) * (WIDE // 256) + part
        into = wide_ref.at[:, pl.ds(pl.multiple_of(part * 256, 256), 256)]
        widen_tile(rows, cols, tile, occ, virt, win, dev, (t0, t1), (s0, s1), into)

    @pl.loop(0, 2)
    def _(half):
        sum_ref[half, :rows, :] = old_ref[half] + dot(ints_ref[0, half], wide_ref[...])

    i = iota((1, WIDE), 1) + pl.program_id(0) * WIDE
    col_live = ((i & 15) < occ[dev]) & ((i >> 4) < virt[dev ^ win[0]])
    col_energy = ecol_ref[...]
    _, _, starts = pair_scalars(occ, virt, win, plane)
    p = iota((OCC_CAP, 1), 0)
    irreps = [2 * plane, 2 * plane + 1]
    occs = [occ[irrep] for irrep in irreps]
    partners = [irrep ^ win[0] for irrep in irreps]
    virts = [virt[partner] for partner in partners]
    live = [(p < o) & col_live for o in occs]

    @pl.loop(0, VIR_CAP // 4)
    def _(group):
        for h in range(2):
            for i in range(4):
                half_q, s = 2 * group + i // 2, i % 2
                q = 2 * half_q + s
                start = half_q * occs[h]
                if h == 1:
                    start = start + starts[s]
                start = jnp.minimum(start, rows)
                block = sum_ref[s, pl.ds(pl.multiple_of((start >> 3) << 3, 8), OCC_CAP + 8), :]
                block = pltpu.roll(block, OCC_CAP + 8 - (start & 7), 0)[:OCC_CAP]
                denom = (eocc_ref[h] - evirt[partners[h], q]) + col_energy
                value = jnp.where(live[h] & (q < virts[h]), block / denom, 0.0)
                at_row = pl.multiple_of((h * VIR_CAP + q) * OCC_CAP, OCC_CAP)
                out_ref[pl.ds(at_row, OCC_CAP), :] = value


def last(rows, cols, scalars, at, inner, ints, own, sib, acc, energies):
    square = pl.BlockSpec((rows, cols), lambda n, *_: (0, 0))
    return pl.pallas_call(
        functools.partial(last_kernel, rows, cols),
        out_shape=jax.ShapeDtypeStruct((2 * BLOCK, BLOCK), F32),
        grid_spec=pltpu.PrefetchScalarGridSpec(
            num_scalar_prefetch=5,
            grid=(BLOCK // WIDE,),
            in_specs=[
                pl.BlockSpec((1, 2, rows, 2 * cols), lambda n, o, v, w, a, k: (k[0], 0, 0, 0)),
                square, square, square, square,
                pl.BlockSpec((2, rows, WIDE), lambda n, *_: (0, 0, n)),
                pl.BlockSpec(memory_space=pltpu.SMEM),
                pl.BlockSpec((2, OCC_CAP, 1), lambda n, *_: (0, 0, 0)),
                pl.BlockSpec((1, WIDE), lambda n, *_: (0, n)),
            ],
            out_specs=pl.BlockSpec((2 * BLOCK, WIDE), lambda n, *_: (0, n)),
            scratch_shapes=[
                pltpu.VMEM((2 * cols, WIDE), BF16),
                pltpu.VMEM((2, rows + OCC_CAP + 8, WIDE), F32),
            ],
        ),
        compiler_params=params(),
        cost_estimate=cost(16 * rows * cols * BLOCK, 8 * rows * cols + 16 * rows * BLOCK),
        name="last_product",
    )(*scalars, at, inner, ints, *own, *sib, acc, *energies)


def after_kernel(*refs):
    pass


def after(kept, awaited):
    whole = pl.BlockSpec(memory_space=pl.ANY)
    return pl.pallas_call(
        after_kernel,
        out_shape=[jax.ShapeDtypeStruct(x.shape, x.dtype) for x in kept],
        in_specs=[whole] * (len(kept) + len(awaited)),
        out_specs=[whole] * len(kept),
        input_output_aliases={i: i for i in range(len(kept))},
        name="after",
    )(*kept, *awaited)


def ring_order(n):
    return list(range(0, 1)) + list(range(1, n, 2)) + [i for i in range(n - 1, 0, -1) if i % 2 == 0]


def branch(rows, nrow, ncol, t2, ints, occ, virt, win, eps_virt, occ_rows, col_energy, at, sources):
    cols = -(-rows // 128) * 128
    scalars = (occ, virt, win)
    order = ring_order(nrow)
    ring = [(order[i], order[(i + 1) % nrow]) for i in range(nrow)]
    swap = [(c, c ^ 1) for c in range(ncol)]

    def to_sibling(x):
        return lax.ppermute(x, "col", swap)

    def around(x):
        return lax.ppermute(x, "row", ring)

    def exchange(x):
        return lax.all_to_all(x, "col", split_axis=0, concat_axis=0, tiled=True)

    even, odd = prep(cols, scalars, t2)
    even, odd = compact_rows(rows, cols, 0, scalars, at, exchange(even), passed=(odd,))
    mine = ints.reshape(2, VIR_CAP // 2, 2, OCC_CAP, BLOCK)
    even_next = around(even)
    small = compact_ints(rows, cols, scalars, at, mine, to_sibling(ints).reshape(mine.shape), even)
    odd, small = compact_rows(rows, cols, 1, scalars, at, exchange(odd), passed=(small,))
    odd, small = after([odd, small], [even_next])
    panel = lax.all_gather(small, "col", axis=0, tiled=False).reshape(ncol // 2, 2, rows, 2 * cols)

    held = [even, odd]
    blocks = []
    for step in range(nrow - 1):
        later = [even_next if step == 0 else around(held[0]), around(held[1])]
        blocks += held + [to_sibling(x) for x in held]
        held = later
    wide = widen(rows, cols, scalars, at, blocks)
    acc = product(rows, cols, sources[: nrow - 1], panel, wide)
    (even,) = after(held[:1], [acc])
    sib_even = to_sibling(even)
    (odd,) = after(held[1:], [acc, sib_even])
    own, sib = [even, odd], [sib_even, to_sibling(odd)]
    energies = (eps_virt, occ_rows, col_energy)
    return last(rows, cols, scalars, at, sources[nrow - 1 :], panel, own, sib, acc, energies)


def choose_kernel(occ, virt, win, index_ref):
    index = jnp.int32(len(SIZES) - 1)
    for pair in range(NIRREP // 2):
        (o_a, o_b), (v_a, v_b), _ = pair_scalars(occ, virt, win, pair)
        most = o_a * ((v_a + 1) >> 1) + o_b * ((v_b + 1) >> 1)
        fits = sum((most <= size).astype(I32) for size in SIZES[1:])
        index = jnp.minimum(index, fits)
    index_ref[0] = index


def choose(occ, virt, win):
    smem = pl.BlockSpec(memory_space=pltpu.SMEM)
    return pl.pallas_call(
        choose_kernel,
        out_shape=jax.ShapeDtypeStruct((1,), I32),
        in_specs=[smem] * 3,
        out_specs=smem,
        name="choose",
    )(occ, virt, win)[0]


def live_device(nrow, ncol, t2, ints, eps_occ, eps_virt, occ, virt, win):
    row, col = lax.axis_index("row"), lax.axis_index("col")
    index = choose(occ, virt, win)
    occ_rows = lax.dynamic_slice(eps_occ, (2 * row, 0), (2, OCC_CAP)).reshape(2, OCC_CAP, 1)
    col_occ = lax.dynamic_slice(eps_occ, (col, 0), (1, OCC_CAP))
    col_virt = lax.dynamic_slice(eps_virt, (col ^ win[0], 0), (1, VIR_CAP))
    col_energy = (col_occ[:, None, :] - col_virt[:, :, None]).reshape(1, BLOCK)
    at = jnp.stack([row, col]).astype(I32)
    order = ring_order(nrow)
    table = [[order[(order.index(z) - t) % nrow] for t in range(nrow)] for z in range(nrow)]
    sources = lax.dynamic_slice(jnp.array(table, I32), (row, 0), (1, nrow)).reshape(nrow)
    operands = (t2, ints, occ, virt, win, eps_virt, occ_rows, col_energy, at, sources)
    return lax.switch(index, [functools.partial(branch, size, nrow, ncol) for size in SIZES], *operands)


def ph_vectors(eps_occ, eps_virt, occ_count, virt_count, window_irrep):
    irreps = jnp.arange(NIRREP, dtype=I32)
    partner = jnp.bitwise_xor(irreps, window_irrep[0])
    onehot = partner[:, None] == irreps[None, :]
    virt_rows = jnp.dot(onehot.astype(F32), eps_virt, precision=lax.Precision.HIGHEST)
    virt_live = jnp.sum(jnp.where(onehot, virt_count[None, :], 0), axis=1)
    energy = eps_occ[:, None, :] - virt_rows[:, :, None]
    slots_occ = jnp.arange(OCC_CAP, dtype=I32)
    slots_virt = jnp.arange(VIR_CAP, dtype=I32)
    live = (slots_occ[None, None, :] < occ_count[:, None, None]) & (
        slots_virt[None, :, None] < virt_live[:, None, None]
    )
    return (energy, live)


def any_device(t2_pairs, cycle_ints, eps_occ, eps_virt, occ_count, virt_count, window_irrep):
    irrep_local = t2_pairs.shape[0]
    virt_local = t2_pairs.shape[4]
    total = NIRREP * VIR_CAP * OCC_CAP
    energy, live = ph_vectors(eps_occ, eps_virt, occ_count, virt_count, window_irrep)
    row_index = lax.axis_index("row")
    col_index = lax.axis_index("col")
    zero_index = jnp.int32(0)
    source_live = lax.dynamic_slice(
        live,
        (row_index * irrep_local, col_index * virt_local, zero_index),
        (irrep_local, virt_local, OCC_CAP),
    )
    full_live = live.reshape(-1)
    ordered = jnp.transpose(t2_pairs, (0, 4, 2, 1, 5, 3)).reshape(
        irrep_local, virt_local, OCC_CAP, total
    )
    keep = source_live[:, :, :, None] & full_live[None, None, None, :]
    ordered = jnp.where(keep, ordered, jnp.zeros_like(ordered))
    moved = lax.all_to_all(ordered, "col", split_axis=3, concat_axis=1, tiled=True)
    amp_local = moved.reshape(irrep_local * VIR_CAP * OCC_CAP, moved.shape[3])
    amp_panel = lax.all_gather(amp_local, "row", axis=0, tiled=True)
    ints_panel = lax.all_gather(cycle_ints, "col", axis=1, tiled=True)
    cycle = jnp.dot(ints_panel, amp_panel, preferred_element_type=F32)
    rows_here, cols_here = cycle.shape
    flat_energy = energy.reshape(-1)
    row_start, col_start = row_index * rows_here, col_index * cols_here
    row_energy = lax.dynamic_slice_in_dim(flat_energy, row_start, rows_here, 0)
    col_energy = lax.dynamic_slice_in_dim(flat_energy, col_start, cols_here, 0)
    row_live = lax.dynamic_slice_in_dim(full_live, row_start, rows_here, 0)
    col_live = lax.dynamic_slice_in_dim(full_live, col_start, cols_here, 0)
    denom = row_energy[:, None] + col_energy[None, :]
    return jnp.where(row_live[:, None] & col_live[None, :], cycle / denom, F32(0.0))


def solution(mesh):
    nrow, ncol = mesh.shape["row"], mesh.shape["col"]
    placed = (P("row", None, None, None, "col", None), P("row", "col"), P(), P(), P(), P(), P())
    body = any_device
    if 2 * nrow == NIRREP and ncol == NIRREP:
        body = functools.partial(live_device, nrow, ncol)
    return jax.shard_map(body, mesh=mesh, in_specs=placed, out_specs=P("row", "col"), check_vma=False)
```

```python
import functools

import jax
import jax.numpy as jnp
from jax import lax
from jax.experimental import pallas as pl
from jax.experimental.pallas import tpu as pltpu
from jax.sharding import PartitionSpec as P

NIRREP = 8
OCC_CAP = 16
VIR_CAP = 64
BLOCK = VIR_CAP * OCC_CAP
SIZES = (1024, 640, 768, 896)
WIDE = 512
F32 = jnp.float32
BF16 = jnp.bfloat16
I32 = jnp.int32
I16 = jnp.int16
VMEM_BYTES = 56 * 1024 * 1024


def iota(shape, dim):
    return lax.broadcasted_iota(I32, shape, dim)


def params():
    return pltpu.CompilerParams(vmem_limit_bytes=VMEM_BYTES)


def cost(flops, nbytes):
    return pl.CostEstimate(flops=flops, bytes_accessed=nbytes, transcendentals=0)


def pair_scalars(occ, virt, win, pair):
    first = 2 * pair
    o_a, o_b = occ[first], occ[first + 1]
    v_a, v_b = virt[first ^ win[0]], virt[(first + 1) ^ win[0]]
    return (o_a, o_b), (v_a, v_b), (o_a * ((v_a + 1) >> 1), o_a * (v_a >> 1))


def place(q, p, second, counts):
    (o_a, o_b), (v_a, v_b), (start_even, start_odd) = counts
    o = jnp.where(second, o_b, o_a)
    v = jnp.where(second, v_b, v_a)
    start = jnp.where(second, jnp.where((q & 1) == 0, start_even, start_odd), 0)
    return jnp.where((p < o) & (q < v), start + (q >> 1) * o + p, -1)


def one_hot(left, right):
    return jnp.where(left.astype(I16) == right.astype(I16), BF16(1.0), BF16(0.0))


def dot(a, b):
    return jnp.dot(a, b, preferred_element_type=F32)


def prep_kernel(size, occ, virt, win, t2_ref, even_ref, odd_ref, x_ref):
    counts = pair_scalars(occ, virt, win, pl.program_id(0))
    row = iota((256, 1), 0)
    source = (((row >> 6) & 1) << 7) | (((row >> 2) & 15) << 3) | ((row & 3) << 1) | (row >> 7)
    by_parity = one_hot(iota((256, 256), 1), source)
    targets = []
    for half in range(2):
        for group in range(4):
            parts = [
                t2_ref[:, half, :, 4 * group + i].astype(F32).reshape(256, VIR_CAP) for i in range(4)
            ]
            x = jnp.concatenate(parts, axis=1).astype(BF16)
            at = (4 * half + group) * 256
            x_ref[:, at : at + 256] = dot(by_parity, x).astype(BF16)
            r = iota((256, 1), 0)
            p, q = 4 * group + (r >> 6), r & 63
            spot = place(q, p, half == 1, counts)
            targets.append(jnp.where(spot >= 0, spot + (q & 1) * size, -1))
    @pl.loop(0, 2)
    def _(core):
        for tile in range(-(-size // 256)):
            col = min(256 * tile, size - 256)
            lane = iota((256, 256), 1) + (col + core * size)
            acc = jnp.zeros((256, 256), F32)
            for chunk in range(4 if col >= BLOCK // 2 else 0, 8):
                acc += dot(x_ref[:, chunk * 256 : chunk * 256 + 256], one_hot(targets[chunk], lane))
            acc = acc.astype(BF16)
            even_ref[core, :, col : col + 256] = acc[:128]
            odd_ref[core, :, col : col + 256] = acc[128:]


def prep(size, scalars, t2):
    shape = jax.ShapeDtypeStruct((NIRREP, 128, size), BF16)
    block = pl.BlockSpec((2, 128, size), lambda k, *_: (k, 0, 0))
    return pl.pallas_call(
        functools.partial(prep_kernel, size),
        out_shape=(shape, shape),
        grid_spec=pltpu.PrefetchScalarGridSpec(
            num_scalar_prefetch=3,
            grid=(NIRREP // 2,),
            in_specs=[
                pl.BlockSpec((2, 2, OCC_CAP, OCC_CAP, 8, VIR_CAP), lambda k, *_: (0, k, 0, 0, 0, 0))
            ],
            out_specs=[block, block],
            scratch_shapes=[pltpu.VMEM((256, 2048), BF16)],
        ),
        compiler_params=params(),
        cost_estimate=cost(2 * 4 * 256 * 2048 * 2 * size, 12 * 2**20),
        name="prep_amplitudes",
    )(*scalars, t2)


def fill_rows(rows, spot, sel_ref):
    @pl.loop(0, rows // 128)
    def _(n):
        first = pl.multiple_of(n * 128, 128)
        sel_ref[pl.ds(first, 128), :] = one_hot(iota((128, BLOCK), 0) + first, spot)


def rows_kernel(rows, parity, count, occ, virt, win, at, x_ref, *refs):
    out_ref, sel_ref = refs[count], refs[-1]
    counts = pair_scalars(occ, virt, win, at[0])
    i = iota((1, BLOCK), 1)
    q = 8 * (i >> 7) + 2 * (i & 3) + parity
    spot = place(q, (i >> 2) & 15, ((i >> 6) & 1) == 1, counts)
    fill_rows(rows, spot, sel_ref)
    cols = out_ref.shape[1]

    @pl.loop(0, -(-cols // 256))
    def _(n):
        lanes = pl.ds(pl.multiple_of(jnp.minimum(n * 256, cols - 256), 128), 256)
        out_ref[:, lanes] = dot(sel_ref[...], x_ref[:, :, lanes].reshape(BLOCK, 256)).astype(BF16)


def compact_rows(rows, cols, parity, scalars, at, x, passed=(), awaited=()):
    whole = pl.BlockSpec(memory_space=pl.ANY)
    return pl.pallas_call(
        functools.partial(rows_kernel, rows, parity, len(passed) + len(awaited)),
        out_shape=[jax.ShapeDtypeStruct((rows, cols), BF16)]
        + [jax.ShapeDtypeStruct(y.shape, y.dtype) for y in passed],
        grid_spec=pltpu.PrefetchScalarGridSpec(
            num_scalar_prefetch=4,
            grid=(1,),
            in_specs=[pl.BlockSpec((NIRREP, 128, cols), lambda n, *_: (0, 0, 0))]
            + [whole] * (len(passed) + len(awaited)),
            out_specs=[pl.BlockSpec((rows, cols), lambda n, *_: (0, 0))] + [whole] * len(passed),
            scratch_shapes=[pltpu.VMEM((rows, BLOCK), BF16)],
        ),
        input_output_aliases={5 + i: 1 + i for i in range(len(passed))},
        compiler_params=params(),
        cost_estimate=cost(4 * rows * BLOCK * cols, 4 * rows * BLOCK),
        name="compact_rows",
    )(*scalars, at, x, *passed, *awaited)


def ints_kernel(rows, cols, occ, virt, win, at, mine_ref, other_ref, awaited, out_ref, sel_ref, cols_ref):
    plane, dev = at[0], at[1]
    parity = dev & 1

    @pl.when(pl.program_id(0) == 0)
    def _():
        counts = pair_scalars(occ, virt, win, plane)
        i = iota((1, BLOCK), 1)
        q = 2 * ((i >> 4) & 31) + parity
        spot = place(q, i & 15, (i >> 9) == 1, counts)
        fill_rows(rows, spot, sel_ref)

    counts = pair_scalars(occ, virt, win, dev >> 1)
    i = iota((BLOCK, 1), 0)
    q, p = i >> 4, i & 15
    lane = iota((BLOCK, 256), 1) + pl.program_id(0) * 256
    picks = []
    for second in (parity == 1, parity == 0):
        spot = place(q, p, second, counts)
        picks.append(one_hot(jnp.where(spot >= 0, spot + (q & 1) * cols, -1), lane))

    @pl.loop(0, 2)
    def _(half):
        at_rows = pl.ds(pl.multiple_of(half * (BLOCK // 2), BLOCK // 2), BLOCK // 2)
        acc = dot(mine_ref[half].reshape(BLOCK // 2, BLOCK), picks[0])
        acc += dot(other_ref[half].reshape(BLOCK // 2, BLOCK), picks[1])
        cols_ref[at_rows, :] = acc.astype(BF16)

    out_ref[...] = dot(sel_ref[...], cols_ref[...]).astype(BF16)


def compact_ints(rows, cols, scalars, at, mine, other, awaited):
    by_parity = pl.BlockSpec(
        (2, VIR_CAP // 2, 1, OCC_CAP, BLOCK), lambda n, o, v, w, a: (0, 0, a[1] & 1, 0, 0)
    )
    return pl.pallas_call(
        functools.partial(ints_kernel, rows, cols),
        out_shape=jax.ShapeDtypeStruct((rows, 2 * cols), BF16),
        grid_spec=pltpu.PrefetchScalarGridSpec(
            num_scalar_prefetch=4,
            grid=(2 * cols // 256,),
            in_specs=[by_parity, by_parity, pl.BlockSpec(memory_space=pl.ANY)],
            out_specs=pl.BlockSpec((rows, 256), lambda n, *_: (0, n)),
            scratch_shapes=[pltpu.VMEM((rows, BLOCK), BF16), pltpu.VMEM((BLOCK, 256), BF16)],
        ),
        compiler_params=params(),
        cost_estimate=cost(16 * BLOCK * BLOCK * cols, 4 * BLOCK * BLOCK + 4 * rows * cols),
        name="compact_ints",
    )(*scalars, at, mine, other, awaited)


def widen_tile(rows, cols, tile, occ, virt, win, dev, own_refs, sib_refs, wide_ref):
    parity = dev & 1
    counts = pair_scalars(occ, virt, win, dev >> 1)
    (o_a, o_b), _, (start_even, start_odd) = counts
    second = parity == 1
    o = jnp.where(second, o_b, o_a)
    i = iota((1, 256), 1) + tile * 256
    q = i >> 4
    spot = place(q, i & 15, second, counts)
    r = iota((256, 256), 0)
    picks = []
    for s in (parity, 1 - parity):
        start = jnp.where(second, jnp.where(s == 0, start_even, start_odd), 0) + 8 * tile * o
        start = jnp.minimum((start >> 7) << 7, cols - 256)
        window = pl.ds(pl.multiple_of(start, 128), 256)
        picks.append((window, one_hot(r + start, jnp.where((q & 1) == s, spot, -1))))
    for piece in range(2):
        x = dot(own_refs[piece][:, picks[0][0]], picks[0][1])
        x += dot(sib_refs[piece][:, picks[1][0]], picks[1][1])
        wide_ref[piece * cols : piece * cols + rows, :] = x.astype(BF16)
        if rows < cols:
            wide_ref[piece * cols + rows : (piece + 1) * cols, :] = jnp.zeros((cols - rows, 256), BF16)


def widen_kernel(rows, cols, slots, occ, virt, win, at, *refs):
    wide_ref = refs[-1]
    for slot in range(slots):

        @pl.when(pl.program_id(0) == slot)
        def _():
            t0, t1, s0, s1 = refs[4 * slot : 4 * slot + 4]
            tile = pl.program_id(1)
            widen_tile(rows, cols, tile, occ, virt, win, at[1], (t0, t1), (s0, s1), wide_ref.at[0])


def widen(rows, cols, scalars, at, blocks):
    slots = len(blocks) // 4
    square = pl.BlockSpec((rows, cols), lambda t, n, *_: (0, 0), pipeline_mode=pl.Buffered(1))
    return pl.pallas_call(
        functools.partial(widen_kernel, rows, cols, slots),
        out_shape=jax.ShapeDtypeStruct((slots, 2 * cols, BLOCK), BF16),
        grid_spec=pltpu.PrefetchScalarGridSpec(
            num_scalar_prefetch=4,
            grid=(slots, BLOCK // 256),
            in_specs=[square] * len(blocks),
            out_specs=pl.BlockSpec((1, 2 * cols, 256), lambda t, n, *_: (t, 0, n)),
        ),
        compiler_params=params(),
        cost_estimate=cost(slots * 8 * rows * 512 * BLOCK, slots * (8 * rows * cols + 4 * cols * BLOCK)),
        name="widen",
    )(*scalars, at, *blocks)


def product_kernel(inner, ints_ref, wide_ref, acc_ref):
    at = pl.ds(pl.multiple_of(pl.program_id(1) * WIDE, WIDE), WIDE)

    @pl.when(pl.program_id(0) == 0)
    def _():
        acc_ref[:, :, at] = jnp.zeros((2, acc_ref.shape[1], WIDE), F32)

    @pl.loop(0, 2)
    def _(half):
        acc_ref[half, :, at] += dot(ints_ref[0, half], wide_ref[0])


def product(rows, cols, inner, ints, wide):
    slots = wide.shape[0]
    return pl.pallas_call(
        product_kernel,
        out_shape=jax.ShapeDtypeStruct((2, rows, BLOCK), F32),
        grid_spec=pltpu.PrefetchScalarGridSpec(
            num_scalar_prefetch=1,
            grid=(slots, BLOCK // WIDE),
            in_specs=[
                pl.BlockSpec((1, 2, rows, 2 * cols), lambda t, n, k: (k[t], 0, 0, 0)),
                pl.BlockSpec((1, 2 * cols, WIDE), lambda t, n, k: (t, 0, n)),
            ],
            out_specs=pl.BlockSpec((2, rows, BLOCK), lambda t, n, k: (0, 0, 0)),
        ),
        compiler_params=params(),
        cost_estimate=cost(16 * slots * rows * cols * BLOCK, slots * 4 * cols * (rows + BLOCK)),
        name="product",
    )(inner, ints, wide)


def last_kernel(
    rows, cols, occ, virt, win, at, inner,
    ints_ref, t0, t1, s0, s1, old_ref, evirt, eocc_ref, ecol_ref, out_ref, wide_ref, sum_ref,
):
    plane, dev = at[0], at[1]

    @pl.loop(0, WIDE // 256)
    def _(part):
        tile = pl.program_id(0) * (WIDE // 256) + part
        into = wide_ref.at[:, pl.ds(pl.multiple_of(part * 256, 256), 256)]
        widen_tile(rows, cols, tile, occ, virt, win, dev, (t0, t1), (s0, s1), into)

    @pl.loop(0, 2)
    def _(half):
        sum_ref[half, :rows, :] = old_ref[half] + dot(ints_ref[0, half], wide_ref[...])

    i = iota((1, WIDE), 1) + pl.program_id(0) * WIDE
    col_live = ((i & 15) < occ[dev]) & ((i >> 4) < virt[dev ^ win[0]])
    col_energy = ecol_ref[...]
    _, _, starts = pair_scalars(occ, virt, win, plane)
    p = iota((OCC_CAP, 1), 0)
    irreps = [2 * plane, 2 * plane + 1]
    occs = [occ[irrep] for irrep in irreps]
    partners = [irrep ^ win[0] for irrep in irreps]
    virts = [virt[partner] for partner in partners]
    live = [(p < o) & col_live for o in occs]

    @pl.loop(0, VIR_CAP // 4)
    def _(group):
        for h in range(2):
            for i in range(4):
                half_q, s = 2 * group + i // 2, i % 2
                q = 2 * half_q + s
                start = half_q * occs[h]
                if h == 1:
                    start = start + starts[s]
                start = jnp.minimum(start, rows)
                block = sum_ref[s, pl.ds(pl.multiple_of((start >> 3) << 3, 8), OCC_CAP + 8), :]
                block = pltpu.roll(block, OCC_CAP + 8 - (start & 7), 0)[:OCC_CAP]
                denom = (eocc_ref[h] - evirt[partners[h], q]) + col_energy
                value = jnp.where(live[h] & (q < virts[h]), block / denom, 0.0)
                at_row = pl.multiple_of((h * VIR_CAP + q) * OCC_CAP, OCC_CAP)
                out_ref[pl.ds(at_row, OCC_CAP), :] = value


def last(rows, cols, scalars, at, inner, ints, own, sib, acc, energies):
    square = pl.BlockSpec((rows, cols), lambda n, *_: (0, 0))
    return pl.pallas_call(
        functools.partial(last_kernel, rows, cols),
        out_shape=jax.ShapeDtypeStruct((2 * BLOCK, BLOCK), F32),
        grid_spec=pltpu.PrefetchScalarGridSpec(
            num_scalar_prefetch=5,
            grid=(BLOCK // WIDE,),
            in_specs=[
                pl.BlockSpec((1, 2, rows, 2 * cols), lambda n, o, v, w, a, k: (k[0], 0, 0, 0)),
                square, square, square, square,
                pl.BlockSpec((2, rows, WIDE), lambda n, *_: (0, 0, n)),
                pl.BlockSpec(memory_space=pltpu.SMEM),
                pl.BlockSpec((2, OCC_CAP, 1), lambda n, *_: (0, 0, 0)),
                pl.BlockSpec((1, WIDE), lambda n, *_: (0, n)),
            ],
            out_specs=pl.BlockSpec((2 * BLOCK, WIDE), lambda n, *_: (0, n)),
            scratch_shapes=[
                pltpu.VMEM((2 * cols, WIDE), BF16),
                pltpu.VMEM((2, rows + OCC_CAP + 8, WIDE), F32),
            ],
        ),
        compiler_params=params(),
        cost_estimate=cost(16 * rows * cols * BLOCK, 8 * rows * cols + 16 * rows * BLOCK),
        name="last_product",
    )(*scalars, at, inner, ints, *own, *sib, acc, *energies)


def after_kernel(*refs):
    pass


def after(kept, awaited):
    whole = pl.BlockSpec(memory_space=pl.ANY)
    return pl.pallas_call(
        after_kernel,
        out_shape=[jax.ShapeDtypeStruct(x.shape, x.dtype) for x in kept],
        in_specs=[whole] * (len(kept) + len(awaited)),
        out_specs=[whole] * len(kept),
        input_output_aliases={i: i for i in range(len(kept))},
        name="after",
    )(*kept, *awaited)


def ring_order(n):
    return list(range(0, 1)) + list(range(1, n, 2)) + [i for i in range(n - 1, 0, -1) if i % 2 == 0]


def branch(rows, nrow, ncol, t2, ints, occ, virt, win, eps_virt, occ_rows, col_energy, at, sources):
    cols = -(-rows // 128) * 128
    scalars = (occ, virt, win)
    order = ring_order(nrow)
    ring = [(order[i], order[(i + 1) % nrow]) for i in range(nrow)]
    swap = [(c, c ^ 1) for c in range(ncol)]

    def to_sibling(x):
        return lax.ppermute(x, "col", swap)

    def around(x):
        return lax.ppermute(x, "row", ring)

    def exchange(x):
        return lax.all_to_all(x, "col", split_axis=0, concat_axis=0, tiled=True)

    even, odd = prep(cols, scalars, t2)
    even, odd = compact_rows(rows, cols, 0, scalars, at, exchange(even), passed=(odd,))
    mine = ints.reshape(2, VIR_CAP // 2, 2, OCC_CAP, BLOCK)
    even_next = around(even)
    small = compact_ints(rows, cols, scalars, at, mine, to_sibling(ints).reshape(mine.shape), even)
    odd, small = compact_rows(rows, cols, 1, scalars, at, exchange(odd), passed=(small,))
    odd, small = after([odd, small], [even_next])
    panel = lax.all_gather(small, "col", axis=0, tiled=False).reshape(ncol // 2, 2, rows, 2 * cols)

    held = [even, odd]
    blocks = []
    for step in range(nrow - 1):
        later = [even_next if step == 0 else around(held[0]), around(held[1])]
        blocks += held + [to_sibling(x) for x in held]
        held = later
    wide = widen(rows, cols, scalars, at, blocks)
    acc = product(rows, cols, sources[: nrow - 1], panel, wide)
    (even,) = after(held[:1], [acc])
    sib_even = to_sibling(even)
    (odd,) = after(held[1:], [acc, sib_even])
    own, sib = [even, odd], [sib_even, to_sibling(odd)]
    energies = (eps_virt, occ_rows, col_energy)
    return last(rows, cols, scalars, at, sources[nrow - 1 :], panel, own, sib, acc, energies)


def choose_kernel(occ, virt, win, index_ref):
    most = jnp.int32(0)
    for pair in range(NIRREP // 2):
        (o_a, o_b), (v_a, v_b), _ = pair_scalars(occ, virt, win, pair)
        most = jnp.maximum(most, o_a * ((v_a + 1) >> 1) + o_b * ((v_b + 1) >> 1))
    index = jnp.int32(SIZES.index(max(SIZES)))
    for size in sorted(SIZES, reverse=True):
        index = jnp.where(most <= size, SIZES.index(size), index)
    index_ref[0] = index


def choose(occ, virt, win):
    smem = pl.BlockSpec(memory_space=pltpu.SMEM)
    return pl.pallas_call(
        choose_kernel,
        out_shape=jax.ShapeDtypeStruct((1,), I32),
        in_specs=[smem] * 3,
        out_specs=smem,
        name="choose",
    )(occ, virt, win)[0]


def live_device(nrow, ncol, t2, ints, eps_occ, eps_virt, occ, virt, win):
    row, col = lax.axis_index("row"), lax.axis_index("col")
    index = choose(occ, virt, win)
    occ_rows = lax.dynamic_slice(eps_occ, (2 * row, 0), (2, OCC_CAP)).reshape(2, OCC_CAP, 1)
    col_occ = lax.dynamic_slice(eps_occ, (col, 0), (1, OCC_CAP))
    col_virt = lax.dynamic_slice(eps_virt, (col ^ win[0], 0), (1, VIR_CAP))
    col_energy = (col_occ[:, None, :] - col_virt[:, :, None]).reshape(1, BLOCK)
    at = jnp.stack([row, col]).astype(I32)
    order = ring_order(nrow)
    table = [[order[(order.index(z) - t) % nrow] for t in range(nrow)] for z in range(nrow)]
    sources = lax.dynamic_slice(jnp.array(table, I32), (row, 0), (1, nrow)).reshape(nrow)
    operands = (t2, ints, occ, virt, win, eps_virt, occ_rows, col_energy, at, sources)
    return lax.switch(index, [functools.partial(branch, size, nrow, ncol) for size in SIZES], *operands)


def ph_vectors(eps_occ, eps_virt, occ_count, virt_count, window_irrep):
    irreps = jnp.arange(NIRREP, dtype=I32)
    partner = jnp.bitwise_xor(irreps, window_irrep[0])
    onehot = partner[:, None] == irreps[None, :]
    virt_rows = jnp.dot(onehot.astype(F32), eps_virt, precision=lax.Precision.HIGHEST)
    virt_live = jnp.sum(jnp.where(onehot, virt_count[None, :], 0), axis=1)
    energy = eps_occ[:, None, :] - virt_rows[:, :, None]
    slots_occ = jnp.arange(OCC_CAP, dtype=I32)
    slots_virt = jnp.arange(VIR_CAP, dtype=I32)
    live = (slots_occ[None, None, :] < occ_count[:, None, None]) & (
        slots_virt[None, :, None] < virt_live[:, None, None]
    )
    return (energy, live)


def any_device(t2_pairs, cycle_ints, eps_occ, eps_virt, occ_count, virt_count, window_irrep):
    irrep_local = t2_pairs.shape[0]
    virt_local = t2_pairs.shape[4]
    total = NIRREP * VIR_CAP * OCC_CAP
    energy, live = ph_vectors(eps_occ, eps_virt, occ_count, virt_count, window_irrep)
    row_index = lax.axis_index("row")
    col_index = lax.axis_index("col")
    zero_index = jnp.int32(0)
    source_live = lax.dynamic_slice(
        live,
        (row_index * irrep_local, col_index * virt_local, zero_index),
        (irrep_local, virt_local, OCC_CAP),
    )
    full_live = live.reshape(-1)
    ordered = jnp.transpose(t2_pairs, (0, 4, 2, 1, 5, 3)).reshape(
        irrep_local, virt_local, OCC_CAP, total
    )
    keep = source_live[:, :, :, None] & full_live[None, None, None, :]
    ordered = jnp.where(keep, ordered, jnp.zeros_like(ordered))
    moved = lax.all_to_all(ordered, "col", split_axis=3, concat_axis=1, tiled=True)
    amp_local = moved.reshape(irrep_local * VIR_CAP * OCC_CAP, moved.shape[3])
    amp_panel = lax.all_gather(amp_local, "row", axis=0, tiled=True)
    ints_panel = lax.all_gather(cycle_ints, "col", axis=1, tiled=True)
    cycle = jnp.dot(ints_panel, amp_panel, preferred_element_type=F32)
    rows_here, cols_here = cycle.shape
    flat_energy = energy.reshape(-1)
    row_start, col_start = row_index * rows_here, col_index * cols_here
    row_energy = lax.dynamic_slice_in_dim(flat_energy, row_start, rows_here, 0)
    col_energy = lax.dynamic_slice_in_dim(flat_energy, col_start, cols_here, 0)
    row_live = lax.dynamic_slice_in_dim(full_live, row_start, rows_here, 0)
    col_live = lax.dynamic_slice_in_dim(full_live, col_start, cols_here, 0)
    denom = row_energy[:, None] + col_energy[None, :]
    return jnp.where(row_live[:, None] & col_live[None, :], cycle / denom, F32(0.0))


def solution(mesh):
    nrow, ncol = mesh.shape["row"], mesh.shape["col"]
    placed = (P("row", None, None, None, "col", None), P("row", "col"), P(), P(), P(), P(), P())
    body = any_device
    if 2 * nrow == NIRREP and ncol == NIRREP:
        body = functools.partial(live_device, nrow, ncol)
    return jax.shard_map(body, mesh=mesh, in_specs=placed, out_specs=P("row", "col"), check_vma=False)
```

```python
import functools

import jax
import jax.numpy as jnp
from jax import lax
from jax.experimental import pallas as pl
from jax.experimental.pallas import tpu as pltpu
from jax.sharding import PartitionSpec as P

NIRREP = 8
OCC_CAP = 16
VIR_CAP = 64
BLOCK = VIR_CAP * OCC_CAP
SIZES = (1024, 896, 768, 640)
WIDE = 512
F32 = jnp.float32
BF16 = jnp.bfloat16
I32 = jnp.int32
I16 = jnp.int16
VMEM_BYTES = 56 * 1024 * 1024


def iota(shape, dim):
    return lax.broadcasted_iota(I32, shape, dim)


def params():
    return pltpu.CompilerParams(vmem_limit_bytes=VMEM_BYTES)


def cost(flops, nbytes):
    return pl.CostEstimate(flops=flops, bytes_accessed=nbytes, transcendentals=0)


def pair_scalars(occ, virt, win, pair):
    first = 2 * pair
    o_a, o_b = occ[first], occ[first + 1]
    v_a, v_b = virt[first ^ win[0]], virt[(first + 1) ^ win[0]]
    return (o_a, o_b), (v_a, v_b), (o_a * ((v_a + 1) >> 1), o_a * (v_a >> 1))


def place(q, p, second, counts):
    (o_a, o_b), (v_a, v_b), (start_even, start_odd) = counts
    o = jnp.where(second, o_b, o_a)
    v = jnp.where(second, v_b, v_a)
    start = jnp.where(second, jnp.where((q & 1) == 0, start_even, start_odd), 0)
    return jnp.where((p < o) & (q < v), start + (q >> 1) * o + p, -1)


def one_hot(left, right):
    return jnp.where(left.astype(I16) == right.astype(I16), BF16(1.0), BF16(0.0))


def dot(a, b):
    return jnp.dot(a, b, preferred_element_type=F32)


def prep_kernel(size, occ, virt, win, t2_ref, even_ref, odd_ref, x_ref):
    counts = pair_scalars(occ, virt, win, pl.program_id(0))
    row = iota((256, 1), 0)
    source = (((row >> 6) & 1) << 7) | (((row >> 2) & 15) << 3) | ((row & 3) << 1) | (row >> 7)
    by_parity = one_hot(iota((256, 256), 1), source)
    targets = []
    for half in range(2):
        for group in range(4):
            parts = [
                t2_ref[:, half, :, 4 * group + i].astype(F32).reshape(256, VIR_CAP) for i in range(4)
            ]
            x = jnp.concatenate(parts, axis=1).astype(BF16)
            at = (4 * half + group) * 256
            x_ref[:, at : at + 256] = dot(by_parity, x).astype(BF16)
            r = iota((256, 1), 0)
            p, q = 4 * group + (r >> 6), r & 63
            spot = place(q, p, half == 1, counts)
            targets.append(jnp.where(spot >= 0, spot + (q & 1) * size, -1))
    @pl.loop(0, 2)
    def _(core):
        for tile in range(-(-size // 256)):
            col = min(256 * tile, size - 256)
            lane = iota((256, 256), 1) + (col + core * size)
            acc = jnp.zeros((256, 256), F32)
            for chunk in range(4 if col >= BLOCK // 2 else 0, 8):
                acc += dot(x_ref[:, chunk * 256 : chunk * 256 + 256], one_hot(targets[chunk], lane))
            acc = acc.astype(BF16)
            even_ref[core, :, col : col + 256] = acc[:128]
            odd_ref[core, :, col : col + 256] = acc[128:]


def prep(size, scalars, t2):
    shape = jax.ShapeDtypeStruct((NIRREP, 128, size), BF16)
    block = pl.BlockSpec((2, 128, size), lambda k, *_: (k, 0, 0))
    return pl.pallas_call(
        functools.partial(prep_kernel, size),
        out_shape=(shape, shape),
        grid_spec=pltpu.PrefetchScalarGridSpec(
            num_scalar_prefetch=3,
            grid=(NIRREP // 2,),
            in_specs=[
                pl.BlockSpec((2, 2, OCC_CAP, OCC_CAP, 8, VIR_CAP), lambda k, *_: (0, k, 0, 0, 0, 0))
            ],
            out_specs=[block, block],
            scratch_shapes=[pltpu.VMEM((256, 2048), BF16)],
        ),
        compiler_params=params(),
        cost_estimate=cost(2 * 4 * 256 * 2048 * 2 * size, 12 * 2**20),
        name="prep_amplitudes",
    )(*scalars, t2)


def fill_rows(rows, spot, sel_ref):
    @pl.loop(0, rows // 128)
    def _(n):
        first = pl.multiple_of(n * 128, 128)
        sel_ref[pl.ds(first, 128), :] = one_hot(iota((128, BLOCK), 0) + first, spot)


def rows_kernel(rows, parity, count, occ, virt, win, at, x_ref, *refs):
    out_ref, sel_ref = refs[count], refs[-1]
    counts = pair_scalars(occ, virt, win, at[0])
    i = iota((1, BLOCK), 1)
    q = 8 * (i >> 7) + 2 * (i & 3) + parity
    spot = place(q, (i >> 2) & 15, ((i >> 6) & 1) == 1, counts)
    fill_rows(rows, spot, sel_ref)
    cols = out_ref.shape[1]

    @pl.loop(0, -(-cols // 256))
    def _(n):
        lanes = pl.ds(pl.multiple_of(jnp.minimum(n * 256, cols - 256), 128), 256)
        out_ref[:, lanes] = dot(sel_ref[...], x_ref[:, :, lanes].reshape(BLOCK, 256)).astype(BF16)


def compact_rows(rows, cols, parity, scalars, at, x, passed=(), awaited=()):
    whole = pl.BlockSpec(memory_space=pl.ANY)
    return pl.pallas_call(
        functools.partial(rows_kernel, rows, parity, len(passed) + len(awaited)),
        out_shape=[jax.ShapeDtypeStruct((rows, cols), BF16)]
        + [jax.ShapeDtypeStruct(y.shape, y.dtype) for y in passed],
        grid_spec=pltpu.PrefetchScalarGridSpec(
            num_scalar_prefetch=4,
            grid=(1,),
            in_specs=[pl.BlockSpec((NIRREP, 128, cols), lambda n, *_: (0, 0, 0))]
            + [whole] * (len(passed) + len(awaited)),
            out_specs=[pl.BlockSpec((rows, cols), lambda n, *_: (0, 0))] + [whole] * len(passed),
            scratch_shapes=[pltpu.VMEM((rows, BLOCK), BF16)],
        ),
        input_output_aliases={5 + i: 1 + i for i in range(len(passed))},
        compiler_params=params(),
        cost_estimate=cost(4 * rows * BLOCK * cols, 4 * rows * BLOCK),
        name="compact_rows",
    )(*scalars, at, x, *passed, *awaited)


def ints_kernel(rows, cols, occ, virt, win, at, mine_ref, other_ref, awaited, out_ref, sel_ref, cols_ref):
    plane, dev = at[0], at[1]
    parity = dev & 1

    @pl.when(pl.program_id(0) == 0)
    def _():
        counts = pair_scalars(occ, virt, win, plane)
        i = iota((1, BLOCK), 1)
        q = 2 * ((i >> 4) & 31) + parity
        spot = place(q, i & 15, (i >> 9) == 1, counts)
        fill_rows(rows, spot, sel_ref)

    counts = pair_scalars(occ, virt, win, dev >> 1)
    i = iota((BLOCK, 1), 0)
    q, p = i >> 4, i & 15
    lane = iota((BLOCK, 256), 1) + pl.program_id(0) * 256
    picks = []
    for second in (parity == 1, parity == 0):
        spot = place(q, p, second, counts)
        picks.append(one_hot(jnp.where(spot >= 0, spot + (q & 1) * cols, -1), lane))

    @pl.loop(0, 2)
    def _(half):
        at_rows = pl.ds(pl.multiple_of(half * (BLOCK // 2), BLOCK // 2), BLOCK // 2)
        acc = dot(mine_ref[half].reshape(BLOCK // 2, BLOCK), picks[0])
        acc += dot(other_ref[half].reshape(BLOCK // 2, BLOCK), picks[1])
        cols_ref[at_rows, :] = acc.astype(BF16)

    out_ref[...] = dot(sel_ref[...], cols_ref[...]).astype(BF16)


def compact_ints(rows, cols, scalars, at, mine, other, awaited):
    by_parity = pl.BlockSpec(
        (2, VIR_CAP // 2, 1, OCC_CAP, BLOCK), lambda n, o, v, w, a: (0, 0, a[1] & 1, 0, 0)
    )
    return pl.pallas_call(
        functools.partial(ints_kernel, rows, cols),
        out_shape=jax.ShapeDtypeStruct((rows, 2 * cols), BF16),
        grid_spec=pltpu.PrefetchScalarGridSpec(
            num_scalar_prefetch=4,
            grid=(2 * cols // 256,),
            in_specs=[by_parity, by_parity, pl.BlockSpec(memory_space=pl.ANY)],
            out_specs=pl.BlockSpec((rows, 256), lambda n, *_: (0, n)),
            scratch_shapes=[pltpu.VMEM((rows, BLOCK), BF16), pltpu.VMEM((BLOCK, 256), BF16)],
        ),
        compiler_params=params(),
        cost_estimate=cost(16 * BLOCK * BLOCK * cols, 4 * BLOCK * BLOCK + 4 * rows * cols),
        name="compact_ints",
    )(*scalars, at, mine, other, awaited)


def widen_tile(rows, cols, tile, occ, virt, win, dev, own_refs, sib_refs, wide_ref):
    parity = dev & 1
    counts = pair_scalars(occ, virt, win, dev >> 1)
    (o_a, o_b), _, (start_even, start_odd) = counts
    second = parity == 1
    o = jnp.where(second, o_b, o_a)
    i = iota((1, 256), 1) + tile * 256
    q = i >> 4
    spot = place(q, i & 15, second, counts)
    r = iota((256, 256), 0)
    picks = []
    for s in (parity, 1 - parity):
        start = jnp.where(second, jnp.where(s == 0, start_even, start_odd), 0) + 8 * tile * o
        start = jnp.minimum((start >> 7) << 7, cols - 256)
        window = pl.ds(pl.multiple_of(start, 128), 256)
        picks.append((window, one_hot(r + start, jnp.where((q & 1) == s, spot, -1))))
    for piece in range(2):
        x = dot(own_refs[piece][:, picks[0][0]], picks[0][1])
        x += dot(sib_refs[piece][:, picks[1][0]], picks[1][1])
        wide_ref[piece * cols : piece * cols + rows, :] = x.astype(BF16)
        if rows < cols:
            wide_ref[piece * cols + rows : (piece + 1) * cols, :] = jnp.zeros((cols - rows, 256), BF16)


def widen_kernel(rows, cols, slots, occ, virt, win, at, *refs):
    wide_ref = refs[-1]
    for slot in range(slots):

        @pl.when(pl.program_id(0) == slot)
        def _():
            t0, t1, s0, s1 = refs[4 * slot : 4 * slot + 4]
            tile = pl.program_id(1)
            widen_tile(rows, cols, tile, occ, virt, win, at[1], (t0, t1), (s0, s1), wide_ref.at[0])


def widen(rows, cols, scalars, at, blocks):
    slots = len(blocks) // 4
    square = pl.BlockSpec((rows, cols), lambda t, n, *_: (0, 0), pipeline_mode=pl.Buffered(1))
    return pl.pallas_call(
        functools.partial(widen_kernel, rows, cols, slots),
        out_shape=jax.ShapeDtypeStruct((slots, 2 * cols, BLOCK), BF16),
        grid_spec=pltpu.PrefetchScalarGridSpec(
            num_scalar_prefetch=4,
            grid=(slots, BLOCK // 256),
            in_specs=[square] * len(blocks),
            out_specs=pl.BlockSpec((1, 2 * cols, 256), lambda t, n, *_: (t, 0, n)),
        ),
        compiler_params=params(),
        cost_estimate=cost(slots * 8 * rows * 512 * BLOCK, slots * (8 * rows * cols + 4 * cols * BLOCK)),
        name="widen",
    )(*scalars, at, *blocks)


def product_kernel(inner, ints_ref, wide_ref, acc_ref):
    at = pl.ds(pl.multiple_of(pl.program_id(1) * WIDE, WIDE), WIDE)

    @pl.when(pl.program_id(0) == 0)
    def _():
        acc_ref[:, :, at] = jnp.zeros((2, acc_ref.shape[1], WIDE), F32)

    @pl.loop(0, 2)
    def _(half):
        acc_ref[half, :, at] += dot(ints_ref[0, half], wide_ref[0])


def product(rows, cols, inner, ints, wide):
    slots = wide.shape[0]
    return pl.pallas_call(
        product_kernel,
        out_shape=jax.ShapeDtypeStruct((2, rows, BLOCK), F32),
        grid_spec=pltpu.PrefetchScalarGridSpec(
            num_scalar_prefetch=1,
            grid=(slots, BLOCK // WIDE),
            in_specs=[
                pl.BlockSpec((1, 2, rows, 2 * cols), lambda t, n, k: (k[t], 0, 0, 0)),
                pl.BlockSpec((1, 2 * cols, WIDE), lambda t, n, k: (t, 0, n)),
            ],
            out_specs=pl.BlockSpec((2, rows, BLOCK), lambda t, n, k: (0, 0, 0)),
        ),
        compiler_params=params(),
        cost_estimate=cost(16 * slots * rows * cols * BLOCK, slots * 4 * cols * (rows + BLOCK)),
        name="product",
    )(inner, ints, wide)


def last_kernel(
    rows, cols, occ, virt, win, at, inner,
    ints_ref, t0, t1, s0, s1, old_ref, evirt, eocc_ref, ecol_ref, out_ref, wide_ref, sum_ref,
):
    plane, dev = at[0], at[1]

    @pl.loop(0, WIDE // 256)
    def _(part):
        tile = pl.program_id(0) * (WIDE // 256) + part
        into = wide_ref.at[:, pl.ds(pl.multiple_of(part * 256, 256), 256)]
        widen_tile(rows, cols, tile, occ, virt, win, dev, (t0, t1), (s0, s1), into)

    @pl.loop(0, 2)
    def _(half):
        sum_ref[half, :rows, :] = old_ref[half] + dot(ints_ref[0, half], wide_ref[...])

    i = iota((1, WIDE), 1) + pl.program_id(0) * WIDE
    col_live = ((i & 15) < occ[dev]) & ((i >> 4) < virt[dev ^ win[0]])
    col_energy = ecol_ref[...]
    _, _, starts = pair_scalars(occ, virt, win, plane)
    p = iota((OCC_CAP, 1), 0)
    irreps = [2 * plane, 2 * plane + 1]
    occs = [occ[irrep] for irrep in irreps]
    partners = [irrep ^ win[0] for irrep in irreps]
    virts = [virt[partner] for partner in partners]
    live = [(p < o) & col_live for o in occs]

    @pl.loop(0, VIR_CAP // 2)
    def _(group):
        for h in range(2):
            for i in range(2):
                half_q, s = group, i
                q = 2 * half_q + s
                start = half_q * occs[h]
                if h == 1:
                    start = start + starts[s]
                start = jnp.minimum(start, rows)
                block = sum_ref[s, pl.ds(pl.multiple_of((start >> 3) << 3, 8), OCC_CAP + 8), :]
                block = pltpu.roll(block, OCC_CAP + 8 - (start & 7), 0)[:OCC_CAP]
                denom = (eocc_ref[h] - evirt[partners[h], q]) + col_energy
                value = jnp.where(live[h] & (q < virts[h]), block / denom, 0.0)
                at_row = pl.multiple_of((h * VIR_CAP + q) * OCC_CAP, OCC_CAP)
                out_ref[pl.ds(at_row, OCC_CAP), :] = value


def last(rows, cols, scalars, at, inner, ints, own, sib, acc, energies):
    square = pl.BlockSpec((rows, cols), lambda n, *_: (0, 0))
    return pl.pallas_call(
        functools.partial(last_kernel, rows, cols),
        out_shape=jax.ShapeDtypeStruct((2 * BLOCK, BLOCK), F32),
        grid_spec=pltpu.PrefetchScalarGridSpec(
            num_scalar_prefetch=5,
            grid=(BLOCK // WIDE,),
            in_specs=[
                pl.BlockSpec((1, 2, rows, 2 * cols), lambda n, o, v, w, a, k: (k[0], 0, 0, 0)),
                square, square, square, square,
                pl.BlockSpec((2, rows, WIDE), lambda n, *_: (0, 0, n)),
                pl.BlockSpec(memory_space=pltpu.SMEM),
                pl.BlockSpec((2, OCC_CAP, 1), lambda n, *_: (0, 0, 0)),
                pl.BlockSpec((1, WIDE), lambda n, *_: (0, n)),
            ],
            out_specs=pl.BlockSpec((2 * BLOCK, WIDE), lambda n, *_: (0, n)),
            scratch_shapes=[
                pltpu.VMEM((2 * cols, WIDE), BF16),
                pltpu.VMEM((2, rows + OCC_CAP + 8, WIDE), F32),
            ],
        ),
        compiler_params=params(),
        cost_estimate=cost(16 * rows * cols * BLOCK, 8 * rows * cols + 16 * rows * BLOCK),
        name="last_product",
    )(*scalars, at, inner, ints, *own, *sib, acc, *energies)


def after_kernel(*refs):
    pass


def after(kept, awaited):
    whole = pl.BlockSpec(memory_space=pl.ANY)
    return pl.pallas_call(
        after_kernel,
        out_shape=[jax.ShapeDtypeStruct(x.shape, x.dtype) for x in kept],
        in_specs=[whole] * (len(kept) + len(awaited)),
        out_specs=[whole] * len(kept),
        input_output_aliases={i: i for i in range(len(kept))},
        name="after",
    )(*kept, *awaited)


def ring_order(n):
    return list(range(0, 1)) + list(range(1, n, 2)) + [i for i in range(n - 1, 0, -1) if i % 2 == 0]


def branch(rows, nrow, ncol, t2, ints, occ, virt, win, eps_virt, occ_rows, col_energy, at, sources):
    cols = -(-rows // 128) * 128
    scalars = (occ, virt, win)
    order = ring_order(nrow)
    ring = [(order[i], order[(i + 1) % nrow]) for i in range(nrow)]
    swap = [(c, c ^ 1) for c in range(ncol)]

    def to_sibling(x):
        return lax.ppermute(x, "col", swap)

    def around(x):
        return lax.ppermute(x, "row", ring)

    def exchange(x):
        return lax.all_to_all(x, "col", split_axis=0, concat_axis=0, tiled=True)

    even, odd = prep(cols, scalars, t2)
    even, odd = compact_rows(rows, cols, 0, scalars, at, exchange(even), passed=(odd,))
    mine = ints.reshape(2, VIR_CAP // 2, 2, OCC_CAP, BLOCK)
    even_next = around(even)
    small = compact_ints(rows, cols, scalars, at, mine, to_sibling(ints).reshape(mine.shape), even)
    odd, small = compact_rows(rows, cols, 1, scalars, at, exchange(odd), passed=(small,))
    odd, small = after([odd, small], [even_next])
    panel = lax.all_gather(small, "col", axis=0, tiled=False).reshape(ncol // 2, 2, rows, 2 * cols)

    held = [even, odd]
    blocks = []
    for step in range(nrow - 1):
        later = [even_next if step == 0 else around(held[0]), around(held[1])]
        blocks += held + [to_sibling(x) for x in held]
        held = later
    wide = widen(rows, cols, scalars, at, blocks)
    acc = product(rows, cols, sources[: nrow - 1], panel, wide)
    (even,) = after(held[:1], [acc])
    sib_even = to_sibling(even)
    (odd,) = after(held[1:], [acc, sib_even])
    own, sib = [even, odd], [sib_even, to_sibling(odd)]
    energies = (eps_virt, occ_rows, col_energy)
    return last(rows, cols, scalars, at, sources[nrow - 1 :], panel, own, sib, acc, energies)


def choose_kernel(occ, virt, win, index_ref):
    index = jnp.int32(len(SIZES) - 1)
    for pair in range(NIRREP // 2):
        (o_a, o_b), (v_a, v_b), _ = pair_scalars(occ, virt, win, pair)
        most = o_a * ((v_a + 1) >> 1) + o_b * ((v_b + 1) >> 1)
        fits = sum((most <= size).astype(I32) for size in SIZES[1:])
        index = jnp.minimum(index, fits)
    index_ref[0] = index


def choose(occ, virt, win):
    smem = pl.BlockSpec(memory_space=pltpu.SMEM)
    return pl.pallas_call(
        choose_kernel,
        out_shape=jax.ShapeDtypeStruct((1,), I32),
        in_specs=[smem] * 3,
        out_specs=smem,
        name="choose",
    )(occ, virt, win)[0]


def live_device(nrow, ncol, t2, ints, eps_occ, eps_virt, occ, virt, win):
    row, col = lax.axis_index("row"), lax.axis_index("col")
    index = choose(occ, virt, win)
    occ_rows = lax.dynamic_slice(eps_occ, (2 * row, 0), (2, OCC_CAP)).reshape(2, OCC_CAP, 1)
    col_occ = lax.dynamic_slice(eps_occ, (col, 0), (1, OCC_CAP))
    col_virt = lax.dynamic_slice(eps_virt, (col ^ win[0], 0), (1, VIR_CAP))
    col_energy = (col_occ[:, None, :] - col_virt[:, :, None]).reshape(1, BLOCK)
    at = jnp.stack([row, col]).astype(I32)
    order = ring_order(nrow)
    table = [[order[(order.index(z) - t) % nrow] for t in range(nrow)] for z in range(nrow)]
    sources = lax.dynamic_slice(jnp.array(table, I32), (row, 0), (1, nrow)).reshape(nrow)
    operands = (t2, ints, occ, virt, win, eps_virt, occ_rows, col_energy, at, sources)
    return lax.switch(index, [functools.partial(branch, size, nrow, ncol) for size in SIZES], *operands)


def ph_vectors(eps_occ, eps_virt, occ_count, virt_count, window_irrep):
    irreps = jnp.arange(NIRREP, dtype=I32)
    partner = jnp.bitwise_xor(irreps, window_irrep[0])
    onehot = partner[:, None] == irreps[None, :]
    virt_rows = jnp.dot(onehot.astype(F32), eps_virt, precision=lax.Precision.HIGHEST)
    virt_live = jnp.sum(jnp.where(onehot, virt_count[None, :], 0), axis=1)
    energy = eps_occ[:, None, :] - virt_rows[:, :, None]
    slots_occ = jnp.arange(OCC_CAP, dtype=I32)
    slots_virt = jnp.arange(VIR_CAP, dtype=I32)
    live = (slots_occ[None, None, :] < occ_count[:, None, None]) & (
        slots_virt[None, :, None] < virt_live[:, None, None]
    )
    return (energy, live)


def any_device(t2_pairs, cycle_ints, eps_occ, eps_virt, occ_count, virt_count, window_irrep):
    irrep_local = t2_pairs.shape[0]
    virt_local = t2_pairs.shape[4]
    total = NIRREP * VIR_CAP * OCC_CAP
    energy, live = ph_vectors(eps_occ, eps_virt, occ_count, virt_count, window_irrep)
    row_index = lax.axis_index("row")
    col_index = lax.axis_index("col")
    zero_index = jnp.int32(0)
    source_live = lax.dynamic_slice(
        live,
        (row_index * irrep_local, col_index * virt_local, zero_index),
        (irrep_local, virt_local, OCC_CAP),
    )
    full_live = live.reshape(-1)
    ordered = jnp.transpose(t2_pairs, (0, 4, 2, 1, 5, 3)).reshape(
        irrep_local, virt_local, OCC_CAP, total
    )
    keep = source_live[:, :, :, None] & full_live[None, None, None, :]
    ordered = jnp.where(keep, ordered, jnp.zeros_like(ordered))
    moved = lax.all_to_all(ordered, "col", split_axis=3, concat_axis=1, tiled=True)
    amp_local = moved.reshape(irrep_local * VIR_CAP * OCC_CAP, moved.shape[3])
    amp_panel = lax.all_gather(amp_local, "row", axis=0, tiled=True)
    ints_panel = lax.all_gather(cycle_ints, "col", axis=1, tiled=True)
    cycle = jnp.dot(ints_panel, amp_panel, preferred_element_type=F32)
    rows_here, cols_here = cycle.shape
    flat_energy = energy.reshape(-1)
    row_start, col_start = row_index * rows_here, col_index * cols_here
    row_energy = lax.dynamic_slice_in_dim(flat_energy, row_start, rows_here, 0)
    col_energy = lax.dynamic_slice_in_dim(flat_energy, col_start, cols_here, 0)
    row_live = lax.dynamic_slice_in_dim(full_live, row_start, rows_here, 0)
    col_live = lax.dynamic_slice_in_dim(full_live, col_start, cols_here, 0)
    denom = row_energy[:, None] + col_energy[None, :]
    return jnp.where(row_live[:, None] & col_live[None, :], cycle / denom, F32(0.0))


def solution(mesh):
    nrow, ncol = mesh.shape["row"], mesh.shape["col"]
    placed = (P("row", None, None, None, "col", None), P("row", "col"), P(), P(), P(), P(), P())
    body = any_device
    if 2 * nrow == NIRREP and ncol == NIRREP:
        body = functools.partial(live_device, nrow, ncol)
    return jax.shard_map(body, mesh=mesh, in_specs=placed, out_specs=P("row", "col"), check_vma=False)
```
